512 devices in a mesh: sx: 32 (over z, core), sy: 16 (over y, x).
Axes of the slice: x: 4, y: 4, z: 16, core: 2. Of those that a mesh axis runs over, the one named last changes fastest.
Arguments:
- queries: bfloat16 [512, 4096], P(('sx', 'sy')), may hold values from -6 to 6
- keys: bfloat16 [262144, 1024], P(('sx', 'sy')), may hold values from -6 to 6
- values: bfloat16 [262144, 1024], P(('sx', 'sy')), may hold values from -6 to 6
- block_ids: int32 [512, 16], replicated, may hold values from 0 to 63, as said below
Outputs:
- attended: bfloat16 [512, 4096], P(('sx', 'sy'))
The draws below stay inside these ranges and needn't reach their ends.
Inputs may be any that keep to these rules, and one draw needn't show every extreme that they name: `block_ids`: each row names 16 different blocks. Among the 32 rows stored on the devices of one sy index, every block is named by exactly 8 rows.
All inputs are finite; a program needn't handle non-finite values.
Results may differ from the reference program's by a relative error of at most 0.0046.
Values may be sent and summed in bfloat16 or wider, within the bound.
No kernel may reach another device: no remote copies, remote signals or barrier semaphores. Data moves between devices by JAX's collectives and lax.ppermute only.
A program may use at most 64 MiB of HBM per device.

```python
import jax
import jax.numpy as jnp
from jax import lax

QUERY_HEADS = 32
KEY_HEADS = 8
HEAD_WIDTH = 128
BLOCK = 4096
DEVICE_TOKENS = 512
ROWS_DEV = 1
QUERY_PER_KEY = 4
CORPUS_TOKENS = 262144
NBLOCKS = 64
TOPK = 16
QUESTION_ROWS = 512
N_SX = 32
N_SY = 16


def draw_keys(key, part):
    key = jax.random.fold_in(key, 1)
    sampled_values = jnp.clip(jax.random.normal(key, (CORPUS_TOKENS, KEY_HEADS * HEAD_WIDTH), jnp.float32), -5.0, 5.0)
    return sampled_values.astype(jnp.bfloat16)


def draw_queries(key, part):
    key = jax.random.fold_in(key, 2)
    sampled_values = jnp.clip(jax.random.normal(key, (QUESTION_ROWS, QUERY_HEADS * HEAD_WIDTH), jnp.float32), -5.0, 5.0)
    return sampled_values.astype(jnp.bfloat16)


def draw_block_ids(key, part):
    key = jax.random.fold_in(key, 3)
    block_count = NBLOCKS
    col_rows = ROWS_DEV * N_SX
    perm_count = col_rows * TOPK // block_count
    scores = jax.random.randint(key, (N_SY, perm_count, block_count), 0, 1 << 20, dtype=jnp.int32)
    sort_order = jnp.argsort(scores * block_count + jnp.arange(block_count, dtype=jnp.int32), axis=-1).astype(jnp.int32)
    selected_blocks = sort_order.reshape(N_SY, col_rows, TOPK)
    mix_key = jax.random.fold_in(key, 4)
    mixing = jax.random.randint(mix_key, (N_SY, col_rows), 0, 1 << 20, dtype=jnp.int32)
    shuffle = jnp.argsort(mixing * col_rows + jnp.arange(col_rows, dtype=jnp.int32), axis=-1).astype(jnp.int32)
    selected_blocks = jnp.take_along_axis(selected_blocks, shuffle[:, :, None], axis=1)
    selected_blocks = selected_blocks.reshape(N_SY, N_SX, ROWS_DEV, TOPK).transpose(1, 0, 2, 3).reshape(QUESTION_ROWS, TOPK)
    return selected_blocks.astype(jnp.int32)


def block_levels(own_key, shape, pieces, smallest, largest):
    gain, own = 1.0, jax.random.fold_in(own_key, 6)
    for axis_at, blocks in pieces:
        steps = jnp.exp(jax.random.uniform(jax.random.fold_in(own, axis_at), (blocks,), jnp.float32, smallest / len(pieces), largest / len(pieces)))
        gain = gain * jnp.repeat(steps, shape[axis_at] // blocks).reshape([-1 if axis == axis_at else 1 for axis in range(len(shape))])
    return gain


def noise(stream_key, dims, deviation, bound, cuts=(), kind=jnp.bfloat16):
    array = deviation * jax.random.normal(stream_key, dims, jnp.float32)
    if cuts:
        array = array * block_levels(stream_key, dims, cuts, -0.22, 0.18)
    return jnp.clip(array, -bound, bound).astype(kind)


def setup_inputs(seed: int = 0) -> dict:
    arg_keys = jax.random.split(jax.random.key(seed), 5)
    queries = draw_queries(jax.random.fold_in(arg_keys[4], 71), 0)
    keys = draw_keys(jax.random.fold_in(arg_keys[4], 71), 0)
    values = noise(arg_keys[2], (CORPUS_TOKENS, KEY_HEADS * HEAD_WIDTH), 1.0, 6.0, ((0, 512),))
    block_ids = draw_block_ids(jax.random.fold_in(arg_keys[4], 71), 0)
    return {"queries": queries, "keys": keys, "values": values, "block_ids": block_ids}


def reference(queries, keys, values, block_ids):
    score_scale = HEAD_WIDTH ** -0.5
    block_scores = QUESTION_ROWS * TOPK // NBLOCKS
    device_parts = BLOCK // DEVICE_TOKENS
    row_index = jnp.arange(QUESTION_ROWS, dtype=jnp.int32)

    def visit_block(running, block_num):
        run_max, run_total, run_numer = running
        named_rows = jnp.any(block_ids == block_num, axis=1)
        ranked = jnp.where(named_rows, 0, QUESTION_ROWS).astype(jnp.int32) + row_index
        sort_order = jnp.argsort(ranked)[:block_scores].astype(jnp.int32)
        selected_blocks = queries[sort_order].astype(jnp.float32).reshape(block_scores, KEY_HEADS, QUERY_PER_KEY, HEAD_WIDTH)
        first_token = (block_num * BLOCK).astype(jnp.int32)
        block_keys = lax.dynamic_slice_in_dim(keys, first_token, BLOCK, 0).astype(jnp.float32)
        block_keys = block_keys.reshape(device_parts, DEVICE_TOKENS, KEY_HEADS, HEAD_WIDTH)
        block_values = lax.dynamic_slice_in_dim(values, first_token, BLOCK, 0).astype(jnp.float32)
        block_values = block_values.reshape(device_parts, DEVICE_TOKENS, KEY_HEADS, HEAD_WIDTH)
        score = jnp.einsum('rhgd,pshd->rhgps', selected_blocks, block_keys) * score_scale
        slab_max = jnp.max(score, axis=-1)
        weights = jnp.exp(score - slab_max[..., None])
        device_total = jnp.sum(weights, axis=-1)
        weights_bf = lax.optimization_barrier(weights.astype(jnp.bfloat16)).astype(jnp.float32)
        slab_out = jnp.einsum('rhgps,pshd->rhgpd', weights_bf, block_values)
        old_max = run_max[sort_order]
        new_max = jnp.maximum(old_max, jnp.max(slab_max, axis=-1))
        old_factor = jnp.exp(old_max - new_max)
        slab_factor = jnp.exp(slab_max - new_max[..., None])
        new_total = run_total[sort_order] * old_factor + jnp.sum(device_total * slab_factor, axis=-1)
        new_numer = run_numer[sort_order] * old_factor[..., None] + jnp.sum(slab_out * slab_factor[..., None], axis=-2)
        run_max = run_max.at[sort_order].set(new_max)
        run_total = run_total.at[sort_order].set(new_total)
        run_numer = run_numer.at[sort_order].set(new_numer)
        return (run_max, run_total, run_numer), None

    initial_state = (jnp.full((QUESTION_ROWS, KEY_HEADS, QUERY_PER_KEY), -1e30, jnp.float32),
                   jnp.zeros((QUESTION_ROWS, KEY_HEADS, QUERY_PER_KEY), jnp.float32),
                   jnp.zeros((QUESTION_ROWS, KEY_HEADS, QUERY_PER_KEY, HEAD_WIDTH), jnp.float32))
    final_state, _ = lax.scan(visit_block, initial_state, jnp.arange(NBLOCKS, dtype=jnp.int32))
    run_max, run_total, run_numer = final_state
    attended = run_numer / run_total[..., None]
    return attended.reshape(QUESTION_ROWS, QUERY_HEADS * HEAD_WIDTH).astype(jnp.bfloat16)
```

```python
import functools

import jax
import jax.numpy as jnp
from jax import lax
from jax.experimental import pallas as pl
from jax.experimental.pallas import tpu as pltpu
from jax.sharding import PartitionSpec as P

QUERY_HEADS = 32
KEY_HEADS = 8
HEAD_WIDTH = 128
BLOCK = 4096
QUERY_PER_KEY = 4
LOG2E = 1.4426950408889634
NEVER = -1e30

HG = 16
FEAT = 256
SLOTS = 8
STAT = 128


def pieces(x):
    hi = x.astype(jnp.bfloat16)
    rest = x - hi.astype(jnp.float32)
    mid = rest.astype(jnp.bfloat16)
    lo = (rest - mid.astype(jnp.float32)).astype(jnp.bfloat16)
    return hi, mid, lo


def slot_onehot(pos, rows, dtype):
    shape = (HG * SLOTS, rows * HG)
    r = lax.broadcasted_iota(jnp.int32, shape, 0)
    c = lax.broadcasted_iota(jnp.int32, shape, 1)
    hit = (pos == r % SLOTS) & (r // SLOTS == c % HG)
    return jnp.where(hit, 1.0, 0.0).astype(dtype)


def select_kernel(pos_ref, q_ref, out_ref):
    rows = q_ref.shape[0] // HG
    q = q_ref[...]
    for p in range(2):
        hot = slot_onehot(pos_ref[p : p + 1, :], rows, jnp.bfloat16)
        picked = jnp.dot(hot, q, preferred_element_type=jnp.float32).astype(jnp.bfloat16)
        for s in range(8):
            out_ref[p * 8 + s] = picked


def attend_kernel(x_ref, k_ref, v_ref, y_ref):
    scale = HEAD_WIDTH ** (-0.5) * LOG2E
    cols = x_ref.shape[0]
    rows = cols * HG
    lane = lax.broadcasted_iota(jnp.int32, (rows, HEAD_WIDTH), 1)
    stats = jnp.zeros((rows, HEAD_WIDTH), jnp.float32)
    for h in range(KEY_HEADS):
        k = k_ref[:, h * HEAD_WIDTH : (h + 1) * HEAD_WIDTH]
        v = v_ref[:, h * HEAD_WIDTH : (h + 1) * HEAD_WIDTH]
        for gl in range(2):
            q = x_ref[:, h * HG : (h + 1) * HG, gl * HEAD_WIDTH : (gl + 1) * HEAD_WIDTH]
            q = q.reshape(rows, HEAD_WIDTH)
            s = lax.dot_general(q, k, (((1,), (1,)), ((), ())), preferred_element_type=jnp.float32)
            m = jnp.max(s, axis=1, keepdims=True)
            w = jnp.exp2((s - m) * scale)
            total = jnp.sum(w, axis=1, keepdims=True)
            o = jnp.dot(w.astype(jnp.bfloat16), v, preferred_element_type=jnp.float32)
            o = (o / total).astype(jnp.bfloat16).reshape(cols, HG, HEAD_WIDTH)
            y_ref[:, h * HG : (h + 1) * HG, gl * HEAD_WIDTH : (gl + 1) * HEAD_WIDTH] = o
            stats = jnp.where(lane == h * 2 + gl, m * scale + jnp.log2(total), stats)
    hi, mid, lo = pieces(stats)
    base = KEY_HEADS * HG
    both = hi.astype(jnp.float32) + pltpu.roll(mid.astype(jnp.float32), 16, 1)
    y_ref[:, base : base + HG, :HEAD_WIDTH] = both.astype(jnp.bfloat16).reshape(cols, HG, HEAD_WIDTH)
    y_ref[:, base : base + HG, HEAD_WIDTH:] = lo.reshape(cols, HG, HEAD_WIDTH)


def merge_kernel(pos_ref, y_ref, out_ref):
    rows = pos_ref.shape[1] // HG
    base = KEY_HEADS * HG
    lane = lax.broadcasted_iota(jnp.int32, (HG, HEAD_WIDTH), 1)
    dense, lse = [], []
    for p in range(2):
        stat = []
        for s in range(8):
            first = y_ref[p * 8 + s, base : base + HG, :HEAD_WIDTH].astype(jnp.float32)
            lo = y_ref[p * 8 + s, base : base + HG, HEAD_WIDTH:].astype(jnp.float32)
            mid = pltpu.roll(first, HEAD_WIDTH - 16, 1)
            stat.append(jnp.where(lane < 16, first + (mid + lo), 0.0))
        top = functools.reduce(jnp.maximum, stat)
        weight = [jnp.exp2(x - top) for x in stat]
        total = functools.reduce(jnp.add, weight)
        inverse = 1.0 / total
        weight = [w * inverse for w in weight]
        block_lse = top + jnp.log2(total)
        heads = []
        for h in range(KEY_HEADS):
            halves = []
            for gl in range(2):
                at = h * 2 + gl
                acc = None
                for s in range(8):
                    x = y_ref[p * 8 + s, h * HG : (h + 1) * HG, gl * HEAD_WIDTH : (gl + 1) * HEAD_WIDTH]
                    x = x.astype(jnp.float32) * weight[s][:, at : at + 1]
                    acc = x if acc is None else acc + x
                halves.append(acc)
            heads.append(jnp.concatenate(halves, axis=1))
        block_out = jnp.concatenate(heads, axis=0)
        hot = slot_onehot(pos_ref[p : p + 1, :], rows, jnp.float32)
        flip = (((0,), (0,)), ((), ()))
        dense.append(
            lax.dot_general(hot, block_out, flip, precision=lax.Precision.HIGHEST, preferred_element_type=jnp.float32)
        )
        tall = jnp.concatenate([block_lse] * KEY_HEADS, axis=0)
        r = lax.broadcasted_iota(jnp.int32, tall.shape, 0)
        c = lax.broadcasted_iota(jnp.int32, tall.shape, 1)
        tall = jnp.where(c == 16, 1.0, jnp.where(c // 2 == r // HG, tall, 0.0))
        moved = lax.dot_general(
            hot, tall, flip, precision=lax.Precision.HIGHEST, preferred_element_type=jnp.float32
        )
        wide = lax.broadcasted_iota(jnp.int32, moved.shape, 1)
        named = moved[:, 16:17] > 0.5
        lse.append(
            [
                jnp.where(
                    named,
                    jnp.sum(jnp.where((wide < 16) & (wide % 2 == gl), moved, 0.0), axis=1, keepdims=True),
                    NEVER,
                )
                for gl in range(2)
            ]
        )
    combine_two(dense, lse, out_ref, rows)


def combine_two(data, lse, out_ref, rows):
    shape = out_ref.shape[:-1]
    ends = []
    for gl in range(2):
        a, b = lse[0][gl], lse[1][gl]
        top = jnp.maximum(a, b)
        wa, wb = jnp.exp2(a - top), jnp.exp2(b - top)
        total = wa + wb
        inverse = 1.0 / total
        lanes = slice(gl * HEAD_WIDTH, (gl + 1) * HEAD_WIDTH)
        mixed = data[0][:, lanes] * (wa * inverse) + data[1][:, lanes] * (wb * inverse)
        out_ref[..., lanes] = mixed.reshape(*shape, HEAD_WIDTH).astype(out_ref.dtype)
        ends.append(top + jnp.log2(total))
    lane = lax.broadcasted_iota(jnp.int32, (mixed.shape[0], STAT), 1)
    if out_ref.dtype == jnp.float32:
        stat = jnp.where(lane == 0, ends[0], jnp.where(lane == 1, ends[1], 0.0))
    else:
        stat = jnp.zeros(lane.shape, jnp.float32)
        for gl in range(2):
            for k, piece in enumerate(pieces(ends[gl])):
                stat = jnp.where(lane == gl * 3 + k, piece.astype(jnp.float32), stat)
    out_ref[..., FEAT:] = stat.reshape(*shape, STAT).astype(out_ref.dtype)


def pair_kernel(a_ref, out_ref):
    rows = a_ref.shape[1]
    data = [a_ref[c, :, :FEAT] for c in range(2)]
    lse = [[a_ref[c, :, FEAT + gl : FEAT + gl + 1] for gl in range(2)] for c in range(2)]
    combine_two(data, lse, out_ref, rows)


def last_kernel(a_ref, out_ref):
    for gl in range(2):
        lse = functools.reduce(
            jnp.add, [a_ref[:, :, FEAT + gl * 3 + k : FEAT + gl * 3 + k + 1].astype(jnp.float32) for k in range(3)]
        )
        weight = jnp.exp2(lse - jnp.max(lse, axis=0, keepdims=True))
        total = jnp.sum(weight, axis=0)
        lanes = slice(gl * HEAD_WIDTH, (gl + 1) * HEAD_WIDTH)
        mixed = jnp.sum(a_ref[:, :, lanes].astype(jnp.float32) * weight, axis=0) / total
        out_ref[:, lanes] = mixed.astype(jnp.bfloat16)


def call(kernel, shape, dtype, name, *args):
    return pl.pallas_call(
        kernel,
        out_shape=jax.ShapeDtypeStruct(shape, dtype),
        in_specs=[pl.BlockSpec(memory_space=pltpu.VMEM)] * len(args),
        out_specs=pl.BlockSpec(memory_space=pltpu.VMEM),
        compiler_params=pltpu.CompilerParams(vmem_limit_bytes=32 * 1024 * 1024),
        name=name,
    )(*args)


def per_device(queries, keys, values, block_ids):
    count_x = lax.axis_size("sx")
    count_y = lax.axis_size("sy")
    index_x = lax.axis_index("sx")
    index_y = lax.axis_index("sy")
    count_z = count_x // 2
    cores = [[2 * z, 2 * z + 1] for z in range(count_z)]
    along_z = [[2 * z + c for z in range(count_z)] for c in range(2)]

    def exchange(x, axis, groups=None):
        return lax.all_to_all(x, axis, split_axis=0, concat_axis=0, tiled=True, axis_index_groups=groups)

    column = lax.dynamic_index_in_dim(block_ids.reshape(count_x, count_y, -1), index_y, 1, keepdims=False)
    wanted = index_x * 2 + jnp.arange(2, dtype=jnp.int32)
    named = jnp.any(column[None] == wanted[:, None, None], axis=2)
    before = jnp.arange(count_x)[None, :] < jnp.arange(count_x)[:, None]
    rank = jnp.sum((named[:, None, :] & before[None]).astype(jnp.int32), axis=2)
    pos = jnp.where(named, rank, -1)
    pos = pos.reshape(2, count_z, 2).transpose(0, 2, 1)
    pos = jnp.repeat(pos.reshape(2, count_x), HG, axis=1)

    own = queries.reshape(1, HG, FEAT)
    got = exchange(jnp.broadcast_to(own, (count_z, HG, FEAT)), "sx", along_z)
    got = got.reshape(1, count_z * HG, FEAT)
    got = exchange(jnp.broadcast_to(got, (2, count_z * HG, FEAT)), "sx", cores)
    q_column = got.reshape(count_x * HG, FEAT)
    asked = call(select_kernel, (count_y, HG * SLOTS, FEAT), jnp.bfloat16, "select", pos, q_column)
    asked = exchange(asked, "sy")
    slab = call(attend_kernel, (count_y, HG * SLOTS + HG, FEAT), jnp.bfloat16, "attend", asked, keys, values)
    slab = exchange(slab, "sy")
    dense = call(merge_kernel, (2, count_z * HG, FEAT + STAT), jnp.float32, "merge", pos, slab)
    dense = exchange(dense, "sx", cores)
    chip = call(pair_kernel, (count_z, HG, FEAT + STAT), jnp.bfloat16, "pair", dense)
    chip = exchange(chip, "sx", along_z)
    out = call(last_kernel, (HG, FEAT), jnp.bfloat16, "last", chip)
    return out.reshape(1, HG * FEAT)


def solution(mesh):
    return jax.shard_map(
        per_device,
        mesh=mesh,
        in_specs=(P(("sx", "sy"), None), P(("sx", "sy"), None), P(("sx", "sy"), None), P()),
        out_specs=P(("sx", "sy"), None),
        check_vma=False,
    )
```

```python
import functools

import jax
import jax.numpy as jnp
from jax import lax
from jax.experimental import pallas as pl
from jax.experimental.pallas import tpu as pltpu
from jax.sharding import PartitionSpec as P

QUERY_HEADS = 32
KEY_HEADS = 8
HEAD_WIDTH = 128
BLOCK = 4096
QUERY_PER_KEY = 4
LOG2E = 1.4426950408889634
NEVER = -1e30

FEAT = QUERY_PER_KEY * HEAD_WIDTH
STAT = 128
ONE_LANE = 12
SLOTS = 8


def pieces(x):
    hi = x.astype(jnp.bfloat16).astype(jnp.float32)
    rest = x - hi
    mid = rest.astype(jnp.bfloat16).astype(jnp.float32)
    return hi, mid, rest - mid


def stat_lanes(lse):
    lane = lax.broadcasted_iota(jnp.int32, (lse[0].shape[0], STAT), 1)
    stat = jnp.where(lane == ONE_LANE, 1.0, 0.0)
    for g in range(QUERY_PER_KEY):
        for k, piece in enumerate(pieces(lse[g])):
            stat = jnp.where(lane == g * 3 + k, piece, stat)
    return stat


def slot_onehot(pos):
    shape = (KEY_HEADS * SLOTS, pos.shape[1])
    r = lax.broadcasted_iota(jnp.int32, shape, 0)
    c = lax.broadcasted_iota(jnp.int32, shape, 1)
    hit = (pos == r % SLOTS) & (r // SLOTS == c % KEY_HEADS)
    return jnp.where(hit, 1.0, 0.0).astype(jnp.bfloat16)


def relay_kernel(k_ref, v_ref, out_ref):
    tokens = k_ref.shape[0]
    for h in range(KEY_HEADS):
        lanes = slice(h * HEAD_WIDTH, (h + 1) * HEAD_WIDTH)
        out_ref[h, :tokens] = k_ref[:, lanes]
        out_ref[h, tokens:] = v_ref[:, lanes]


def select_kernel(pos_ref, q_ref, out_ref):
    q = q_ref[...].astype(jnp.float32).reshape(-1, FEAT).astype(jnp.bfloat16)
    for b in range(4):
        hot = slot_onehot(pos_ref[b : b + 1, :])
        picked = jnp.dot(hot, q, preferred_element_type=jnp.float32)
        picked = picked.reshape(KEY_HEADS, SLOTS, FEAT).astype(jnp.bfloat16)
        out_ref[b * KEY_HEADS : (b + 1) * KEY_HEADS] = picked


def attend_kernel(x_ref, kv_ref, y_ref):
    scale = HEAD_WIDTH ** (-0.5) * LOG2E
    columns = x_ref.shape[0] // 2
    tokens = kv_ref.shape[1] // 2
    rows = columns * SLOTS
    lse = []
    for g in range(QUERY_PER_KEY):
        lanes = slice(g * HEAD_WIDTH, (g + 1) * HEAD_WIDTH)
        q = x_ref[:columns, :, lanes].astype(jnp.float32) + x_ref[columns:, :, lanes].astype(jnp.float32)
        q = q.reshape(rows, HEAD_WIDTH).astype(jnp.bfloat16)
        tops, totals, sums = [], [], []
        for slab in range(kv_ref.shape[0]):
            k = kv_ref[slab, :tokens]
            v = kv_ref[slab, tokens:]
            s = lax.dot_general(q, k, (((1,), (1,)), ((), ())), preferred_element_type=jnp.float32)
            m = jnp.max(s, axis=1, keepdims=True)
            w = jnp.exp2((s - m) * scale)
            tops.append(m)
            totals.append(jnp.sum(w, axis=1, keepdims=True))
            sums.append(jnp.dot(w.astype(jnp.bfloat16), v, preferred_element_type=jnp.float32))
        top = functools.reduce(jnp.maximum, tops)
        weights = [jnp.exp2((m - top) * scale) for m in tops]
        total = functools.reduce(jnp.add, [w * t for w, t in zip(weights, totals)])
        out = functools.reduce(jnp.add, [w * o for w, o in zip(weights, sums)]) / total
        out = out.reshape(columns, SLOTS, HEAD_WIDTH).astype(jnp.bfloat16)
        y_ref[:columns, :, lanes] = out
        y_ref[columns:, :, lanes] = out
        lse.append(top * scale + jnp.log2(total))
    stat = stat_lanes(lse).reshape(columns, SLOTS, STAT).astype(jnp.bfloat16)
    y_ref[:columns, :, FEAT:] = stat
    y_ref[columns:, :, FEAT:] = stat


def merge_kernel(pos_ref, y_ref, out_ref):
    flip = (((0,), (0,)), ((), ()))
    parts = []
    for b in range(4):
        y = y_ref[b * KEY_HEADS : (b + 1) * KEY_HEADS].astype(jnp.float32)
        y = y.reshape(KEY_HEADS * SLOTS, FEAT + STAT).astype(jnp.bfloat16)
        hot = slot_onehot(pos_ref[b : b + 1, :])
        parts.append(lax.dot_general(hot, y, flip, preferred_element_type=jnp.float32))
    named = [x[:, FEAT + ONE_LANE : FEAT + ONE_LANE + 1] > 0.5 for x in parts]
    shape = out_ref.shape[:-1]
    ends = []
    for g in range(QUERY_PER_KEY):
        lanes = slice(g * HEAD_WIDTH, (g + 1) * HEAD_WIDTH)
        at = FEAT + 3 * g
        lse = [
            jnp.where(n, x[:, at : at + 1] + (x[:, at + 1 : at + 2] + x[:, at + 2 : at + 3]), NEVER)
            for n, x in zip(named, parts)
        ]
        top = functools.reduce(jnp.maximum, lse)
        weights = [jnp.exp2(x - top) for x in lse]
        total = functools.reduce(jnp.add, weights)
        out = functools.reduce(jnp.add, [w * x[:, lanes] for w, x in zip(weights, parts)]) / total
        out_ref[:, :, lanes] = out.reshape(*shape, HEAD_WIDTH).astype(jnp.bfloat16)
        ends.append(top + jnp.log2(total))
    out_ref[:, :, FEAT:] = stat_lanes(ends).reshape(*shape, STAT).astype(jnp.bfloat16)


def last_kernel(a_ref, out_ref):
    for g in range(QUERY_PER_KEY):
        at = FEAT + 3 * g
        lse = [a_ref[:, :, at + k : at + k + 1].astype(jnp.float32) for k in range(3)]
        lse = lse[0] + (lse[1] + lse[2])
        weight = jnp.exp2(lse - jnp.max(lse, axis=0, keepdims=True))
        total = jnp.sum(weight, axis=0)
        lanes = slice(g * HEAD_WIDTH, (g + 1) * HEAD_WIDTH)
        mixed = jnp.sum(a_ref[:, :, lanes].astype(jnp.float32) * weight, axis=0) / total
        out_ref[:, lanes] = mixed.astype(jnp.bfloat16)


def call(kernel, shape, dtype, name, *args):
    return pl.pallas_call(
        kernel,
        out_shape=jax.ShapeDtypeStruct(shape, dtype),
        in_specs=[pl.BlockSpec(memory_space=pltpu.VMEM)] * len(args),
        out_specs=pl.BlockSpec(memory_space=pltpu.VMEM),
        compiler_params=pltpu.CompilerParams(vmem_limit_bytes=40 * 1024 * 1024),
        name=name,
    )(*args)


def per_device(queries, keys, values, block_ids):
    count_x = lax.axis_size("sx")
    count_y = lax.axis_size("sy")
    index_x = lax.axis_index("sx")
    index_y = lax.axis_index("sy")
    count_z = count_x // 2
    index_z, core = index_x // 2, index_x % 2
    tokens = keys.shape[0]
    slabs = BLOCK // tokens
    along_z = [[2 * z + c for z in range(count_z)] for c in range(2)]
    block_devices = [list(range(start, start + slabs)) for start in range(0, count_y, slabs)]
    plane = 2 * count_y
    planes = [list(range(z * plane, (z + 1) * plane)) for z in range(count_z)]

    def exchange(x, axis, groups):
        return lax.all_to_all(x, axis, split_axis=0, concat_axis=0, tiled=True, axis_index_groups=groups)

    column = lax.dynamic_index_in_dim(block_ids.reshape(count_x, count_y, -1), index_y, 1, keepdims=False)
    wanted = index_z * 4 + jnp.arange(4, dtype=jnp.int32)
    named = jnp.any(column[None] == wanted[:, None, None], axis=2)
    before = jnp.arange(count_x)[None, :] < jnp.arange(count_x)[:, None]
    rank = jnp.sum((named[:, None, :] & before[None]).astype(jnp.int32), axis=2)
    pos = jnp.where(named, rank, -1).reshape(4, count_z, 2)
    pos = lax.dynamic_index_in_dim(pos, core, 2, keepdims=False)
    pos = jnp.repeat(pos, KEY_HEADS, axis=1)

    rows = lax.all_gather(queries.reshape(KEY_HEADS, FEAT), "sx", axis=0, axis_index_groups=along_z)
    kv = call(relay_kernel, (KEY_HEADS, 2 * tokens, HEAD_WIDTH), jnp.bfloat16, "relay", keys, values)
    kv = exchange(kv, "sy", block_devices)
    asked = call(select_kernel, (plane, SLOTS, FEAT), jnp.bfloat16, "select", pos, rows)
    asked = exchange(asked, ("sx", "sy"), planes)
    part = call(attend_kernel, (plane, SLOTS, FEAT + STAT), jnp.bfloat16, "attend", asked, kv)
    part = exchange(part, ("sx", "sy"), planes)
    part = call(merge_kernel, (count_z, KEY_HEADS, FEAT + STAT), jnp.bfloat16, "merge", pos, part)
    part = exchange(part, "sx", along_z)
    out = call(last_kernel, (KEY_HEADS, FEAT), jnp.bfloat16, "last", part)
    return out.reshape(1, KEY_HEADS * FEAT)


def solution(mesh):
    return jax.shard_map(
        per_device,
        mesh=mesh,
        in_specs=(P(("sx", "sy"), None), P(("sx", "sy"), None), P(("sx", "sy"), None), P()),
        out_specs=P(("sx", "sy"), None),
        check_vma=False,
    )
```

```python
import functools

import jax
import jax.numpy as jnp
from jax import lax
from jax.experimental import pallas as pl
from jax.experimental.pallas import tpu as pltpu
from jax.sharding import PartitionSpec as P

QUERY_HEADS = 32
KEY_HEADS = 8
HEAD_WIDTH = 128
BLOCK = 4096
QUERY_PER_KEY = 4
LOG2E = 1.4426950408889634
NEVER = -1e30

FEAT = QUERY_PER_KEY * HEAD_WIDTH
STAT = 128
ONE_LANE = 12
SLOTS = 8


def pieces(x):
    hi = x.astype(jnp.bfloat16).astype(jnp.float32)
    rest = x - hi
    mid = rest.astype(jnp.bfloat16).astype(jnp.float32)
    return hi, mid, rest - mid


def stat_lanes(lse):
    lane = lax.broadcasted_iota(jnp.int32, (lse[0].shape[0], STAT), 1)
    stat = jnp.where(lane == ONE_LANE, 1.0, 0.0)
    for g in range(QUERY_PER_KEY):
        for k, piece in enumerate(pieces(lse[g])):
            stat = jnp.where(lane == g * 3 + k, piece, stat)
    return stat


def slot_onehot(pos):
    shape = (KEY_HEADS * SLOTS, pos.shape[1])
    r = lax.broadcasted_iota(jnp.int32, shape, 0)
    c = lax.broadcasted_iota(jnp.int32, shape, 1)
    hit = (pos == r % SLOTS) & (r // SLOTS == c % KEY_HEADS)
    return jnp.where(hit, 1.0, 0.0).astype(jnp.bfloat16)


def relay_kernel(k_ref, v_ref, out_ref):
    tokens = k_ref.shape[0]
    for h in range(KEY_HEADS):
        lanes = slice(h * HEAD_WIDTH, (h + 1) * HEAD_WIDTH)
        out_ref[h, :tokens] = k_ref[:, lanes]
        out_ref[h, tokens:] = v_ref[:, lanes]


def select_kernel(pos_ref, q_ref, out_ref):
    q = q_ref[...].astype(jnp.float32).reshape(-1, FEAT).astype(jnp.bfloat16)
    for b in range(4):
        hot = slot_onehot(pos_ref[b : b + 1, :])
        picked = jnp.dot(hot, q, preferred_element_type=jnp.float32)
        picked = picked.reshape(KEY_HEADS, SLOTS, FEAT).astype(jnp.bfloat16)
        out_ref[b * KEY_HEADS : (b + 1) * KEY_HEADS] = picked


def attend_kernel(x_ref, kv_ref, y_ref):
    scale = HEAD_WIDTH ** (-0.5) * LOG2E
    columns = x_ref.shape[0] // 2
    tokens = kv_ref.shape[1] // 2
    rows = columns * SLOTS
    lse = []
    for g in range(QUERY_PER_KEY):
        lanes = slice(g * HEAD_WIDTH, (g + 1) * HEAD_WIDTH)
        q = x_ref[:columns, :, lanes].astype(jnp.float32) + x_ref[columns:, :, lanes].astype(jnp.float32)
        q = q.reshape(rows, HEAD_WIDTH).astype(jnp.bfloat16)
        tops, totals, sums = [], [], []
        for slab in range(kv_ref.shape[0]):
            k = kv_ref[slab, :tokens]
            v = kv_ref[slab, tokens:]
            s = lax.dot_general(q, k, (((1,), (1,)), ((), ())), preferred_element_type=jnp.float32)
            m = jnp.max(s, axis=1, keepdims=True)
            w = jnp.exp2((s - m) * scale)
            tops.append(m)
            totals.append(jnp.sum(w, axis=1, keepdims=True))
            sums.append(jnp.dot(w.astype(jnp.bfloat16), v, preferred_element_type=jnp.float32))
        top = functools.reduce(jnp.maximum, tops)
        weights = [jnp.exp2((m - top) * scale) for m in tops]
        total = functools.reduce(jnp.add, [w * t for w, t in zip(weights, totals)])
        out = functools.reduce(jnp.add, [w * o for w, o in zip(weights, sums)]) / total
        out = out.reshape(columns, SLOTS, HEAD_WIDTH).astype(jnp.bfloat16)
        y_ref[:columns, :, lanes] = out
        y_ref[columns:, :, lanes] = out
        lse.append(top * scale + jnp.log2(total))
    stat = stat_lanes(lse).reshape(columns, SLOTS, STAT).astype(jnp.bfloat16)
    y_ref[:columns, :, FEAT:] = stat
    y_ref[columns:, :, FEAT:] = stat


def merge_kernel(pos_ref, y_ref, out_ref):
    flip = (((0,), (0,)), ((), ()))
    parts = []
    for b in range(4):
        y = y_ref[b * KEY_HEADS : (b + 1) * KEY_HEADS].astype(jnp.float32)
        y = y.reshape(KEY_HEADS * SLOTS, FEAT + STAT).astype(jnp.bfloat16)
        hot = slot_onehot(pos_ref[b : b + 1, :])
        parts.append(lax.dot_general(hot, y, flip, preferred_element_type=jnp.float32))
    named = [x[:, FEAT + ONE_LANE : FEAT + ONE_LANE + 1] > 0.5 for x in parts]
    shape = out_ref.shape[:-1]
    ends = []
    for g in range(QUERY_PER_KEY):
        lanes = slice(g * HEAD_WIDTH, (g + 1) * HEAD_WIDTH)
        at = FEAT + 3 * g
        lse = [
            jnp.where(n, x[:, at : at + 1] + (x[:, at + 1 : at + 2] + x[:, at + 2 : at + 3]), NEVER)
            for n, x in zip(named, parts)
        ]
        top = functools.reduce(jnp.maximum, lse)
        weights = [jnp.exp2(x - top) for x in lse]
        total = functools.reduce(jnp.add, weights)
        out = functools.reduce(jnp.add, [w * x[:, lanes] for w, x in zip(weights, parts)]) / total
        out_ref[:, :, lanes] = out.reshape(*shape, HEAD_WIDTH).astype(jnp.bfloat16)
        ends.append(top + jnp.log2(total))
    out_ref[:, :, FEAT:] = stat_lanes(ends).reshape(*shape, STAT).astype(jnp.bfloat16)


def last_kernel(a_ref, out_ref):
    for g in range(QUERY_PER_KEY):
        at = FEAT + 3 * g
        lse = [a_ref[:, :, at + k : at + k + 1].astype(jnp.float32) for k in range(3)]
        lse = lse[0] + (lse[1] + lse[2])
        weight = jnp.exp2(lse - jnp.max(lse, axis=0, keepdims=True))
        total = jnp.sum(weight, axis=0)
        lanes = slice(g * HEAD_WIDTH, (g + 1) * HEAD_WIDTH)
        mixed = jnp.sum(a_ref[:, :, lanes].astype(jnp.float32) * weight, axis=0) / total
        out_ref[:, lanes] = mixed.astype(jnp.bfloat16)


def call(kernel, shape, dtype, name, *args):
    return pl.pallas_call(
        kernel,
        out_shape=jax.ShapeDtypeStruct(shape, dtype),
        in_specs=[pl.BlockSpec(memory_space=pltpu.VMEM)] * len(args),
        out_specs=pl.BlockSpec(memory_space=pltpu.VMEM),
        compiler_params=pltpu.CompilerParams(vmem_limit_bytes=40 * 1024 * 1024),
        name=name,
    )(*args)


def per_device(queries, keys, values, block_ids):
    count_x = lax.axis_size("sx")
    count_y = lax.axis_size("sy")
    index_x = lax.axis_index("sx")
    index_y = lax.axis_index("sy")
    count_z = count_x // 2
    index_z, core = index_x // 2, index_x % 2
    tokens = keys.shape[0]
    slabs = BLOCK // tokens
    along_z = [[2 * z + c for z in range(count_z)] for c in range(2)]
    block_devices = [list(range(start, start + slabs)) for start in range(0, count_y, slabs)]
    plane = 2 * count_y
    planes = [list(range(z * plane, (z + 1) * plane)) for z in range(count_z)]

    def exchange(x, axis, groups):
        return lax.all_to_all(x, axis, split_axis=0, concat_axis=0, tiled=True, axis_index_groups=groups)

    column = lax.dynamic_index_in_dim(block_ids.reshape(count_x, count_y, -1), index_y, 1, keepdims=False)
    wanted = index_z * 4 + jnp.arange(4, dtype=jnp.int32)
    named = jnp.any(column[None] == wanted[:, None, None], axis=2)
    before = jnp.arange(count_x)[None, :] < jnp.arange(count_x)[:, None]
    rank = jnp.sum((named[:, None, :] & before[None]).astype(jnp.int32), axis=2)
    pos = jnp.where(named, rank, -1).reshape(4, count_z, 2)
    pos = lax.dynamic_index_in_dim(pos, core, 2, keepdims=False)
    pos = jnp.repeat(pos, KEY_HEADS, axis=1)

    rows = lax.all_gather(queries.reshape(KEY_HEADS, FEAT), "sx", axis=0, axis_index_groups=along_z)
    kv = call(relay_kernel, (KEY_HEADS, 2 * tokens, HEAD_WIDTH), jnp.bfloat16, "relay", keys, values)
    kv = exchange(kv, "sy", block_devices)
    rows, pos, kv = lax.optimization_barrier((rows, pos, kv))
    asked = call(select_kernel, (plane, SLOTS, FEAT), jnp.bfloat16, "select", pos, rows)
    asked = exchange(asked, ("sx", "sy"), planes)
    part = call(attend_kernel, (plane, SLOTS, FEAT + STAT), jnp.bfloat16, "attend", asked, kv)
    part = exchange(part, ("sx", "sy"), planes)
    part = call(merge_kernel, (count_z, KEY_HEADS, FEAT + STAT), jnp.bfloat16, "merge", pos, part)
    part = exchange(part, "sx", along_z)
    out = call(last_kernel, (KEY_HEADS, FEAT), jnp.bfloat16, "last", part)
    return out.reshape(1, KEY_HEADS * FEAT)


def solution(mesh):
    return jax.shard_map(
        per_device,
        mesh=mesh,
        in_specs=(P(("sx", "sy"), None), P(("sx", "sy"), None), P(("sx", "sy"), None), P()),
        out_specs=P(("sx", "sy"), None),
        check_vma=False,
    )
```

```python
import functools

import jax
import jax.numpy as jnp
from jax import lax
from jax.experimental import pallas as pl
from jax.experimental.pallas import tpu as pltpu
from jax.sharding import PartitionSpec as P

QUERY_HEADS = 32
KEY_HEADS = 8
HEAD_WIDTH = 128
BLOCK = 4096
QUERY_PER_KEY = 4
LOG2E = 1.4426950408889634
NEVER = -1e30

FEAT = QUERY_PER_KEY * HEAD_WIDTH
STAT = 128
ONE_LANE = 12
SLOTS = 8


def pieces(x):
    hi = x.astype(jnp.bfloat16).astype(jnp.float32)
    rest = x - hi
    mid = rest.astype(jnp.bfloat16).astype(jnp.float32)
    return hi, mid, rest - mid


def stat_lanes(lse):
    lane = lax.broadcasted_iota(jnp.int32, (lse[0].shape[0], STAT), 1)
    stat = jnp.where(lane == ONE_LANE, 1.0, 0.0)
    for g in range(QUERY_PER_KEY):
        for k, piece in enumerate(pieces(lse[g])):
            stat = jnp.where(lane == g * 3 + k, piece, stat)
    return stat


def slot_onehot(pos):
    shape = (KEY_HEADS * SLOTS, pos.shape[1])
    r = lax.broadcasted_iota(jnp.int32, shape, 0)
    c = lax.broadcasted_iota(jnp.int32, shape, 1)
    hit = (pos == r % SLOTS) & (r // SLOTS == c % KEY_HEADS)
    return jnp.where(hit, 1.0, 0.0).astype(jnp.bfloat16)


def relay_kernel(k_ref, v_ref, out_ref):
    tokens = k_ref.shape[0]
    for h in range(KEY_HEADS):
        lanes = slice(h * HEAD_WIDTH, (h + 1) * HEAD_WIDTH)
        out_ref[h, :tokens] = k_ref[:, lanes]
        out_ref[h, tokens:] = v_ref[:, lanes]


def by_head_kernel(x_ref, out_ref):
    n = x_ref.shape[0]
    rows = n // QUERY_PER_KEY
    r = lax.broadcasted_iota(jnp.int32, (n, n), 0)
    c = lax.broadcasted_iota(jnp.int32, (n, n), 1)
    hot = jnp.where((c % QUERY_PER_KEY == r // rows) & (c // QUERY_PER_KEY == r % rows), 1.0, 0.0)
    x = jnp.dot(hot.astype(jnp.bfloat16), x_ref[...], preferred_element_type=jnp.float32)
    out_ref[...] = x.astype(jnp.bfloat16)


def attend_kernel(pos_ref, x_ref, kv_ref, y_ref):
    scale = HEAD_WIDTH ** (-0.5) * LOG2E
    columns = y_ref.shape[0] // 2
    tokens = kv_ref.shape[1] // 2
    rows = columns * SLOTS
    everyone = pos_ref.shape[1]
    r = lax.broadcasted_iota(jnp.int32, (rows, everyone), 0)
    c = lax.broadcasted_iota(jnp.int32, (rows, everyone), 1)
    hit = (pos_ref[...] == r % SLOTS) & (r // SLOTS == c % columns)
    hot = jnp.where(hit, 1.0, 0.0).astype(jnp.bfloat16)
    q = [
        jnp.dot(hot, x_ref[:, g].reshape(everyone, HEAD_WIDTH), preferred_element_type=jnp.float32)
        for g in range(QUERY_PER_KEY)
    ]
    q = jnp.concatenate([x.astype(jnp.bfloat16) for x in q], axis=0)
    ones = jnp.ones((tokens, HEAD_WIDTH), jnp.bfloat16)
    tops, sums = [], []
    for slab in range(kv_ref.shape[0]):
        k = kv_ref[slab, :tokens]
        v = jnp.concatenate([kv_ref[slab, tokens:], ones], axis=1)
        s = lax.dot_general(q, k, (((1,), (1,)), ((), ())), preferred_element_type=jnp.float32)
        m = jnp.max(s, axis=1, keepdims=True)
        w = jnp.exp2((s - m) * scale).astype(jnp.bfloat16)
        tops.append(m)
        sums.append(jnp.dot(w, v, preferred_element_type=jnp.float32))
    top = functools.reduce(jnp.maximum, tops)
    both = functools.reduce(jnp.add, [jnp.exp2((m - top) * scale) * x for m, x in zip(tops, sums)])
    total = both[:, HEAD_WIDTH:]
    out = both[:, :HEAD_WIDTH] / total
    lse = top * scale + jnp.log2(total[:, :1])
    ends = []
    for g in range(QUERY_PER_KEY):
        part = out[g * rows : (g + 1) * rows].reshape(columns, SLOTS, HEAD_WIDTH).astype(jnp.bfloat16)
        lanes = slice(g * HEAD_WIDTH, (g + 1) * HEAD_WIDTH)
        y_ref[:columns, :, lanes] = part
        y_ref[columns:, :, lanes] = part
        ends.append(lse[g * rows : (g + 1) * rows])
    stat = stat_lanes(ends).reshape(columns, SLOTS, STAT).astype(jnp.bfloat16)
    y_ref[:columns, :, FEAT:] = stat
    y_ref[columns:, :, FEAT:] = stat


def merge_kernel(pos_ref, y_ref, out_ref):
    flip = (((0,), (0,)), ((), ()))
    parts = []
    for b in range(4):
        y = y_ref[b * KEY_HEADS : (b + 1) * KEY_HEADS].astype(jnp.float32)
        y = y.reshape(KEY_HEADS * SLOTS, FEAT + STAT).astype(jnp.bfloat16)
        hot = slot_onehot(pos_ref[b : b + 1, :])
        parts.append(lax.dot_general(hot, y, flip, preferred_element_type=jnp.float32))
    named = [x[:, FEAT + ONE_LANE : FEAT + ONE_LANE + 1] > 0.5 for x in parts]
    shape = out_ref.shape[:-1]
    ends = []
    for g in range(QUERY_PER_KEY):
        lanes = slice(g * HEAD_WIDTH, (g + 1) * HEAD_WIDTH)
        at = FEAT + 3 * g
        lse = [
            jnp.where(n, x[:, at : at + 1] + (x[:, at + 1 : at + 2] + x[:, at + 2 : at + 3]), NEVER)
            for n, x in zip(named, parts)
        ]
        top = functools.reduce(jnp.maximum, lse)
        weights = [jnp.exp2(x - top) for x in lse]
        total = functools.reduce(jnp.add, weights)
        out = functools.reduce(jnp.add, [w * x[:, lanes] for w, x in zip(weights, parts)]) / total
        out_ref[:, :, lanes] = out.reshape(*shape, HEAD_WIDTH).astype(jnp.bfloat16)
        ends.append(top + jnp.log2(total))
    out_ref[:, :, FEAT:] = stat_lanes(ends).reshape(*shape, STAT).astype(jnp.bfloat16)


def last_kernel(a_ref, out_ref):
    for g in range(QUERY_PER_KEY):
        at = FEAT + 3 * g
        lse = [a_ref[:, :, at + k : at + k + 1].astype(jnp.float32) for k in range(3)]
        lse = lse[0] + (lse[1] + lse[2])
        weight = jnp.exp2(lse - jnp.max(lse, axis=0, keepdims=True))
        total = jnp.sum(weight, axis=0)
        lanes = slice(g * HEAD_WIDTH, (g + 1) * HEAD_WIDTH)
        mixed = jnp.sum(a_ref[:, :, lanes].astype(jnp.float32) * weight, axis=0) / total
        out_ref[:, lanes] = mixed.astype(jnp.bfloat16)


def call(kernel, shape, dtype, name, *args):
    return pl.pallas_call(
        kernel,
        out_shape=jax.ShapeDtypeStruct(shape, dtype),
        in_specs=[pl.BlockSpec(memory_space=pltpu.VMEM)] * len(args),
        out_specs=pl.BlockSpec(memory_space=pltpu.VMEM),
        compiler_params=pltpu.CompilerParams(vmem_limit_bytes=40 * 1024 * 1024),
        name=name,
    )(*args)


def per_device(queries, keys, values, block_ids):
    count_x = lax.axis_size("sx")
    count_y = lax.axis_size("sy")
    index_x = lax.axis_index("sx")
    index_y = lax.axis_index("sy")
    count_z = count_x // 2
    index_z, core = index_x // 2, index_x % 2
    tokens = keys.shape[0]
    slabs = BLOCK // tokens
    along_z = [[2 * z + c for z in range(count_z)] for c in range(2)]
    block_devices = [list(range(start, start + slabs)) for start in range(0, count_y, slabs)]
    plane = 2 * count_y
    planes = [list(range(z * plane, (z + 1) * plane)) for z in range(count_z)]

    def exchange(x, axis, groups):
        return lax.all_to_all(x, axis, split_axis=0, concat_axis=0, tiled=True, axis_index_groups=groups)

    def ranks(block_named):
        before = jnp.arange(count_x)[None, :] < jnp.arange(count_x)[:, None]
        rank = jnp.sum((block_named[:, None] & before[None, :, :, None]).astype(jnp.int32), axis=2)
        return jnp.where(block_named, rank, -1)

    ids = block_ids.reshape(1, count_x, count_y, -1)
    my_block = index_x * 2 + index_y // slabs
    pos_in = ranks(jnp.any(ids == my_block, axis=3)).reshape(1, count_x * count_y)
    column = lax.dynamic_slice_in_dim(ids, index_y, 1, 2)
    wanted = (index_z * 4 + jnp.arange(4, dtype=jnp.int32)).reshape(4, 1, 1, 1)
    pos_out = ranks(jnp.any(column == wanted, axis=3)).reshape(4, count_z, 2)
    pos_out = lax.dynamic_index_in_dim(pos_out, core, 2, keepdims=False)
    pos_out = jnp.repeat(pos_out, KEY_HEADS, axis=1)

    own = queries.reshape(1, KEY_HEADS, QUERY_PER_KEY, HEAD_WIDTH)
    own = jnp.broadcast_to(own, (4, KEY_HEADS, QUERY_PER_KEY, HEAD_WIDTH))
    slices = exchange(own.reshape(plane, QUERY_PER_KEY, HEAD_WIDTH), ("sx", "sy"), planes)
    kv = call(relay_kernel, (KEY_HEADS, 2 * tokens, HEAD_WIDTH), jnp.bfloat16, "relay", keys, values)
    slices, kv, pos_in, pos_out = lax.optimization_barrier((slices, kv, pos_in, pos_out))
    kv = exchange(kv, "sy", block_devices)
    slices = slices.reshape(plane * QUERY_PER_KEY, HEAD_WIDTH)
    slices = call(by_head_kernel, slices.shape, jnp.bfloat16, "by_head", slices)
    slices = slices.reshape(QUERY_PER_KEY, plane, HEAD_WIDTH)
    rows = lax.all_gather(slices, "sx", axis=0, axis_index_groups=along_z)
    part = call(attend_kernel, (plane, SLOTS, FEAT + STAT), jnp.bfloat16, "attend", pos_in, rows, kv)
    part = exchange(part, ("sx", "sy"), planes)
    part = call(merge_kernel, (count_z, KEY_HEADS, FEAT + STAT), jnp.bfloat16, "merge", pos_out, part)
    part = exchange(part, "sx", along_z)
    out = call(last_kernel, (KEY_HEADS, FEAT), jnp.bfloat16, "last", part)
    return out.reshape(1, KEY_HEADS * FEAT)


def solution(mesh):
    return jax.shard_map(
        per_device,
        mesh=mesh,
        in_specs=(P(("sx", "sy"), None), P(("sx", "sy"), None), P(("sx", "sy"), None), P()),
        out_specs=P(("sx", "sy"), None),
        check_vma=False,
    )
```

```python
import functools

import jax
import jax.numpy as jnp
from jax import lax
from jax.experimental import pallas as pl
from jax.experimental.pallas import tpu as pltpu
from jax.sharding import PartitionSpec as P

QUERY_HEADS = 32
KEY_HEADS = 8
HEAD_WIDTH = 128
BLOCK = 4096
QUERY_PER_KEY = 4
LOG2E = 1.4426950408889634
NEVER = -1e30

FEAT = QUERY_PER_KEY * HEAD_WIDTH
STAT = 128
ONE_LANE = 12
SLOTS = 8


def pieces(x):
    hi = x.astype(jnp.bfloat16).astype(jnp.float32)
    rest = x - hi
    mid = rest.astype(jnp.bfloat16).astype(jnp.float32)
    return hi, mid, rest - mid


def stat_lanes(lse):
    lane = lax.broadcasted_iota(jnp.int32, (lse[0].shape[0], STAT), 1)
    stat = jnp.where(lane == ONE_LANE, 1.0, 0.0)
    for g in range(QUERY_PER_KEY):
        for k, piece in enumerate(pieces(lse[g])):
            stat = jnp.where(lane == g * 3 + k, piece, stat)
    return stat


def slot_onehot(pos):
    shape = (KEY_HEADS * SLOTS, pos.shape[1])
    r = lax.broadcasted_iota(jnp.int32, shape, 0)
    c = lax.broadcasted_iota(jnp.int32, shape, 1)
    hit = (pos == r % SLOTS) & (r // SLOTS == c % KEY_HEADS)
    return jnp.where(hit, 1.0, 0.0).astype(jnp.bfloat16)


def relay_kernel(me_ref, k_ref, v_ref, *out_refs):
    tokens = k_ref.shape[0]
    for i, out_ref in enumerate(out_refs):
        head = jnp.bitwise_xor(me_ref[0], i)
        lanes = pl.ds(pl.multiple_of(head * HEAD_WIDTH, HEAD_WIDTH), HEAD_WIDTH)
        out_ref[:tokens] = k_ref[:, lanes]
        out_ref[tokens:] = v_ref[:, lanes]


def select_kernel(pos_ref, q_ref, out_ref):
    q = q_ref[...].astype(jnp.float32).reshape(-1, FEAT).astype(jnp.bfloat16)
    for b in range(4):
        hot = slot_onehot(pos_ref[b : b + 1, :])
        picked = jnp.dot(hot, q, preferred_element_type=jnp.float32)
        picked = picked.reshape(KEY_HEADS, SLOTS, FEAT).astype(jnp.bfloat16)
        out_ref[b * KEY_HEADS : (b + 1) * KEY_HEADS] = picked


def attend_kernel(x_ref, *refs):
    kv_refs, y_ref = refs[:-1], refs[-1]
    scale = HEAD_WIDTH ** (-0.5) * LOG2E
    columns = y_ref.shape[0] // 2
    tokens = kv_refs[0].shape[0] // 2
    rows = columns * SLOTS
    x = x_ref[:columns].astype(jnp.float32) + x_ref[columns:].astype(jnp.float32)
    x = x.reshape(rows, FEAT).astype(jnp.bfloat16)
    q = [x[:, g * HEAD_WIDTH : (g + 1) * HEAD_WIDTH] for g in range(QUERY_PER_KEY)]
    q = jnp.concatenate(q, axis=0)
    ones = jnp.ones((tokens, HEAD_WIDTH), jnp.bfloat16)
    tops, sums = [], []
    for kv_ref in kv_refs:
        k = kv_ref[:tokens]
        v = jnp.concatenate([kv_ref[tokens:], ones], axis=1)
        s = lax.dot_general(q, k, (((1,), (1,)), ((), ())), preferred_element_type=jnp.float32)
        m = jnp.max(s, axis=1, keepdims=True)
        w = jnp.exp2((s - m) * scale).astype(jnp.bfloat16)
        tops.append(m)
        sums.append(jnp.dot(w, v, preferred_element_type=jnp.float32))
    top = functools.reduce(jnp.maximum, tops)
    both = functools.reduce(jnp.add, [jnp.exp2((m - top) * scale) * x for m, x in zip(tops, sums)])
    total = both[:, HEAD_WIDTH:]
    out = both[:, :HEAD_WIDTH] / total
    lse = top * scale + jnp.log2(total[:, :1])
    ends = []
    for g in range(QUERY_PER_KEY):
        part = out[g * rows : (g + 1) * rows].reshape(columns, SLOTS, HEAD_WIDTH).astype(jnp.bfloat16)
        lanes = slice(g * HEAD_WIDTH, (g + 1) * HEAD_WIDTH)
        y_ref[:columns, :, lanes] = part
        y_ref[columns:, :, lanes] = part
        ends.append(lse[g * rows : (g + 1) * rows])
    stat = stat_lanes(ends).reshape(columns, SLOTS, STAT).astype(jnp.bfloat16)
    y_ref[:columns, :, FEAT:] = stat
    y_ref[columns:, :, FEAT:] = stat


def merge_kernel(pos_ref, y_ref, out_ref):
    flip = (((0,), (0,)), ((), ()))
    parts = []
    for b in range(4):
        y = y_ref[b * KEY_HEADS : (b + 1) * KEY_HEADS].astype(jnp.float32)
        y = y.reshape(KEY_HEADS * SLOTS, FEAT + STAT).astype(jnp.bfloat16)
        hot = slot_onehot(pos_ref[b : b + 1, :])
        parts.append(lax.dot_general(hot, y, flip, preferred_element_type=jnp.float32))
    named = [x[:, FEAT + ONE_LANE : FEAT + ONE_LANE + 1] > 0.5 for x in parts]
    shape = out_ref.shape[:-1]
    ends = []
    for g in range(QUERY_PER_KEY):
        lanes = slice(g * HEAD_WIDTH, (g + 1) * HEAD_WIDTH)
        at = FEAT + 3 * g
        lse = [
            jnp.where(n, x[:, at : at + 1] + (x[:, at + 1 : at + 2] + x[:, at + 2 : at + 3]), NEVER)
            for n, x in zip(named, parts)
        ]
        top = functools.reduce(jnp.maximum, lse)
        weights = [jnp.exp2(x - top) for x in lse]
        total = functools.reduce(jnp.add, weights)
        out = functools.reduce(jnp.add, [w * x[:, lanes] for w, x in zip(weights, parts)]) / total
        out_ref[:, :, lanes] = out.reshape(*shape, HEAD_WIDTH).astype(jnp.bfloat16)
        ends.append(top + jnp.log2(total))
    out_ref[:, :, FEAT:] = stat_lanes(ends).reshape(*shape, STAT).astype(jnp.bfloat16)


def last_kernel(a_ref, out_ref):
    for g in range(QUERY_PER_KEY):
        at = FEAT + 3 * g
        lse = [a_ref[:, :, at + k : at + k + 1].astype(jnp.float32) for k in range(3)]
        lse = lse[0] + (lse[1] + lse[2])
        weight = jnp.exp2(lse - jnp.max(lse, axis=0, keepdims=True))
        total = jnp.sum(weight, axis=0)
        lanes = slice(g * HEAD_WIDTH, (g + 1) * HEAD_WIDTH)
        mixed = jnp.sum(a_ref[:, :, lanes].astype(jnp.float32) * weight, axis=0) / total
        out_ref[:, lanes] = mixed.astype(jnp.bfloat16)


def call(kernel, shape, dtype, name, *args):
    return pl.pallas_call(
        kernel,
        out_shape=jax.ShapeDtypeStruct(shape, dtype),
        in_specs=[pl.BlockSpec(memory_space=pltpu.VMEM)] * len(args),
        out_specs=pl.BlockSpec(memory_space=pltpu.VMEM),
        compiler_params=pltpu.CompilerParams(vmem_limit_bytes=40 * 1024 * 1024),
        name=name,
    )(*args)


def per_device(queries, keys, values, block_ids):
    count_x = lax.axis_size("sx")
    count_y = lax.axis_size("sy")
    index_x = lax.axis_index("sx")
    index_y = lax.axis_index("sy")
    count_z = count_x // 2
    index_z, core = index_x // 2, index_x % 2
    tokens = keys.shape[0]
    slabs = BLOCK // tokens
    along_z = [[2 * z + c for z in range(count_z)] for c in range(2)]
    plane = 2 * count_y
    planes = [list(range(z * plane, (z + 1) * plane)) for z in range(count_z)]

    def exchange(x, axis, groups):
        return lax.all_to_all(x, axis, split_axis=0, concat_axis=0, tiled=True, axis_index_groups=groups)

    column = lax.dynamic_index_in_dim(block_ids.reshape(count_x, count_y, -1), index_y, 1, keepdims=False)
    wanted = index_z * 4 + jnp.arange(4, dtype=jnp.int32)
    named = jnp.any(column[None] == wanted[:, None, None], axis=2)
    before = jnp.arange(count_x)[None, :] < jnp.arange(count_x)[:, None]
    rank = jnp.sum((named[:, None, :] & before[None]).astype(jnp.int32), axis=2)
    pos = jnp.where(named, rank, -1).reshape(4, count_z, 2)
    pos = lax.dynamic_index_in_dim(pos, core, 2, keepdims=False)
    pos = jnp.repeat(pos, KEY_HEADS, axis=1)

    own = jnp.broadcast_to(queries.reshape(1, KEY_HEADS, FEAT), (count_z, KEY_HEADS, FEAT))
    rows = exchange(own, "sx", along_z)
    me = (index_y % slabs).astype(jnp.int32).reshape(1)
    vmem = pl.BlockSpec(memory_space=pltpu.VMEM)
    kv = pl.pallas_call(
        relay_kernel,
        out_shape=[jax.ShapeDtypeStruct((2 * tokens, HEAD_WIDTH), jnp.bfloat16)] * slabs,
        in_specs=[pl.BlockSpec(memory_space=pltpu.SMEM), vmem, vmem],
        out_specs=[vmem] * slabs,
        compiler_params=pltpu.CompilerParams(vmem_limit_bytes=40 * 1024 * 1024),
        name="relay",
    )(me, keys, values)
    kv = [kv[0]] + [lax.ppermute(kv[i], "sy", [(d, d ^ i) for d in range(count_y)]) for i in range(1, slabs)]
    asked = call(select_kernel, (plane, SLOTS, FEAT), jnp.bfloat16, "select", pos, rows)
    asked = exchange(asked, ("sx", "sy"), planes)
    part = call(attend_kernel, (plane, SLOTS, FEAT + STAT), jnp.bfloat16, "attend", asked, *kv)
    part = exchange(part, ("sx", "sy"), planes)
    part = call(merge_kernel, (count_z, KEY_HEADS, FEAT + STAT), jnp.bfloat16, "merge", pos, part)
    part = exchange(part, "sx", along_z)
    out = call(last_kernel, (KEY_HEADS, FEAT), jnp.bfloat16, "last", part)
    return out.reshape(1, KEY_HEADS * FEAT)


def solution(mesh):
    return jax.shard_map(
        per_device,
        mesh=mesh,
        in_specs=(P(("sx", "sy"), None), P(("sx", "sy"), None), P(("sx", "sy"), None), P()),
        out_specs=P(("sx", "sy"), None),
        check_vma=False,
    )
```

```python
import functools

import jax
import jax.numpy as jnp
from jax import lax
from jax.experimental import pallas as pl
from jax.experimental.pallas import tpu as pltpu
from jax.sharding import PartitionSpec as P

QUERY_HEADS = 32
KEY_HEADS = 8
HEAD_WIDTH = 128
BLOCK = 4096
QUERY_PER_KEY = 4
LOG2E = 1.4426950408889634
NEVER = -1e30

FEAT = QUERY_PER_KEY * HEAD_WIDTH
STAT = 128
ONE_LANE = 12
SLOTS = 8

HEADS = 2
PARTNERS = (0, 1, 4, 5)
HALVES = ((0, 1, 4, 5), (2, 3, 6, 7))


def heads_of(s):
    return ((s // 4) * 2 + s % 2) * HEADS


def pieces(x):
    hi = x.astype(jnp.bfloat16).astype(jnp.float32)
    rest = x - hi
    mid = rest.astype(jnp.bfloat16).astype(jnp.float32)
    return hi, mid, rest - mid


def stat_lanes(lse):
    lane = lax.broadcasted_iota(jnp.int32, (lse[0].shape[0], STAT), 1)
    stat = jnp.where(lane == ONE_LANE, 1.0, 0.0)
    for g in range(QUERY_PER_KEY):
        for k, piece in enumerate(pieces(lse[g])):
            stat = jnp.where(lane == g * 3 + k, piece, stat)
    return stat


def slot_onehot(pos):
    shape = (KEY_HEADS * SLOTS, pos.shape[1])
    r = lax.broadcasted_iota(jnp.int32, shape, 0)
    c = lax.broadcasted_iota(jnp.int32, shape, 1)
    hit = (pos == r % SLOTS) & (r // SLOTS == c % KEY_HEADS)
    return jnp.where(hit, 1.0, 0.0).astype(jnp.bfloat16)


def relay_kernel(at_ref, k_ref, v_ref, *out_refs):
    tokens = k_ref.shape[0]
    width = out_refs[0].shape[1]
    for i, out_ref in enumerate(out_refs):
        lanes = pl.ds(pl.multiple_of(at_ref[i] * width, width), width)
        out_ref[:tokens] = k_ref[:, lanes]
        out_ref[tokens:] = v_ref[:, lanes]


def select_kernel(pos_ref, q_ref, out_ref):
    q = q_ref[...].astype(jnp.float32).reshape(-1, FEAT).astype(jnp.bfloat16)
    for b in range(4):
        hot = slot_onehot(pos_ref[b : b + 1, :])
        picked = jnp.dot(hot, q, preferred_element_type=jnp.float32).astype(jnp.bfloat16)
        for s in range(8):
            first = heads_of(s) * SLOTS
            out_ref[b * 8 + s] = picked[first : first + HEADS * SLOTS]


def attend_kernel(x_ref, *refs):
    kv_refs, y_ref = refs[:-1], refs[-1]
    scale = HEAD_WIDTH ** (-0.5) * LOG2E
    columns = y_ref.shape[0] // 2
    tokens = kv_refs[0].shape[0] // 2
    rows = columns * SLOTS
    ones = jnp.ones((tokens, HEAD_WIDTH), jnp.bfloat16)
    x = x_ref[:columns].astype(jnp.float32) + x_ref[columns:].astype(jnp.float32)
    for h in range(HEADS):
        q = x[:, h * SLOTS : (h + 1) * SLOTS].reshape(rows, FEAT).astype(jnp.bfloat16)
        q = [q[:, g * HEAD_WIDTH : (g + 1) * HEAD_WIDTH] for g in range(QUERY_PER_KEY)]
        q = jnp.concatenate(q, axis=0)
        own = slice(h * HEAD_WIDTH, (h + 1) * HEAD_WIDTH)
        tops, sums = [], []
        for kv_ref in kv_refs:
            k = kv_ref[:tokens, own]
            v = jnp.concatenate([kv_ref[tokens:, own], ones], axis=1)
            s = lax.dot_general(q, k, (((1,), (1,)), ((), ())), preferred_element_type=jnp.float32)
            m = jnp.max(s, axis=1, keepdims=True)
            w = jnp.exp2((s - m) * scale).astype(jnp.bfloat16)
            tops.append(m)
            sums.append(jnp.dot(w, v, preferred_element_type=jnp.float32))
        top = functools.reduce(jnp.maximum, tops)
        both = functools.reduce(jnp.add, [jnp.exp2((m - top) * scale) * x for m, x in zip(tops, sums)])
        total = both[:, HEAD_WIDTH:]
        out = both[:, :HEAD_WIDTH] / total
        lse = top * scale + jnp.log2(total[:, :1])
        slots = slice(h * SLOTS, (h + 1) * SLOTS)
        ends = []
        for g in range(QUERY_PER_KEY):
            part = out[g * rows : (g + 1) * rows].reshape(columns, SLOTS, HEAD_WIDTH).astype(jnp.bfloat16)
            lanes = slice(g * HEAD_WIDTH, (g + 1) * HEAD_WIDTH)
            y_ref[:columns, slots, lanes] = part
            y_ref[columns:, slots, lanes] = part
            ends.append(lse[g * rows : (g + 1) * rows])
        stat = stat_lanes(ends).reshape(columns, SLOTS, STAT).astype(jnp.bfloat16)
        y_ref[:columns, slots, FEAT:] = stat
        y_ref[columns:, slots, FEAT:] = stat


def merge_kernel(pos_ref, y_ref, out_ref):
    flip = (((0,), (0,)), ((), ()))
    parts = []
    for b in range(4):
        hot = slot_onehot(pos_ref[b : b + 1, :])
        for half in range(2):
            y = [y_ref[b * 8 + s] for s in HALVES[half]]
            y = jnp.concatenate(y, axis=0)
            parts.append(lax.dot_general(hot, y, flip, preferred_element_type=jnp.float32))
    named = [x[:, FEAT + ONE_LANE : FEAT + ONE_LANE + 1] > 0.5 for x in parts]
    shape = out_ref.shape[:-1]
    ends = []
    for g in range(QUERY_PER_KEY):
        lanes = slice(g * HEAD_WIDTH, (g + 1) * HEAD_WIDTH)
        at = FEAT + 3 * g
        lse = [
            jnp.where(n, x[:, at : at + 1] + (x[:, at + 1 : at + 2] + x[:, at + 2 : at + 3]), NEVER)
            for n, x in zip(named, parts)
        ]
        top = functools.reduce(jnp.maximum, lse)
        weights = [jnp.exp2(x - top) for x in lse]
        total = functools.reduce(jnp.add, weights)
        out = functools.reduce(jnp.add, [w * x[:, lanes] for w, x in zip(weights, parts)]) / total
        out_ref[:, :, lanes] = out.reshape(*shape, HEAD_WIDTH).astype(jnp.bfloat16)
        ends.append(top + jnp.log2(total))
    out_ref[:, :, FEAT:] = stat_lanes(ends).reshape(*shape, STAT).astype(jnp.bfloat16)


def last_kernel(a_ref, out_ref):
    for g in range(QUERY_PER_KEY):
        at = FEAT + 3 * g
        lse = [a_ref[:, :, at + k : at + k + 1].astype(jnp.float32) for k in range(3)]
        lse = lse[0] + (lse[1] + lse[2])
        weight = jnp.exp2(lse - jnp.max(lse, axis=0, keepdims=True))
        total = jnp.sum(weight, axis=0)
        lanes = slice(g * HEAD_WIDTH, (g + 1) * HEAD_WIDTH)
        mixed = jnp.sum(a_ref[:, :, lanes].astype(jnp.float32) * weight, axis=0) / total
        out_ref[:, lanes] = mixed.astype(jnp.bfloat16)


def call(kernel, shape, dtype, name, *args):
    return pl.pallas_call(
        kernel,
        out_shape=jax.ShapeDtypeStruct(shape, dtype),
        in_specs=[pl.BlockSpec(memory_space=pltpu.VMEM)] * len(args),
        out_specs=pl.BlockSpec(memory_space=pltpu.VMEM),
        compiler_params=pltpu.CompilerParams(vmem_limit_bytes=40 * 1024 * 1024),
        name=name,
    )(*args)


def per_device(queries, keys, values, block_ids):
    count_x = lax.axis_size("sx")
    count_y = lax.axis_size("sy")
    index_x = lax.axis_index("sx")
    index_y = lax.axis_index("sy")
    count_z = count_x // 2
    index_z, core = index_x // 2, index_x % 2
    tokens = keys.shape[0]
    slabs = BLOCK // tokens
    along_z = [[2 * z + c for z in range(count_z)] for c in range(2)]
    plane = 2 * count_y
    planes = [list(range(z * plane, (z + 1) * plane)) for z in range(count_z)]

    def exchange(x, axis, groups):
        return lax.all_to_all(x, axis, split_axis=0, concat_axis=0, tiled=True, axis_index_groups=groups)

    column = lax.dynamic_index_in_dim(block_ids.reshape(count_x, count_y, -1), index_y, 1, keepdims=False)
    wanted = index_z * 4 + jnp.arange(4, dtype=jnp.int32)
    named = jnp.any(column[None] == wanted[:, None, None], axis=2)
    before = jnp.arange(count_x)[None, :] < jnp.arange(count_x)[:, None]
    rank = jnp.sum((named[:, None, :] & before[None]).astype(jnp.int32), axis=2)
    pos = jnp.where(named, rank, -1).reshape(4, count_z, 2)
    pos = lax.dynamic_index_in_dim(pos, core, 2, keepdims=False)
    pos = jnp.repeat(pos, KEY_HEADS, axis=1)

    own = jnp.broadcast_to(queries.reshape(1, KEY_HEADS, FEAT), (count_z, KEY_HEADS, FEAT))
    rows = exchange(own, "sx", along_z)
    me = (index_y % slabs).astype(jnp.int32)
    at = jnp.stack([heads_of(jnp.bitwise_xor(me, i)) // HEADS for i in PARTNERS])
    vmem = pl.BlockSpec(memory_space=pltpu.VMEM)
    kv = pl.pallas_call(
        relay_kernel,
        out_shape=[jax.ShapeDtypeStruct((2 * tokens, HEADS * HEAD_WIDTH), jnp.bfloat16)] * len(PARTNERS),
        in_specs=[pl.BlockSpec(memory_space=pltpu.SMEM), vmem, vmem],
        out_specs=[vmem] * len(PARTNERS),
        compiler_params=pltpu.CompilerParams(vmem_limit_bytes=40 * 1024 * 1024),
        name="relay",
    )(at, keys, values)
    swaps = [lax.ppermute(x, "sy", [(d, d ^ i) for d in range(count_y)]) for i, x in zip(PARTNERS[1:], kv[1:])]
    asked = call(select_kernel, (plane, HEADS * SLOTS, FEAT), jnp.bfloat16, "select", pos, rows)
    asked = exchange(asked, ("sx", "sy"), planes)
    part = call(attend_kernel, (plane, HEADS * SLOTS, FEAT + STAT), jnp.bfloat16, "attend", asked, kv[0], *swaps)
    part = exchange(part, ("sx", "sy"), planes)
    part = call(merge_kernel, (count_z, KEY_HEADS, FEAT + STAT), jnp.bfloat16, "merge", pos, part)
    part = exchange(part, "sx", along_z)
    out = call(last_kernel, (KEY_HEADS, FEAT), jnp.bfloat16, "last", part)
    return out.reshape(1, KEY_HEADS * FEAT)


def solution(mesh):
    return jax.shard_map(
        per_device,
        mesh=mesh,
        in_specs=(P(("sx", "sy"), None), P(("sx", "sy"), None), P(("sx", "sy"), None), P()),
        out_specs=P(("sx", "sy"), None),
        check_vma=False,
    )
```

```python
import functools

import jax
import jax.numpy as jnp
from jax import lax
from jax.experimental import pallas as pl
from jax.experimental.pallas import tpu as pltpu
from jax.sharding import PartitionSpec as P

QUERY_HEADS = 32
KEY_HEADS = 8
HEAD_WIDTH = 128
BLOCK = 4096
QUERY_PER_KEY = 4
LOG2E = 1.4426950408889634
NEVER = -1e30

SIDE = 4
SLOTS = 8
FEAT = QUERY_PER_KEY * HEAD_WIDTH
STAT = 128
ONE_LANE = 12
PART_ROWS = 12
SWAPS = (2, 6, 7, 5, 3, 4, 1)
EARLY = 2


def pieces(x):
    hi = x.astype(jnp.bfloat16).astype(jnp.float32)
    rest = x - hi
    mid = rest.astype(jnp.bfloat16).astype(jnp.float32)
    return hi, mid, rest - mid


def stat_lanes(lse):
    lane = lax.broadcasted_iota(jnp.int32, (lse[0].shape[0], STAT), 1)
    stat = jnp.zeros(lane.shape, jnp.float32)
    for at, x in enumerate(lse):
        for k, piece in enumerate(pieces(x)):
            stat = jnp.where(lane == at * 3 + k, piece, stat)
    return stat


def find_kernel(here_ref, ids_ref, pos_ref):
    z, core, y = here_ref[0], here_ref[1], here_ref[2]
    count = ids_ref.shape[1]
    ids = ids_ref[...]
    b = lax.broadcasted_iota(jnp.int32, (8, count), 0)
    named = jnp.zeros((8, count), jnp.float32)
    for block in range(4):
        hit = jnp.max(jnp.where(ids == z * 4 + block, 1.0, 0.0), axis=0, keepdims=True)
        named = jnp.where(b == block, hit, named)
    columns = count // SIDE
    r = lax.broadcasted_iota(jnp.int32, (count, columns), 0)
    c = lax.broadcasted_iota(jnp.int32, (count, columns), 1)
    own = jnp.where(r == (c // SIDE) * (SIDE * SIDE) + y * SIDE + c % SIDE, 1.0, 0.0)
    named = jnp.dot(named, own, preferred_element_type=jnp.float32)
    r = lax.broadcasted_iota(jnp.int32, (columns, columns), 0)
    c = lax.broadcasted_iota(jnp.int32, (columns, columns), 1)
    before = jnp.where((r % SIDE == c % SIDE) & (r < c), 1.0, 0.0)
    rank = jnp.dot(named, before, preferred_element_type=jnp.float32)
    pos = jnp.where(named > 0.5, rank, -1.0)
    side = jnp.where(r == (c // SIDE) * (2 * SIDE) + core * SIDE + c % SIDE, 1.0, 0.0)
    pos = jnp.dot(pos, side, preferred_element_type=jnp.float32)
    pos_ref[...] = pos[:, : pos_ref.shape[1]]


def slot_onehot(pos):
    shape = (SIDE * SLOTS, pos.shape[1])
    r = lax.broadcasted_iota(jnp.int32, shape, 0)
    c = lax.broadcasted_iota(jnp.int32, shape, 1)
    hit = (pos == (r % SLOTS).astype(jnp.float32)) & (r // SLOTS == c % SIDE)
    return jnp.where(hit, 1.0, 0.0).astype(jnp.bfloat16)


def relay_kernel(me_ref, k_ref, v_ref, *out_refs):
    tokens = k_ref.shape[0]
    for i, out_ref in zip((0,) + SWAPS, out_refs):
        head = jnp.bitwise_xor(me_ref[0], i)
        lanes = pl.ds(pl.multiple_of(head * HEAD_WIDTH, HEAD_WIDTH), HEAD_WIDTH)
        out_ref[:tokens] = k_ref[:, lanes]
        out_ref[tokens:] = v_ref[:, lanes]


def select_kernel(pos_ref, q_ref, out_ref, wide_ref):
    rows = pos_ref.shape[1]
    wide_ref[...] = q_ref[...].astype(jnp.float32)
    for y0 in range(2):
        q = [wide_ref[pl.ds(y0 * SIDE + g, rows, stride=2 * SIDE), :] for g in range(QUERY_PER_KEY)]
        q = jnp.concatenate(q, axis=1).astype(jnp.bfloat16)
        for b in range(4):
            hot = slot_onehot(pos_ref[b : b + 1, :])
            picked = jnp.dot(hot, q, preferred_element_type=jnp.float32)
            out_ref[b * 2 + y0] = picked.astype(jnp.bfloat16)


def attend_kernel(x_ref, *refs):
    kv_refs, y_ref = refs[:-1], refs[-1]
    scale = HEAD_WIDTH ** (-0.5) * LOG2E
    tokens = kv_refs[0].shape[0] // 2
    slots = x_ref.shape[1]
    rows = SIDE * slots
    ones = jnp.ones((tokens, HEAD_WIDTH), jnp.bfloat16)
    x = x_ref[:SIDE].astype(jnp.float32) + x_ref[SIDE:].astype(jnp.float32)
    x = x.reshape(rows, FEAT).astype(jnp.bfloat16)
    q = [x[:, g * HEAD_WIDTH : (g + 1) * HEAD_WIDTH] for g in range(QUERY_PER_KEY)]
    q = jnp.concatenate(q, axis=0)
    tops, sums = [], []
    for kv_ref in kv_refs:
        k = kv_ref[:tokens]
        v = jnp.concatenate([kv_ref[tokens:], ones], axis=1)
        s = lax.dot_general(q, k, (((1,), (1,)), ((), ())), preferred_element_type=jnp.float32)
        m = jnp.max(s, axis=1, keepdims=True)
        w = jnp.exp2((s - m) * scale).astype(jnp.bfloat16)
        tops.append(m)
        sums.append(jnp.dot(w, v, preferred_element_type=jnp.float32))
    top = functools.reduce(jnp.maximum, tops)
    both = functools.reduce(jnp.add, [jnp.exp2((m - top) * scale) * x for m, x in zip(tops, sums)])
    total = both[:, HEAD_WIDTH:]
    out = (both[:, :HEAD_WIDTH] / total).astype(jnp.bfloat16)
    lse = top * scale + jnp.log2(total[:, :1])
    parts = [out[g * rows : (g + 1) * rows].reshape(SIDE, slots, HEAD_WIDTH) for g in range(QUERY_PER_KEY)]
    stat = stat_lanes([lse[g * rows : (g + 1) * rows] for g in range(QUERY_PER_KEY)])
    lane = lax.broadcasted_iota(jnp.int32, stat.shape, 1)
    stat = jnp.where(lane == ONE_LANE, 1.0, stat).astype(jnp.bfloat16).reshape(SIDE, slots, STAT)
    for core in range(2):
        dest = slice(core * SIDE, (core + 1) * SIDE)
        for g in range(QUERY_PER_KEY):
            y_ref[dest, :, g * HEAD_WIDTH : (g + 1) * HEAD_WIDTH] = parts[g]
        y_ref[dest, :, FEAT:] = stat


def merge_kernel(pos_ref, y_ref, out_ref, wide_ref):
    flip = (((0,), (0,)), ((), ()))
    rows = pos_ref.shape[1]
    hots = [slot_onehot(pos_ref[b : b + 1, :]) for b in range(4)]
    ends = []
    for y0 in range(2):
        parts = [
            lax.dot_general(hots[b], y_ref[b * 2 + y0], flip, preferred_element_type=jnp.float32) for b in range(4)
        ]
        named = [x[:, FEAT + ONE_LANE : FEAT + ONE_LANE + 1] > 0.5 for x in parts]
        for g in range(QUERY_PER_KEY):
            lanes = slice(g * HEAD_WIDTH, (g + 1) * HEAD_WIDTH)
            at = FEAT + 3 * g
            lse = [
                jnp.where(n, x[:, at : at + 1] + (x[:, at + 1 : at + 2] + x[:, at + 2 : at + 3]), NEVER)
                for n, x in zip(named, parts)
            ]
            top = functools.reduce(jnp.maximum, lse)
            weights = [jnp.exp2(x - top) for x in lse]
            total = functools.reduce(jnp.add, weights)
            out = functools.reduce(jnp.add, [w * x[:, lanes] for w, x in zip(weights, parts)]) / total
            wide_ref[pl.ds(y0 * SIDE + g, rows, stride=PART_ROWS), :] = out
            ends.append(top + jnp.log2(total))
    wide_ref[pl.ds(2 * SIDE, rows, stride=PART_ROWS), :] = stat_lanes(ends)
    for r in range(2 * SIDE + 1, PART_ROWS):
        wide_ref[pl.ds(r, rows, stride=PART_ROWS), :] = jnp.zeros((rows, HEAD_WIDTH), jnp.float32)
    out_ref[...] = wide_ref[...].astype(jnp.bfloat16)


def last_kernel(a_ref, out_ref, wide_ref):
    count = a_ref.shape[0] // (SIDE * PART_ROWS)
    wide_ref[...] = a_ref[...].astype(jnp.float32)

    def over_z(x, r):
        return wide_ref[pl.ds(x * PART_ROWS + r, count, stride=SIDE * PART_ROWS), :]

    for x in range(SIDE):
        stat = over_z(x, 2 * SIDE)
        for y0 in range(2):
            outs = []
            for g in range(QUERY_PER_KEY):
                r = y0 * SIDE + g
                lse = stat[:, 3 * r : 3 * r + 1] + (stat[:, 3 * r + 1 : 3 * r + 2] + stat[:, 3 * r + 2 : 3 * r + 3])
                weight = jnp.exp2(lse - jnp.max(lse, axis=0, keepdims=True))
                total = jnp.sum(weight, axis=0, keepdims=True)
                outs.append(jnp.sum(over_z(x, r) * weight, axis=0, keepdims=True) / total)
            head = y0 * SIDE + x
            out_ref[:, head * FEAT : (head + 1) * FEAT] = jnp.concatenate(outs, axis=1).astype(jnp.bfloat16)


def call(kernel, shape, dtype, name, *args, scratch=()):
    return pl.pallas_call(
        kernel,
        out_shape=jax.ShapeDtypeStruct(shape, dtype),
        in_specs=[pl.BlockSpec(memory_space=pltpu.VMEM)] * len(args),
        out_specs=pl.BlockSpec(memory_space=pltpu.VMEM),
        scratch_shapes=[pltpu.VMEM(s, jnp.float32) for s in scratch],
        compiler_params=pltpu.CompilerParams(vmem_limit_bytes=40 * 1024 * 1024),
        name=name,
    )(*args)


def per_device(queries, keys, values, block_ids):
    count_x = lax.axis_size("sx")
    count_y = lax.axis_size("sy")
    index_x = lax.axis_index("sx")
    index_y = lax.axis_index("sy")
    count_z = count_x // 2
    tokens = keys.shape[0]
    slabs = BLOCK // tokens
    rows = count_z * SIDE

    def groups(key):
        found = {}
        for sx in range(count_x):
            for sy in range(count_y):
                found.setdefault(key(sx // 2, sx % 2, sy // SIDE, sy % SIDE), []).append(sx * count_y + sy)
        return list(found.values())

    along_zx = groups(lambda z, core, y, x: (core, y))
    along_cy = groups(lambda z, core, y, x: (z, x))

    def exchange(x, members):
        return lax.all_to_all(x, ("sx", "sy"), split_axis=0, concat_axis=0, tiled=True, axis_index_groups=members)

    vmem = pl.BlockSpec(memory_space=pltpu.VMEM)
    smem = pl.BlockSpec(memory_space=pltpu.SMEM)

    own = queries.reshape(2, SIDE, QUERY_PER_KEY, HEAD_WIDTH).transpose(1, 0, 2, 3)
    own = own.reshape(1, SIDE, 2 * SIDE, HEAD_WIDTH)
    own = jnp.broadcast_to(own, (count_z, SIDE, 2 * SIDE, HEAD_WIDTH))
    own = exchange(own.reshape(rows, 2 * SIDE, HEAD_WIDTH), along_zx)

    here = jnp.stack([index_x // 2, index_x % 2, index_y // SIDE]).astype(jnp.int32)
    pos = pl.pallas_call(
        find_kernel,
        out_shape=jax.ShapeDtypeStruct((8, rows), jnp.float32),
        in_specs=[smem, vmem],
        out_specs=vmem,
        name="find",
    )(here, block_ids.T)

    me = (index_y % slabs).astype(jnp.int32).reshape(1)
    kv = pl.pallas_call(
        relay_kernel,
        out_shape=[jax.ShapeDtypeStruct((2 * tokens, HEAD_WIDTH), jnp.bfloat16)] * slabs,
        in_specs=[smem, vmem, vmem],
        out_specs=[vmem] * slabs,
        compiler_params=pltpu.CompilerParams(vmem_limit_bytes=40 * 1024 * 1024),
        name="relay",
    )(me, keys, values)

    def swap(x, i):
        return lax.ppermute(x, "sy", [(d, d ^ i) for d in range(count_y)])

    early = [swap(x, i) for x, i in zip(kv[1 : EARLY + 1], SWAPS)]
    asked = call(
        select_kernel,
        (2 * SIDE, SIDE * SLOTS, FEAT),
        jnp.bfloat16,
        "select",
        pos,
        own.reshape(rows * 2 * SIDE, HEAD_WIDTH),
        scratch=[(rows * 2 * SIDE, HEAD_WIDTH)],
    )
    asked, *late = lax.optimization_barrier((asked, *kv[EARLY + 1 :]))
    asked = exchange(asked, along_cy)
    late = [swap(x, i) for x, i in zip(late, SWAPS[EARLY:])]
    part = call(
        attend_kernel, (2 * SIDE, SIDE * SLOTS, FEAT + STAT), jnp.bfloat16, "attend", asked, kv[0], *early, *late
    )
    part = exchange(part, along_cy)
    shape = (rows * PART_ROWS, HEAD_WIDTH)
    part = call(merge_kernel, shape, jnp.bfloat16, "merge", pos, part, scratch=[shape])
    part = exchange(part.reshape(rows, PART_ROWS // SIDE, SIDE, HEAD_WIDTH), along_zx)
    return call(
        last_kernel, (1, QUERY_HEADS * HEAD_WIDTH), jnp.bfloat16, "last", part.reshape(shape), scratch=[shape]
    )


def solution(mesh):
    return jax.shard_map(
        per_device,
        mesh=mesh,
        in_specs=(P(("sx", "sy"), None), P(("sx", "sy"), None), P(("sx", "sy"), None), P()),
        out_specs=P(("sx", "sy"), None),
        check_vma=False,
    )
```

```python
import functools

import jax
import jax.numpy as jnp
from jax import lax
from jax.experimental import pallas as pl
from jax.experimental.pallas import tpu as pltpu
from jax.sharding import PartitionSpec as P

QUERY_HEADS = 32
KEY_HEADS = 8
HEAD_WIDTH = 128
BLOCK = 4096
QUERY_PER_KEY = 4
LOG2E = 1.4426950408889634
NEVER = -1e30

FEAT = QUERY_PER_KEY * HEAD_WIDTH
STAT = 128
ONE_LANE = 12
SLOTS = 8


def pieces(x):
    hi = x.astype(jnp.bfloat16).astype(jnp.float32)
    rest = x - hi
    mid = rest.astype(jnp.bfloat16).astype(jnp.float32)
    return hi, mid, rest - mid


def stat_lanes(lse):
    lane = lax.broadcasted_iota(jnp.int32, (lse[0].shape[0], STAT), 1)
    stat = jnp.where(lane == ONE_LANE, 1.0, 0.0)
    for g in range(QUERY_PER_KEY):
        for k, piece in enumerate(pieces(lse[g])):
            stat = jnp.where(lane == g * 3 + k, piece, stat)
    return stat


def find_kernel(ids_ref, in_ref, out_ref):
    count_x, count_y = lax.axis_size("sx"), lax.axis_size("sy")
    index_x, index_y = lax.axis_index("sx"), lax.axis_index("sy")
    z, core = index_x // 2, index_x % 2
    lanes = 128
    r = lax.broadcasted_iota(jnp.int32, (count_x * count_y, lanes), 0)
    c = lax.broadcasted_iota(jnp.int32, (count_x * count_y, lanes), 1)
    own = jnp.where((r == c * count_y + index_y) & (c < count_x), 1.0, 0.0).astype(jnp.bfloat16)
    ids = ids_ref[...].astype(jnp.float32).astype(jnp.bfloat16)
    column = jnp.dot(ids, own, preferred_element_type=jnp.float32)
    b = lax.broadcasted_iota(jnp.int32, (8, lanes), 0)
    c = lax.broadcasted_iota(jnp.int32, (8, lanes), 1)
    named = jnp.zeros((8, lanes), jnp.float32)
    for block in range(4):
        wanted = (z * 4 + block).astype(jnp.float32)
        hit = jnp.max(jnp.where(column == wanted, 1.0, 0.0), axis=0, keepdims=True)
        named = jnp.where((b == block) & (c < count_x), hit, named)
    r = lax.broadcasted_iota(jnp.int32, (lanes, lanes), 0)
    c = lax.broadcasted_iota(jnp.int32, (lanes, lanes), 1)
    before = jnp.where(r < c, 1.0, 0.0).astype(jnp.bfloat16)
    rank = jnp.dot(named.astype(jnp.bfloat16), before, preferred_element_type=jnp.float32)
    pos = jnp.where(named > 0.5, rank, -1.0).astype(jnp.bfloat16)
    side = jnp.where(r == (c // KEY_HEADS) * 2 + core, 1.0, 0.0).astype(jnp.bfloat16)
    out_ref[...] = jnp.dot(pos, side, preferred_element_type=jnp.float32)
    shape = (lanes, in_ref.shape[1])
    r = lax.broadcasted_iota(jnp.int32, shape, 0)
    c = lax.broadcasted_iota(jnp.int32, shape, 1)
    both = jnp.where(r == c // KEY_HEADS, 1.0, 0.0).astype(jnp.bfloat16)
    in_ref[...] = jnp.dot(pos, both, preferred_element_type=jnp.float32)


def slot_onehot(pos):
    shape = (KEY_HEADS * SLOTS, pos.shape[1])
    r = lax.broadcasted_iota(jnp.int32, shape, 0)
    c = lax.broadcasted_iota(jnp.int32, shape, 1)
    hit = (pos == (r % SLOTS).astype(jnp.float32)) & (r // SLOTS == c % KEY_HEADS)
    return jnp.where(hit, 1.0, 0.0).astype(jnp.bfloat16)


def relay_kernel(k_ref, v_ref, out_ref, k_here, v_here, by_head, in_sems, out_sems):
    tokens = k_ref.shape[0]
    chunks = in_sems.shape[1]
    step = tokens // chunks
    pairs = [(i, j) for i in range(chunks) for j in range(2)]
    there, here = (k_ref, v_ref), (k_here, v_here)
    arriving = {}
    for i, j in pairs:
        part = pl.ds(i * step, step)
        arriving[i, j] = pltpu.make_async_copy(there[j].at[part], here[j].at[part], in_sems.at[j, i])
        arriving[i, j].start()
    leaving = []
    for i, j in pairs:
        arriving[i, j].wait()
        start = j * tokens + i * step
        for h in range(KEY_HEADS):
            lanes = slice(h * HEAD_WIDTH, (h + 1) * HEAD_WIDTH)
            by_head[h, start : start + step] = here[j][i * step : (i + 1) * step, lanes]
        part = pl.ds(start, step)
        leaving.append(pltpu.make_async_copy(by_head.at[:, part], out_ref.at[:, part], out_sems.at[j, i]))
        leaving[-1].start()
    for copy in leaving:
        copy.wait()


def select_kernel(pos_ref, q_ref, out_ref):
    q = q_ref[...].astype(jnp.float32).reshape(-1, FEAT).astype(jnp.bfloat16)
    for b in range(4):
        hot = slot_onehot(pos_ref[b : b + 1, :])
        picked = jnp.dot(hot, q, preferred_element_type=jnp.float32)
        picked = picked.reshape(KEY_HEADS, SLOTS, FEAT).astype(jnp.bfloat16)
        out_ref[b * KEY_HEADS : (b + 1) * KEY_HEADS] = picked


def attend_kernel(x_ref, kv_ref, y_ref):
    scale = HEAD_WIDTH ** (-0.5) * LOG2E
    columns = x_ref.shape[0] // 2
    tokens = kv_ref.shape[1] // 2
    rows = columns * SLOTS
    ones = jnp.ones((tokens, HEAD_WIDTH), jnp.bfloat16)
    x = x_ref[columns:].astype(jnp.float32).reshape(rows, FEAT).astype(jnp.bfloat16)
    q = [x[:, g * HEAD_WIDTH : (g + 1) * HEAD_WIDTH] for g in range(QUERY_PER_KEY)]
    q = jnp.concatenate(q, axis=0)
    tops, sums = [], []
    for slab in range(kv_ref.shape[0]):
        k = kv_ref[slab, :tokens]
        v = jnp.concatenate([kv_ref[slab, tokens:], ones], axis=1)
        s = lax.dot_general(q, k, (((1,), (1,)), ((), ())), preferred_element_type=jnp.float32)
        m = jnp.max(s, axis=1, keepdims=True)
        w = jnp.exp2((s - m) * scale).astype(jnp.bfloat16)
        tops.append(m)
        sums.append(jnp.dot(w, v, preferred_element_type=jnp.float32))
    top = functools.reduce(jnp.maximum, tops)
    both = functools.reduce(jnp.add, [jnp.exp2((m - top) * scale) * x for m, x in zip(tops, sums)])
    total = both[:, HEAD_WIDTH:]
    out = both[:, :HEAD_WIDTH] / total
    lse = top * scale + jnp.log2(total[:, :1])
    ends = []
    for g in range(QUERY_PER_KEY):
        part = out[g * rows : (g + 1) * rows].reshape(columns, SLOTS, HEAD_WIDTH).astype(jnp.bfloat16)
        lanes = slice(g * HEAD_WIDTH, (g + 1) * HEAD_WIDTH)
        y_ref[:columns, :, lanes] = part
        y_ref[columns:, :, lanes] = part
        ends.append(lse[g * rows : (g + 1) * rows])
    stat = stat_lanes(ends).reshape(columns, SLOTS, STAT).astype(jnp.bfloat16)
    y_ref[:columns, :, FEAT:] = stat
    y_ref[columns:, :, FEAT:] = stat


def merge_kernel(pos_ref, y_ref, out_ref):
    flip = (((0,), (0,)), ((), ()))
    parts = []
    for b in range(4):
        y = y_ref[b * KEY_HEADS : (b + 1) * KEY_HEADS].astype(jnp.float32)
        y = y.reshape(KEY_HEADS * SLOTS, FEAT + STAT).astype(jnp.bfloat16)
        hot = slot_onehot(pos_ref[b : b + 1, :])
        parts.append(lax.dot_general(hot, y, flip, preferred_element_type=jnp.float32))
    named = [x[:, FEAT + ONE_LANE : FEAT + ONE_LANE + 1] > 0.5 for x in parts]
    shape = out_ref.shape[:-1]
    ends = []
    for g in range(QUERY_PER_KEY):
        lanes = slice(g * HEAD_WIDTH, (g + 1) * HEAD_WIDTH)
        at = FEAT + 3 * g
        lse = [
            jnp.where(n, x[:, at : at + 1] + (x[:, at + 1 : at + 2] + x[:, at + 2 : at + 3]), NEVER)
            for n, x in zip(named, parts)
        ]
        top = functools.reduce(jnp.maximum, lse)
        weights = [jnp.exp2(x - top) for x in lse]
        total = functools.reduce(jnp.add, weights)
        out = functools.reduce(jnp.add, [w * x[:, lanes] for w, x in zip(weights, parts)]) / total
        out_ref[:, :, lanes] = out.reshape(*shape, HEAD_WIDTH).astype(jnp.bfloat16)
        ends.append(top + jnp.log2(total))
    out_ref[:, :, FEAT:] = stat_lanes(ends).reshape(*shape, STAT).astype(jnp.bfloat16)


def last_kernel(a_ref, out_ref):
    for g in range(QUERY_PER_KEY):
        at = FEAT + 3 * g
        lse = [a_ref[:, :, at + k : at + k + 1].astype(jnp.float32) for k in range(3)]
        lse = lse[0] + (lse[1] + lse[2])
        weight = jnp.exp2(lse - jnp.max(lse, axis=0, keepdims=True))
        total = jnp.sum(weight, axis=0)
        lanes = slice(g * HEAD_WIDTH, (g + 1) * HEAD_WIDTH)
        mixed = jnp.sum(a_ref[:, :, lanes].astype(jnp.float32) * weight, axis=0) / total
        for h in range(KEY_HEADS):
            head = h * FEAT + g * HEAD_WIDTH
            out_ref[:, head : head + HEAD_WIDTH] = mixed[h : h + 1].astype(jnp.bfloat16)


def call(kernel, shape, dtype, name, *args):
    return pl.pallas_call(
        kernel,
        out_shape=jax.ShapeDtypeStruct(shape, dtype),
        in_specs=[pl.BlockSpec(memory_space=pltpu.VMEM)] * len(args),
        out_specs=pl.BlockSpec(memory_space=pltpu.VMEM),
        compiler_params=pltpu.CompilerParams(vmem_limit_bytes=40 * 1024 * 1024),
        name=name,
    )(*args)


def per_device(queries, keys, values, block_ids):
    count_x = lax.axis_size("sx")
    count_y = lax.axis_size("sy")
    count_z = count_x // 2
    tokens = keys.shape[0]
    slabs = BLOCK // tokens
    cores = [[2 * z, 2 * z + 1] for z in range(count_z)]
    along_z = [[2 * z + c for z in range(count_z)] for c in range(2)]
    block_devices = [list(range(start, start + slabs)) for start in range(0, count_y, slabs)]
    plane = 2 * count_y
    planes = [list(range(z * plane, (z + 1) * plane)) for z in range(count_z)]
    core_1_along_z = [[(2 * z + 1) * count_y + y for z in range(count_z)] for y in range(count_y)]
    core_0_planes = [[2 * z * count_y + y for y in range(count_y)] for z in range(count_z)]

    def exchange(x, axis, groups):
        return lax.all_to_all(x, axis, split_axis=0, concat_axis=0, tiled=True, axis_index_groups=groups)

    vmem = pl.BlockSpec(memory_space=pltpu.VMEM)
    hbm = pl.BlockSpec(memory_space=pltpu.HBM)
    kv = pl.pallas_call(
        relay_kernel,
        out_shape=jax.ShapeDtypeStruct((KEY_HEADS, 2 * tokens, HEAD_WIDTH), jnp.bfloat16),
        in_specs=[hbm, hbm],
        out_specs=hbm,
        scratch_shapes=[
            pltpu.VMEM(keys.shape, keys.dtype),
            pltpu.VMEM(values.shape, values.dtype),
            pltpu.VMEM((KEY_HEADS, 2 * tokens, HEAD_WIDTH), keys.dtype),
            pltpu.SemaphoreType.DMA((2, 4)),
            pltpu.SemaphoreType.DMA((2, 4)),
        ],
        compiler_params=pltpu.CompilerParams(vmem_limit_bytes=60 * 1024 * 1024),
        name="relay",
    )(keys, values)
    kv = exchange(kv, "sy", block_devices)

    pos_in, pos_out = pl.pallas_call(
        find_kernel,
        out_shape=[
            jax.ShapeDtypeStruct((8, count_x * KEY_HEADS), jnp.float32),
            jax.ShapeDtypeStruct((8, count_z * KEY_HEADS), jnp.float32),
        ],
        in_specs=[vmem],
        out_specs=[vmem, vmem],
        name="find",
    )(block_ids.T)
    rows = lax.all_gather(queries.reshape(KEY_HEADS, FEAT), "sx", axis=0, axis_index_groups=cores)
    rows = lax.all_gather(rows, ("sx", "sy"), axis=0, axis_index_groups=core_1_along_z + core_0_planes)
    rows, pos_in, pos_out, kv = lax.optimization_barrier((rows, pos_in, pos_out, kv))
    rows = rows.reshape(count_x, KEY_HEADS, FEAT)
    asked = call(select_kernel, (plane, SLOTS, FEAT), jnp.bfloat16, "select", pos_in, rows)
    asked = exchange(asked, ("sx", "sy"), planes)
    part = call(attend_kernel, (plane, SLOTS, FEAT + STAT), jnp.bfloat16, "attend", asked, kv)
    part = exchange(part, ("sx", "sy"), planes)
    part = call(merge_kernel, (count_z, KEY_HEADS, FEAT + STAT), jnp.bfloat16, "merge", pos_out, part)
    part = exchange(part, "sx", along_z)
    return call(last_kernel, (1, KEY_HEADS * FEAT), jnp.bfloat16, "last", part)


def solution(mesh):
    return jax.shard_map(
        per_device,
        mesh=mesh,
        in_specs=(P(("sx", "sy"), None), P(("sx", "sy"), None), P(("sx", "sy"), None), P()),
        out_specs=P(("sx", "sy"), None),
        check_vma=False,
    )
```

```python
import functools

import jax
import jax.numpy as jnp
from jax import lax
from jax.experimental import pallas as pl
from jax.experimental.pallas import tpu as pltpu
from jax.sharding import PartitionSpec as P

QUERY_HEADS = 32
KEY_HEADS = 8
HEAD_WIDTH = 128
BLOCK = 4096
QUERY_PER_KEY = 4
LOG2E = 1.4426950408889634
NEVER = -1e30

FEAT = QUERY_PER_KEY * HEAD_WIDTH
SLOTS = 8
SLABS = 8
HALF = KEY_HEADS // 2
PARTNER = (1, 4)
STAT = 128
ONE_LANE = 12


def half_of(core, s):
    return jnp.where(core == 0, s % 2, s // 4)


def pieces(x):
    hi = x.astype(jnp.bfloat16).astype(jnp.float32)
    rest = x - hi
    mid = rest.astype(jnp.bfloat16).astype(jnp.float32)
    return hi, mid, rest - mid


def stat_lanes(lse):
    lane = lax.broadcasted_iota(jnp.int32, (lse[0].shape[0], STAT), 1)
    stat = jnp.zeros(lane.shape, jnp.float32)
    for at, x in enumerate(lse):
        for k, piece in enumerate(pieces(x)):
            stat = jnp.where(lane == at * 3 + k, piece, stat)
    return stat


def find_kernel(ids_ref, pos_ref):
    count_x, count_y = lax.axis_size("sx"), lax.axis_size("sy")
    index_x, index_y = lax.axis_index("sx"), lax.axis_index("sy")
    lanes = 128
    r = lax.broadcasted_iota(jnp.int32, (count_x * count_y, lanes), 0)
    c = lax.broadcasted_iota(jnp.int32, (count_x * count_y, lanes), 1)
    row = (c % (count_x // 2)) * 2 + c // (count_x // 2)
    own = jnp.where((r == row * count_y + index_y) & (c < count_x), 1.0, 0.0).astype(jnp.bfloat16)
    ids = ids_ref[...].astype(jnp.float32).astype(jnp.bfloat16)
    column = jnp.dot(ids, own, preferred_element_type=jnp.float32)
    b = lax.broadcasted_iota(jnp.int32, (8, lanes), 0)
    c = lax.broadcasted_iota(jnp.int32, (8, lanes), 1)
    named = jnp.zeros((8, lanes), jnp.float32)
    for block in range(2):
        wanted = (index_x * 2 + block).astype(jnp.float32)
        hit = jnp.max(jnp.where(column == wanted, 1.0, 0.0), axis=0, keepdims=True)
        named = jnp.where((b == block) & (c < count_x), hit, named)
    r = lax.broadcasted_iota(jnp.int32, (lanes, lanes), 0)
    c = lax.broadcasted_iota(jnp.int32, (lanes, lanes), 1)
    before = jnp.where(r < c, 1.0, 0.0).astype(jnp.bfloat16)
    rank = jnp.dot(named.astype(jnp.bfloat16), before, preferred_element_type=jnp.float32)
    pos = jnp.where(named > 0.5, rank, -1.0).astype(jnp.bfloat16)
    shape = (lanes, pos_ref.shape[1])
    r = lax.broadcasted_iota(jnp.int32, shape, 0)
    c = lax.broadcasted_iota(jnp.int32, shape, 1)
    heads = jnp.where(r == c // KEY_HEADS, 1.0, 0.0).astype(jnp.bfloat16)
    pos_ref[...] = jnp.dot(pos, heads, preferred_element_type=jnp.float32)


def slot_onehot(pos, dtype):
    shape = (KEY_HEADS * SLOTS, pos.shape[1])
    r = lax.broadcasted_iota(jnp.int32, shape, 0)
    c = lax.broadcasted_iota(jnp.int32, shape, 1)
    hit = (pos == (r % SLOTS).astype(jnp.float32)) & (r // SLOTS == c % KEY_HEADS)
    return jnp.where(hit, 1.0, 0.0).astype(dtype)


def relay_kernel(k_ref, v_ref, out_ref, here, in_sems, out_sems):
    core = lax.axis_index("sx") % 2
    theirs = 1 - half_of(core, lax.axis_index("sy") % SLABS)
    tokens, width = k_ref.shape[0], out_ref.shape[1]
    lanes = pl.ds(pl.multiple_of(theirs * width, width), width)
    chunks = in_sems.shape[1]
    step = tokens // chunks
    pairs = [(i, j) for i in range(chunks) for j in range(2)]
    there = (k_ref, v_ref)
    arriving, leaving = {}, []
    for i, j in pairs:
        to = pl.ds(j * tokens + i * step, step)
        arriving[i, j] = pltpu.make_async_copy(there[j].at[pl.ds(i * step, step), lanes], here.at[to], in_sems.at[j, i])
        arriving[i, j].start()
    for i, j in pairs:
        arriving[i, j].wait()
        to = pl.ds(j * tokens + i * step, step)
        leaving.append(pltpu.make_async_copy(here.at[to], out_ref.at[to], out_sems.at[j, i]))
        leaving[-1].start()
    for copy in leaving:
        copy.wait()


def select_kernel(pos_ref, q_ref, out_ref, halves):
    core = lax.axis_index("sx") % 2
    q = q_ref[...].astype(jnp.float32).reshape(-1, FEAT).astype(jnp.bfloat16)
    for p in range(2):
        hot = slot_onehot(pos_ref[p : p + 1, :], jnp.bfloat16)
        picked = jnp.dot(hot, q, preferred_element_type=jnp.float32)
        for h in range(KEY_HEADS):
            lanes = slice((h % HALF) * FEAT, (h % HALF + 1) * FEAT)
            halves[p, h // HALF, :, lanes] = picked[h * SLOTS : (h + 1) * SLOTS].astype(jnp.bfloat16)
        for s in range(SLABS):
            out_ref[p * SLABS + s] = halves[p, half_of(core, s)]


def attend_kernel(x_ref, k_ref, v_ref, kv_ref, y_ref):
    scale = HEAD_WIDTH ** (-0.5) * LOG2E
    mine = half_of(lax.axis_index("sx") % 2, lax.axis_index("sy") % SLABS)
    columns, tokens = x_ref.shape[0], k_ref.shape[0]
    rows = columns * SLOTS
    ones = jnp.ones((tokens, HEAD_WIDTH), jnp.bfloat16)
    ends = []
    for h in range(HALF):
        x = x_ref[:, :, h * FEAT : (h + 1) * FEAT].astype(jnp.float32).reshape(rows, FEAT).astype(jnp.bfloat16)
        q = [x[:, g * HEAD_WIDTH : (g + 1) * HEAD_WIDTH] for g in range(QUERY_PER_KEY)]
        q = jnp.concatenate(q, axis=0)
        there = pl.ds(pl.multiple_of((mine * HALF + h) * HEAD_WIDTH, HEAD_WIDTH), HEAD_WIDTH)
        here = slice(h * HEAD_WIDTH, (h + 1) * HEAD_WIDTH)
        slabs = ((k_ref[:, there], v_ref[:, there]), (kv_ref[:tokens, here], kv_ref[tokens:, here]))
        tops, sums = [], []
        for k, v in slabs:
            v = jnp.concatenate([v, ones], axis=1)
            s = lax.dot_general(q, k, (((1,), (1,)), ((), ())), preferred_element_type=jnp.float32)
            m = jnp.max(s, axis=1, keepdims=True)
            w = jnp.exp2((s - m) * scale).astype(jnp.bfloat16)
            tops.append(m)
            sums.append(jnp.dot(w, v, preferred_element_type=jnp.float32))
        top = functools.reduce(jnp.maximum, tops)
        both = functools.reduce(jnp.add, [jnp.exp2((m - top) * scale) * o for m, o in zip(tops, sums)])
        total = both[:, HEAD_WIDTH:]
        out = both[:, :HEAD_WIDTH] / total
        lse = top * scale + jnp.log2(total[:, :1])
        for g in range(QUERY_PER_KEY):
            part = out[g * rows : (g + 1) * rows].reshape(columns, SLOTS, HEAD_WIDTH).astype(jnp.bfloat16)
            at = (h * QUERY_PER_KEY + g) * HEAD_WIDTH
            y_ref[:, :, at : at + HEAD_WIDTH] = part
            ends.append(lse[g * rows : (g + 1) * rows])
    stat = stat_lanes(ends).reshape(columns, SLOTS, STAT).astype(jnp.bfloat16)
    y_ref[:, :, HALF * FEAT :] = stat


def merge_kernel(pos_ref, y_ref, out_ref):
    core = lax.axis_index("sx") % 2
    flip = (((0,), (0,)), ((), ()))
    data, lse = [], []
    for p in range(2):
        tall = []
        for half in range(2):
            froms = [p * SLABS + jnp.where(core == 0, 2 * t + half, HALF * half + t) for t in range(4)]
            ends = []
            for s in froms:
                stat = y_ref[s, :, HALF * FEAT :].astype(jnp.float32)
                ends.append(stat + (pltpu.roll(stat, STAT - 1, 1) + pltpu.roll(stat, STAT - 2, 1)))
            top = functools.reduce(jnp.maximum, ends)
            weights = [jnp.exp2(x - top) for x in ends]
            total = functools.reduce(jnp.add, weights)
            inverse = 1.0 / total
            weights = [w * inverse for w in weights]
            block = top + jnp.log2(total)
            for h in range(HALF):
                pair = []
                for g in range(QUERY_PER_KEY):
                    n = h * QUERY_PER_KEY + g
                    lanes = slice(n * HEAD_WIDTH, (n + 1) * HEAD_WIDTH)
                    terms = [w[:, 3 * n : 3 * n + 1] * y_ref[s, :, lanes].astype(jnp.float32) for w, s in zip(weights, froms)]
                    pair.append(functools.reduce(jnp.add, terms))
                shift = 3 * h * QUERY_PER_KEY
                stat = block if shift == 0 else pltpu.roll(block, STAT - shift, 1)
                lane = lax.broadcasted_iota(jnp.int32, stat.shape, 1)
                stat = jnp.where(lane == ONE_LANE, 1.0, jnp.where(lane < ONE_LANE, stat, 0.0))
                tall.append(jnp.concatenate(pair + [stat], axis=1))
        hot = slot_onehot(pos_ref[p : p + 1, :], jnp.float32)
        dense = lax.dot_general(
            hot,
            jnp.concatenate(tall, axis=0),
            flip,
            precision=lax.Precision.HIGHEST,
            preferred_element_type=jnp.float32,
        )
        named = dense[:, FEAT + ONE_LANE : FEAT + ONE_LANE + 1] > 0.5
        data.append(dense)
        lse.append(
            [jnp.where(named, dense[:, FEAT + 3 * g : FEAT + 3 * g + 1], NEVER) for g in range(QUERY_PER_KEY)]
        )
    combine_two(data, lse, out_ref)


def combine_two(data, lse, out_ref):
    shape = out_ref.shape[:-1]
    ends = []
    for g in range(QUERY_PER_KEY):
        a, b = lse[0][g], lse[1][g]
        top = jnp.maximum(a, b)
        wa, wb = jnp.exp2(a - top), jnp.exp2(b - top)
        total = wa + wb
        inverse = 1.0 / total
        lanes = slice(g * HEAD_WIDTH, (g + 1) * HEAD_WIDTH)
        mixed = data[0][:, lanes] * (wa * inverse) + data[1][:, lanes] * (wb * inverse)
        out_ref[..., lanes] = mixed.reshape(*shape, HEAD_WIDTH).astype(out_ref.dtype)
        ends.append(top + jnp.log2(total))
    if out_ref.dtype == jnp.float32:
        lane = lax.broadcasted_iota(jnp.int32, (mixed.shape[0], STAT), 1)
        stat = jnp.zeros(lane.shape, jnp.float32)
        for g in range(QUERY_PER_KEY):
            stat = jnp.where(lane == g, ends[g], stat)
    else:
        stat = stat_lanes(ends)
    out_ref[..., FEAT:] = stat.reshape(*shape, STAT).astype(out_ref.dtype)


def pair_kernel(a_ref, out_ref):
    data = [a_ref[c, :, :FEAT] for c in range(2)]
    lse = [[a_ref[c, :, FEAT + g : FEAT + g + 1] for g in range(QUERY_PER_KEY)] for c in range(2)]
    combine_two(data, lse, out_ref)


def last_kernel(a_ref, out_ref):
    for g in range(QUERY_PER_KEY):
        at = FEAT + 3 * g
        lse = [a_ref[:, :, at + k : at + k + 1].astype(jnp.float32) for k in range(3)]
        lse = lse[0] + (lse[1] + lse[2])
        weight = jnp.exp2(lse - jnp.max(lse, axis=0, keepdims=True))
        total = jnp.sum(weight, axis=0)
        lanes = slice(g * HEAD_WIDTH, (g + 1) * HEAD_WIDTH)
        mixed = jnp.sum(a_ref[:, :, lanes].astype(jnp.float32) * weight, axis=0) / total
        for h in range(KEY_HEADS):
            head = h * FEAT + g * HEAD_WIDTH
            out_ref[:, head : head + HEAD_WIDTH] = mixed[h : h + 1].astype(jnp.bfloat16)


def call(kernel, shape, dtype, name, *args, scratch=()):
    return pl.pallas_call(
        kernel,
        out_shape=jax.ShapeDtypeStruct(shape, dtype),
        in_specs=[pl.BlockSpec(memory_space=pltpu.VMEM)] * len(args),
        out_specs=pl.BlockSpec(memory_space=pltpu.VMEM),
        scratch_shapes=list(scratch),
        compiler_params=pltpu.CompilerParams(vmem_limit_bytes=40 * 1024 * 1024),
        name=name,
    )(*args)


def per_device(queries, keys, values, block_ids):
    count_x = lax.axis_size("sx")
    count_y = lax.axis_size("sy")
    count_z = count_x // 2
    tokens = keys.shape[0]
    cores = [[2 * z, 2 * z + 1] for z in range(count_z)]
    along_z = [[2 * z + c for z in range(count_z)] for c in range(2)]
    partners = [
        (x * count_y + y, x * count_y + (y ^ PARTNER[x % 2])) for x in range(count_x) for y in range(count_y)
    ]

    def exchange(x, axis, groups=None):
        return lax.all_to_all(x, axis, split_axis=0, concat_axis=0, tiled=True, axis_index_groups=groups)

    own = jnp.broadcast_to(queries.reshape(1, KEY_HEADS, FEAT), (count_z, KEY_HEADS, FEAT))
    rows = exchange(own, "sx", along_z)

    hbm = pl.BlockSpec(memory_space=pltpu.HBM)
    width = HALF * HEAD_WIDTH
    kv = pl.pallas_call(
        relay_kernel,
        out_shape=jax.ShapeDtypeStruct((2 * tokens, width), keys.dtype),
        in_specs=[hbm, hbm],
        out_specs=hbm,
        scratch_shapes=[
            pltpu.VMEM((2 * tokens, width), keys.dtype),
            pltpu.SemaphoreType.DMA((2, 4)),
            pltpu.SemaphoreType.DMA((2, 4)),
        ],
        compiler_params=pltpu.CompilerParams(vmem_limit_bytes=60 * 1024 * 1024),
        name="relay",
    )(keys, values)
    kv = lax.ppermute(kv, ("sx", "sy"), partners)

    pos = call(find_kernel, (8, count_x * KEY_HEADS), jnp.float32, "find", block_ids.T)
    rows = lax.all_gather(rows, "sx", axis=0, axis_index_groups=cores)
    rows = rows.reshape(count_x, KEY_HEADS, FEAT)
    asked = call(
        select_kernel,
        (count_y, SLOTS, HALF * FEAT),
        jnp.bfloat16,
        "select",
        pos,
        rows,
        scratch=[pltpu.VMEM((2, 2, SLOTS, HALF * FEAT), jnp.bfloat16)],
    )
    asked = exchange(asked, "sy")
    part = call(attend_kernel, (count_y, SLOTS, HALF * FEAT + STAT), jnp.bfloat16, "attend", asked, keys, values, kv)
    part = exchange(part, "sy")
    part = call(merge_kernel, (2, count_z * KEY_HEADS, FEAT + STAT), jnp.float32, "merge", pos, part)
    part = exchange(part, "sx", cores)
    part = call(pair_kernel, (count_z, KEY_HEADS, FEAT + STAT), jnp.bfloat16, "pair", part)
    part = exchange(part, "sx", along_z)
    return call(last_kernel, (1, KEY_HEADS * FEAT), jnp.bfloat16, "last", part)


def solution(mesh):
    return jax.shard_map(
        per_device,
        mesh=mesh,
        in_specs=(P(("sx", "sy"), None), P(("sx", "sy"), None), P(("sx", "sy"), None), P()),
        out_specs=P(("sx", "sy"), None),
        check_vma=False,
    )
```

```python
import functools

import jax
import jax.numpy as jnp
from jax import lax
from jax.experimental import pallas as pl
from jax.experimental.pallas import tpu as pltpu
from jax.sharding import PartitionSpec as P

QUERY_HEADS = 32
KEY_HEADS = 8
HEAD_WIDTH = 128
BLOCK = 4096
QUERY_PER_KEY = 4
LOG2E = 1.4426950408889634
NEVER = -1e30

FEAT = QUERY_PER_KEY * HEAD_WIDTH
SLOTS = 8
SLABS = 8
SHARE = KEY_HEADS // 4
PARTNERS = ((1, 4, 5), (3, 4, 7))
STAT = 128
ONE_LANE = 12


def share_of(s):
    return (s // 4) * 2 + s % 2


def pieces(x):
    hi = x.astype(jnp.bfloat16).astype(jnp.float32)
    rest = x - hi
    mid = rest.astype(jnp.bfloat16).astype(jnp.float32)
    return hi, mid, rest - mid


def stat_lanes(lse):
    lane = lax.broadcasted_iota(jnp.int32, (lse[0].shape[0], STAT), 1)
    stat = jnp.zeros(lane.shape, jnp.float32)
    for at, x in enumerate(lse):
        for k, piece in enumerate(pieces(x)):
            stat = jnp.where(lane == at * 3 + k, piece, stat)
    return stat


def find_kernel(ids_ref, pos_ref):
    count_x, count_y = lax.axis_size("sx"), lax.axis_size("sy")
    index_x, index_y = lax.axis_index("sx"), lax.axis_index("sy")
    lanes = 128
    r = lax.broadcasted_iota(jnp.int32, (count_x * count_y, lanes), 0)
    c = lax.broadcasted_iota(jnp.int32, (count_x * count_y, lanes), 1)
    row = (c % (count_x // 2)) * 2 + c // (count_x // 2)
    own = jnp.where((r == row * count_y + index_y) & (c < count_x), 1.0, 0.0).astype(jnp.bfloat16)
    ids = ids_ref[...].astype(jnp.float32).astype(jnp.bfloat16)
    column = jnp.dot(ids, own, preferred_element_type=jnp.float32)
    b = lax.broadcasted_iota(jnp.int32, (8, lanes), 0)
    c = lax.broadcasted_iota(jnp.int32, (8, lanes), 1)
    named = jnp.zeros((8, lanes), jnp.float32)
    for block in range(2):
        wanted = (index_x * 2 + block).astype(jnp.float32)
        hit = jnp.max(jnp.where(column == wanted, 1.0, 0.0), axis=0, keepdims=True)
        named = jnp.where((b == block) & (c < count_x), hit, named)
    r = lax.broadcasted_iota(jnp.int32, (lanes, lanes), 0)
    c = lax.broadcasted_iota(jnp.int32, (lanes, lanes), 1)
    before = jnp.where(r < c, 1.0, 0.0).astype(jnp.bfloat16)
    rank = jnp.dot(named.astype(jnp.bfloat16), before, preferred_element_type=jnp.float32)
    pos = jnp.where(named > 0.5, rank, -1.0).astype(jnp.bfloat16)
    shape = (lanes, pos_ref.shape[1])
    r = lax.broadcasted_iota(jnp.int32, shape, 0)
    c = lax.broadcasted_iota(jnp.int32, shape, 1)
    heads = jnp.where(r == c // KEY_HEADS, 1.0, 0.0).astype(jnp.bfloat16)
    pos_ref[...] = jnp.dot(pos, heads, preferred_element_type=jnp.float32)


def slot_onehot(pos):
    shape = (KEY_HEADS * SLOTS, pos.shape[1])
    r = lax.broadcasted_iota(jnp.int32, shape, 0)
    c = lax.broadcasted_iota(jnp.int32, shape, 1)
    hit = (pos == (r % SLOTS).astype(jnp.float32)) & (r // SLOTS == c % KEY_HEADS)
    return jnp.where(hit, 1.0, 0.0).astype(jnp.bfloat16)


def copies_kernel(q_ref, out_ref):
    q = q_ref[...].astype(jnp.float32)
    q = jnp.concatenate([q[:, h * FEAT : (h + 1) * FEAT] for h in range(KEY_HEADS)], axis=0).astype(jnp.bfloat16)
    for z in range(out_ref.shape[0]):
        out_ref[z] = q


def relay_kernel(k_ref, v_ref, *refs):
    count = len(PARTNERS[0])
    out_refs, (here, in_sems, out_sems) = refs[:count], refs[count:]
    core, s = lax.axis_index("sx") % 2, lax.axis_index("sy") % SLABS
    tokens, width = k_ref.shape[0], out_refs[0].shape[1]
    there = (k_ref, v_ref)
    arriving, leaving = {}, []
    for i in range(count):
        partner = jnp.bitwise_xor(s, jnp.where(core == 0, PARTNERS[0][i], PARTNERS[1][i]))
        lanes = pl.ds(pl.multiple_of(share_of(partner) * width, width), width)
        for j in range(2):
            to = here.at[i, pl.ds(j * tokens, tokens)]
            arriving[i, j] = pltpu.make_async_copy(there[j].at[:, lanes], to, in_sems.at[i, j])
            arriving[i, j].start()
    for i in range(count):
        for j in range(2):
            arriving[i, j].wait()
            part = pl.ds(j * tokens, tokens)
            leaving.append(pltpu.make_async_copy(here.at[i, part], out_refs[i].at[part], out_sems.at[i, j]))
            leaving[-1].start()
    for copy in leaving:
        copy.wait()


def select_kernel(pos_ref, q_ref, out_ref):
    q = q_ref[...].astype(jnp.float32).reshape(-1, FEAT).astype(jnp.bfloat16)
    for p in range(2):
        hot = slot_onehot(pos_ref[p : p + 1, :])
        picked = jnp.dot(hot, q, preferred_element_type=jnp.float32).astype(jnp.bfloat16)
        heads = [picked[h * SLOTS : (h + 1) * SLOTS] for h in range(KEY_HEADS)]
        for s in range(SLABS):
            for h in range(SHARE):
                out_ref[p * SLABS + s, :, h * FEAT : (h + 1) * FEAT] = heads[share_of(s) * SHARE + h]


def attend_kernel(x_ref, k_ref, v_ref, *refs):
    kv_refs, y_ref = refs[:-1], refs[-1]
    scale = HEAD_WIDTH ** (-0.5) * LOG2E
    mine = share_of(lax.axis_index("sy") % SLABS)
    columns, tokens = x_ref.shape[0], k_ref.shape[0]
    rows = columns * SLOTS
    ones = jnp.ones((tokens, HEAD_WIDTH), jnp.bfloat16)
    ends = []
    for h in range(SHARE):
        x = x_ref[:, :, h * FEAT : (h + 1) * FEAT].astype(jnp.float32).reshape(rows, FEAT).astype(jnp.bfloat16)
        q = [x[:, g * HEAD_WIDTH : (g + 1) * HEAD_WIDTH] for g in range(QUERY_PER_KEY)]
        q = jnp.concatenate(q, axis=0)
        there = pl.ds(pl.multiple_of((mine * SHARE + h) * HEAD_WIDTH, HEAD_WIDTH), HEAD_WIDTH)
        here = slice(h * HEAD_WIDTH, (h + 1) * HEAD_WIDTH)
        slabs = [(k_ref[:, there], v_ref[:, there])]
        slabs += [(kv_ref[:tokens, here], kv_ref[tokens:, here]) for kv_ref in kv_refs]
        tops, sums = [], []
        for k, v in slabs:
            v = jnp.concatenate([v, ones], axis=1)
            s = lax.dot_general(q, k, (((1,), (1,)), ((), ())), preferred_element_type=jnp.float32)
            m = jnp.max(s, axis=1, keepdims=True)
            w = jnp.exp2((s - m) * scale).astype(jnp.bfloat16)
            tops.append(m)
            sums.append(jnp.dot(w, v, preferred_element_type=jnp.float32))
        top = functools.reduce(jnp.maximum, tops)
        both = functools.reduce(jnp.add, [jnp.exp2((m - top) * scale) * o for m, o in zip(tops, sums)])
        total = both[:, HEAD_WIDTH:]
        out = both[:, :HEAD_WIDTH] / total
        lse = top * scale + jnp.log2(total[:, :1])
        for g in range(QUERY_PER_KEY):
            part = out[g * rows : (g + 1) * rows].reshape(columns, SLOTS, HEAD_WIDTH).astype(jnp.bfloat16)
            at = (h * QUERY_PER_KEY + g) * HEAD_WIDTH
            y_ref[:, :, at : at + HEAD_WIDTH] = part
            ends.append(lse[g * rows : (g + 1) * rows])
    stat = stat_lanes(ends).reshape(columns, SLOTS, STAT).astype(jnp.bfloat16)
    y_ref[:, :, SHARE * FEAT :] = stat


def merge_kernel(pos_ref, y_ref, mine_ref, theirs_ref):
    core = lax.axis_index("sx") % 2
    flip = (((0,), (0,)), ((), ()))
    lane = lax.broadcasted_iota(jnp.int32, (SLOTS, STAT), 1)
    data, lse = [], []
    for p in range(2):
        tall = []
        for share in range(4):
            froms = [p * SLABS + s for s in range(SLABS) if share_of(s) == share]
            ends = []
            for s in froms:
                stat = y_ref[s, :, SHARE * FEAT :].astype(jnp.float32)
                ends.append(stat + (pltpu.roll(stat, STAT - 1, 1) + pltpu.roll(stat, STAT - 2, 1)))
            top = functools.reduce(jnp.maximum, ends)
            weights = [jnp.exp2(x - top) for x in ends]
            total = functools.reduce(jnp.add, weights)
            inverse = 1.0 / total
            weights = [w * inverse for w in weights]
            block = top + jnp.log2(total)
            for h in range(SHARE):
                heads = []
                for g in range(QUERY_PER_KEY):
                    n = h * QUERY_PER_KEY + g
                    lanes = slice(n * HEAD_WIDTH, (n + 1) * HEAD_WIDTH)
                    terms = [w[:, 3 * n : 3 * n + 1] * y_ref[s, :, lanes].astype(jnp.float32) for w, s in zip(weights, froms)]
                    heads.append(functools.reduce(jnp.add, terms))
                shift = 3 * h * QUERY_PER_KEY
                stat = block if shift == 0 else pltpu.roll(block, STAT - shift, 1)
                stat = jnp.where(lane == ONE_LANE, 1.0, jnp.where(lane < ONE_LANE, stat, 0.0))
                tall.append(jnp.concatenate(heads + [stat], axis=1))
        tall = jnp.concatenate([x.astype(jnp.bfloat16) for x in pieces(jnp.concatenate(tall, axis=0))], axis=0)
        hot = jnp.concatenate([slot_onehot(pos_ref[p : p + 1, :])] * 3, axis=0)
        dense = lax.dot_general(hot, tall, flip, preferred_element_type=jnp.float32)
        named = dense[:, FEAT + ONE_LANE : FEAT + ONE_LANE + 1] > 0.5
        data.append(dense)
        lse.append(
            [jnp.where(named, dense[:, FEAT + 3 * g : FEAT + 3 * g + 1], NEVER) for g in range(QUERY_PER_KEY)]
        )
    rows = mine_ref.shape[0]
    for out_ref, is_first in ((mine_ref, core == 0), (theirs_ref, core == 1)):

        def side(x):
            return jnp.where(is_first, x[:rows], x[rows:])

        combine_two([side(x) for x in data], [[side(x) for x in y] for y in lse], out_ref)


def combine_two(data, lse, out_ref):
    shape = out_ref.shape[:-1]
    ends = []
    for g in range(QUERY_PER_KEY):
        a, b = lse[0][g], lse[1][g]
        top = jnp.maximum(a, b)
        wa, wb = jnp.exp2(a - top), jnp.exp2(b - top)
        total = wa + wb
        inverse = 1.0 / total
        lanes = slice(g * HEAD_WIDTH, (g + 1) * HEAD_WIDTH)
        mixed = data[0][:, lanes] * (wa * inverse) + data[1][:, lanes] * (wb * inverse)
        out_ref[..., lanes] = mixed.reshape(*shape, HEAD_WIDTH).astype(out_ref.dtype)
        ends.append(top + jnp.log2(total))
    if out_ref.dtype == jnp.float32:
        lane = lax.broadcasted_iota(jnp.int32, (mixed.shape[0], STAT), 1)
        stat = jnp.zeros(lane.shape, jnp.float32)
        for g in range(QUERY_PER_KEY):
            stat = jnp.where(lane == g, ends[g], stat)
    else:
        stat = stat_lanes(ends)
    out_ref[..., FEAT:] = stat.reshape(*shape, STAT).astype(out_ref.dtype)


def pair_kernel(mine_ref, pair_ref, out_ref):
    other = 1 - lax.axis_index("sx") % 2
    data = [mine_ref[:, :FEAT], pair_ref[other, :, :FEAT]]
    lse = [[x[:, g : g + 1] for g in range(QUERY_PER_KEY)] for x in (mine_ref[:, FEAT:], pair_ref[other, :, FEAT:])]
    combine_two(data, lse, out_ref)


def last_kernel(a_ref, out_ref):
    stat = a_ref[:, :, FEAT:].astype(jnp.float32)
    lse = stat + (pltpu.roll(stat, STAT - 1, 2) + pltpu.roll(stat, STAT - 2, 2))
    weight = jnp.exp2(lse - jnp.max(lse, axis=0, keepdims=True))
    weight = weight / jnp.sum(weight, axis=0, keepdims=True)
    for g in range(QUERY_PER_KEY):
        lanes = slice(g * HEAD_WIDTH, (g + 1) * HEAD_WIDTH)
        mixed = jnp.sum(a_ref[:, :, lanes].astype(jnp.float32) * weight[:, :, 3 * g : 3 * g + 1], axis=0)
        for h in range(KEY_HEADS):
            head = h * FEAT + g * HEAD_WIDTH
            out_ref[:, head : head + HEAD_WIDTH] = mixed[h : h + 1].astype(jnp.bfloat16)


def call(kernel, out, name, *args):
    return pl.pallas_call(
        kernel,
        out_shape=out,
        in_specs=[pl.BlockSpec(memory_space=pltpu.VMEM)] * len(args),
        out_specs=jax.tree.map(lambda _: pl.BlockSpec(memory_space=pltpu.VMEM), out),
        compiler_params=pltpu.CompilerParams(vmem_limit_bytes=40 * 1024 * 1024),
        name=name,
    )(*args)


def per_device(queries, keys, values, block_ids):
    count_x = lax.axis_size("sx")
    count_y = lax.axis_size("sy")
    count_z = count_x // 2
    tokens = keys.shape[0]
    cores = [[2 * z, 2 * z + 1] for z in range(count_z)]
    along_z = [[2 * z + c for z in range(count_z)] for c in range(2)]

    def exchange(x, axis, groups=None):
        return lax.all_to_all(x, axis, split_axis=0, concat_axis=0, tiled=True, axis_index_groups=groups)

    def swap(x, i):
        pairs = [(a * count_y + b, a * count_y + (b ^ PARTNERS[a % 2][i])) for a in range(count_x) for b in range(count_y)]
        return lax.ppermute(x, ("sx", "sy"), pairs)

    def half(*shape):
        return jax.ShapeDtypeStruct(shape, jnp.bfloat16)

    def full(*shape):
        return jax.ShapeDtypeStruct(shape, jnp.float32)

    own = call(copies_kernel, half(count_z, KEY_HEADS, FEAT), "copies", queries)
    rows = exchange(own, "sx", along_z)

    hbm = pl.BlockSpec(memory_space=pltpu.HBM)
    width = SHARE * HEAD_WIDTH
    count = len(PARTNERS[0])
    kv = pl.pallas_call(
        relay_kernel,
        out_shape=[half(2 * tokens, width)] * count,
        in_specs=[hbm, hbm],
        out_specs=[hbm] * count,
        scratch_shapes=[
            pltpu.VMEM((count, 2 * tokens, width), jnp.bfloat16),
            pltpu.SemaphoreType.DMA((count, 2)),
            pltpu.SemaphoreType.DMA((count, 2)),
        ],
        compiler_params=pltpu.CompilerParams(vmem_limit_bytes=60 * 1024 * 1024),
        name="relay",
    )(keys, values)
    kv = [swap(x, i) for i, x in enumerate(kv)]

    pos = call(find_kernel, full(8, count_x * KEY_HEADS), "find", block_ids.T)
    rows = lax.all_gather(rows, "sx", axis=0, axis_index_groups=cores)
    rows = rows.reshape(count_x, KEY_HEADS, FEAT)
    asked = call(select_kernel, half(count_y, SLOTS, SHARE * FEAT), "select", pos, rows)
    asked = exchange(asked, "sy")
    part = call(attend_kernel, half(count_y, SLOTS, SHARE * FEAT + STAT), "attend", asked, keys, values, *kv)
    part = exchange(part, "sy")
    side = full(count_z * KEY_HEADS, FEAT + STAT)
    mine, theirs = call(merge_kernel, [side, side], "merge", pos, part)
    pair = lax.all_gather(theirs, "sx", axis=0, axis_index_groups=cores)
    part = call(pair_kernel, half(count_z, KEY_HEADS, FEAT + STAT), "pair", mine, pair)
    part = exchange(part, "sx", along_z)
    return call(last_kernel, half(1, KEY_HEADS * FEAT), "last", part)


def solution(mesh):
    return jax.shard_map(
        per_device,
        mesh=mesh,
        in_specs=(P(("sx", "sy"), None), P(("sx", "sy"), None), P(("sx", "sy"), None), P()),
        out_specs=P(("sx", "sy"), None),
        check_vma=False,
    )
```

```python
import functools

import jax
import jax.numpy as jnp
from jax import lax
from jax.experimental import pallas as pl
from jax.experimental.pallas import tpu as pltpu
from jax.sharding import PartitionSpec as P

QUERY_HEADS = 32
KEY_HEADS = 8
HEAD_WIDTH = 128
BLOCK = 4096
QUERY_PER_KEY = 4
LOG2E = 1.4426950408889634
NEVER = -1e30

FEAT = QUERY_PER_KEY * HEAD_WIDTH
SLOTS = 8
SLABS = 8
HALF = KEY_HEADS // 2
PARTNER = (1, 4)
STAT = 128
ONE_LANE = 12


ASK_FIRST = 11
ANSWER_FIRST = 8


def z_order(count, first):
    return [(i + first) % count for i in range(count)]


def half_of(core, s):
    return jnp.where(core == 0, s % 2, s // 4)


def pieces(x):
    hi = x.astype(jnp.bfloat16).astype(jnp.float32)
    rest = x - hi
    mid = rest.astype(jnp.bfloat16).astype(jnp.float32)
    return hi, mid, rest - mid


def stat_lanes(lse):
    lane = lax.broadcasted_iota(jnp.int32, (lse[0].shape[0], STAT), 1)
    stat = jnp.zeros(lane.shape, jnp.float32)
    for at, x in enumerate(lse):
        for k, piece in enumerate(pieces(x)):
            stat = jnp.where(lane == at * 3 + k, piece, stat)
    return stat


def find_kernel(ids_ref, ask_ref, answer_ref):
    count_x, count_y = lax.axis_size("sx"), lax.axis_size("sy")
    index_x, index_y = lax.axis_index("sx"), lax.axis_index("sy")
    count_z = count_x // 2
    lanes = 128
    r = lax.broadcasted_iota(jnp.int32, (count_x * count_y, lanes), 0)
    c = lax.broadcasted_iota(jnp.int32, (count_x * count_y, lanes), 1)
    own = jnp.where((r == c * count_y + index_y) & (c < count_x), 1.0, 0.0).astype(jnp.bfloat16)
    ids = ids_ref[...].astype(jnp.float32).astype(jnp.bfloat16)
    column = jnp.dot(ids, own, preferred_element_type=jnp.float32)
    b = lax.broadcasted_iota(jnp.int32, (8, lanes), 0)
    c = lax.broadcasted_iota(jnp.int32, (8, lanes), 1)
    named = jnp.zeros((8, lanes), jnp.float32)
    for block in range(2):
        wanted = (index_x * 2 + block).astype(jnp.float32)
        hit = jnp.max(jnp.where(column == wanted, 1.0, 0.0), axis=0, keepdims=True)
        named = jnp.where((b == block) & (c < count_x), hit, named)
    r = lax.broadcasted_iota(jnp.int32, (lanes, lanes), 0)
    c = lax.broadcasted_iota(jnp.int32, (lanes, lanes), 1)
    before = jnp.where(r < c, 1.0, 0.0).astype(jnp.bfloat16)
    rank = jnp.dot(named.astype(jnp.bfloat16), before, preferred_element_type=jnp.float32)
    pos = jnp.where(named > 0.5, rank, -1.0).astype(jnp.bfloat16)
    for out_ref, first in ((ask_ref, ASK_FIRST), (answer_ref, ANSWER_FIRST)):
        shape = (lanes, out_ref.shape[1])
        r = lax.broadcasted_iota(jnp.int32, shape, 0)
        c = lax.broadcasted_iota(jnp.int32, shape, 1) // KEY_HEADS
        row = ((c + first) % count_z) * 2 + c // count_z
        spread = jnp.where(r == row, 1.0, 0.0).astype(jnp.bfloat16)
        out_ref[...] = jnp.dot(pos, spread, preferred_element_type=jnp.float32)


def slot_onehot(pos):
    shape = (KEY_HEADS * SLOTS, pos.shape[1])
    r = lax.broadcasted_iota(jnp.int32, shape, 0)
    c = lax.broadcasted_iota(jnp.int32, shape, 1)
    hit = (pos == (r % SLOTS).astype(jnp.float32)) & (r // SLOTS == c % KEY_HEADS)
    return jnp.where(hit, 1.0, 0.0).astype(jnp.bfloat16)


def copies_kernel(q_ref, out_ref):
    q = q_ref[...].astype(jnp.float32)
    q = jnp.concatenate([q[:, h * FEAT : (h + 1) * FEAT] for h in range(KEY_HEADS)], axis=0).astype(jnp.bfloat16)
    for z in range(out_ref.shape[0]):
        out_ref[z] = q


def relay_kernel(k_ref, v_ref, out_ref, here, in_sems, out_sems):
    core = lax.axis_index("sx") % 2
    theirs = 1 - half_of(core, lax.axis_index("sy") % SLABS)
    tokens, width = k_ref.shape[0], out_ref.shape[1]
    lanes = pl.ds(pl.multiple_of(theirs * width, width), width)
    chunks = in_sems.shape[1]
    step = tokens // chunks
    pairs = [(i, j) for i in range(chunks) for j in range(2)]
    there = (k_ref, v_ref)
    arriving, leaving = {}, []
    for i, j in pairs:
        to = pl.ds(j * tokens + i * step, step)
        arriving[i, j] = pltpu.make_async_copy(there[j].at[pl.ds(i * step, step), lanes], here.at[to], in_sems.at[j, i])
        arriving[i, j].start()
    for i, j in pairs:
        arriving[i, j].wait()
        to = pl.ds(j * tokens + i * step, step)
        leaving.append(pltpu.make_async_copy(here.at[to], out_ref.at[to], out_sems.at[j, i]))
        leaving[-1].start()
    for copy in leaving:
        copy.wait()


def select_kernel(pos_ref, q_ref, out_ref, halves):
    core = lax.axis_index("sx") % 2
    q = q_ref[...].astype(jnp.float32).reshape(-1, FEAT).astype(jnp.bfloat16)
    for p in range(2):
        hot = slot_onehot(pos_ref[p : p + 1, :])
        picked = jnp.dot(hot, q, preferred_element_type=jnp.float32)
        for h in range(KEY_HEADS):
            lanes = slice((h % HALF) * FEAT, (h % HALF + 1) * FEAT)
            halves[p, h // HALF, :, lanes] = picked[h * SLOTS : (h + 1) * SLOTS].astype(jnp.bfloat16)
        for s in range(SLABS):
            out_ref[p * SLABS + s] = halves[p, half_of(core, s)]


def attend_kernel(x_ref, k_ref, v_ref, kv_ref, y_ref):
    scale = HEAD_WIDTH ** (-0.5) * LOG2E
    mine = half_of(lax.axis_index("sx") % 2, lax.axis_index("sy") % SLABS)
    columns, tokens = x_ref.shape[0], k_ref.shape[0]
    rows = columns * SLOTS
    ones = jnp.ones((tokens, HEAD_WIDTH), jnp.bfloat16)
    ends = []
    for h in range(HALF):
        x = x_ref[:, :, h * FEAT : (h + 1) * FEAT].astype(jnp.float32).reshape(rows, FEAT).astype(jnp.bfloat16)
        q = [x[:, g * HEAD_WIDTH : (g + 1) * HEAD_WIDTH] for g in range(QUERY_PER_KEY)]
        q = jnp.concatenate(q, axis=0)
        there = pl.ds(pl.multiple_of((mine * HALF + h) * HEAD_WIDTH, HEAD_WIDTH), HEAD_WIDTH)
        here = slice(h * HEAD_WIDTH, (h + 1) * HEAD_WIDTH)
        slabs = ((k_ref[:, there], v_ref[:, there]), (kv_ref[:tokens, here], kv_ref[tokens:, here]))
        tops, sums = [], []
        for k, v in slabs:
            v = jnp.concatenate([v, ones], axis=1)
            s = lax.dot_general(q, k, (((1,), (1,)), ((), ())), preferred_element_type=jnp.float32)
            m = jnp.max(s, axis=1, keepdims=True)
            w = jnp.exp2((s - m) * scale).astype(jnp.bfloat16)
            tops.append(m)
            sums.append(jnp.dot(w, v, preferred_element_type=jnp.float32))
        top = functools.reduce(jnp.maximum, tops)
        both = functools.reduce(jnp.add, [jnp.exp2((m - top) * scale) * o for m, o in zip(tops, sums)])
        total = both[:, HEAD_WIDTH:]
        out = both[:, :HEAD_WIDTH] / total
        lse = top * scale + jnp.log2(total[:, :1])
        for g in range(QUERY_PER_KEY):
            part = out[g * rows : (g + 1) * rows].reshape(columns, SLOTS, HEAD_WIDTH).astype(jnp.bfloat16)
            at = (h * QUERY_PER_KEY + g) * HEAD_WIDTH
            y_ref[:, :, at : at + HEAD_WIDTH] = part
            ends.append(lse[g * rows : (g + 1) * rows])
    stat = stat_lanes(ends).reshape(columns, SLOTS, STAT).astype(jnp.bfloat16)
    y_ref[:, :, HALF * FEAT :] = stat


def merge_kernel(pos_ref, y_ref, mine_ref, theirs_ref):
    core = lax.axis_index("sx") % 2
    flip = (((0,), (0,)), ((), ()))
    lane = lax.broadcasted_iota(jnp.int32, (SLOTS, STAT), 1)
    data, lse = [], []
    for p in range(2):
        tall = []
        for half in range(2):
            froms = [p * SLABS + jnp.where(core == 0, 2 * t + half, HALF * half + t) for t in range(4)]
            ends = []
            for s in froms:
                stat = y_ref[s, :, HALF * FEAT :].astype(jnp.float32)
                ends.append(stat + (pltpu.roll(stat, STAT - 1, 1) + pltpu.roll(stat, STAT - 2, 1)))
            top = functools.reduce(jnp.maximum, ends)
            weights = [jnp.exp2(x - top) for x in ends]
            total = functools.reduce(jnp.add, weights)
            inverse = 1.0 / total
            weights = [w * inverse for w in weights]
            block = top + jnp.log2(total)
            for h in range(HALF):
                heads = []
                for g in range(QUERY_PER_KEY):
                    n = h * QUERY_PER_KEY + g
                    lanes = slice(n * HEAD_WIDTH, (n + 1) * HEAD_WIDTH)
                    terms = [w[:, 3 * n : 3 * n + 1] * y_ref[s, :, lanes].astype(jnp.float32) for w, s in zip(weights, froms)]
                    heads.append(functools.reduce(jnp.add, terms))
                shift = 3 * h * QUERY_PER_KEY
                stat = block if shift == 0 else pltpu.roll(block, STAT - shift, 1)
                stat = jnp.where(lane == ONE_LANE, 1.0, jnp.where(lane < ONE_LANE, stat, 0.0))
                tall.append(jnp.concatenate(heads + [stat], axis=1))
        tall = jnp.concatenate([x.astype(jnp.bfloat16) for x in pieces(jnp.concatenate(tall, axis=0))], axis=0)
        hot = jnp.concatenate([slot_onehot(pos_ref[p : p + 1, :])] * 3, axis=0)
        dense = lax.dot_general(hot, tall, flip, preferred_element_type=jnp.float32)
        named = dense[:, FEAT + ONE_LANE : FEAT + ONE_LANE + 1] > 0.5
        data.append(dense)
        lse.append(
            [jnp.where(named, dense[:, FEAT + 3 * g : FEAT + 3 * g + 1], NEVER) for g in range(QUERY_PER_KEY)]
        )
    rows = mine_ref.shape[0]
    for out_ref, is_first in ((mine_ref, core == 0), (theirs_ref, core == 1)):

        def side(x):
            return jnp.where(is_first, x[:rows], x[rows:])

        combine_two([side(x) for x in data], [[side(x) for x in y] for y in lse], out_ref)


def combine_two(data, lse, out_ref):
    shape = out_ref.shape[:-1]
    ends = []
    for g in range(QUERY_PER_KEY):
        a, b = lse[0][g], lse[1][g]
        top = jnp.maximum(a, b)
        wa, wb = jnp.exp2(a - top), jnp.exp2(b - top)
        total = wa + wb
        inverse = 1.0 / total
        lanes = slice(g * HEAD_WIDTH, (g + 1) * HEAD_WIDTH)
        mixed = data[0][:, lanes] * (wa * inverse) + data[1][:, lanes] * (wb * inverse)
        out_ref[..., lanes] = mixed.reshape(*shape, HEAD_WIDTH).astype(out_ref.dtype)
        ends.append(top + jnp.log2(total))
    if out_ref.dtype == jnp.float32:
        lane = lax.broadcasted_iota(jnp.int32, (mixed.shape[0], STAT), 1)
        stat = jnp.zeros(lane.shape, jnp.float32)
        for g in range(QUERY_PER_KEY):
            stat = jnp.where(lane == g, ends[g], stat)
    else:
        stat = stat_lanes(ends)
    out_ref[..., FEAT:] = stat.reshape(*shape, STAT).astype(out_ref.dtype)


def pair_kernel(mine_ref, pair_ref, out_ref):
    other = 1 - lax.axis_index("sx") % 2
    data = [mine_ref[:, :FEAT], pair_ref[other, :, :FEAT]]
    lse = [[x[:, g : g + 1] for g in range(QUERY_PER_KEY)] for x in (mine_ref[:, FEAT:], pair_ref[other, :, FEAT:])]
    combine_two(data, lse, out_ref)


def last_kernel(a_ref, out_ref):
    stat = a_ref[:, :, FEAT:].astype(jnp.float32)
    lse = stat + (pltpu.roll(stat, STAT - 1, 2) + pltpu.roll(stat, STAT - 2, 2))
    weight = jnp.exp2(lse - jnp.max(lse, axis=0, keepdims=True))
    weight = weight / jnp.sum(weight, axis=0, keepdims=True)
    for g in range(QUERY_PER_KEY):
        lanes = slice(g * HEAD_WIDTH, (g + 1) * HEAD_WIDTH)
        mixed = jnp.sum(a_ref[:, :, lanes].astype(jnp.float32) * weight[:, :, 3 * g : 3 * g + 1], axis=0)
        for h in range(KEY_HEADS):
            head = h * FEAT + g * HEAD_WIDTH
            out_ref[:, head : head + HEAD_WIDTH] = mixed[h : h + 1].astype(jnp.bfloat16)


def call(kernel, out, name, *args, scratch=()):
    return pl.pallas_call(
        kernel,
        out_shape=out,
        in_specs=[pl.BlockSpec(memory_space=pltpu.VMEM)] * len(args),
        out_specs=jax.tree.map(lambda _: pl.BlockSpec(memory_space=pltpu.VMEM), out),
        scratch_shapes=list(scratch),
        compiler_params=pltpu.CompilerParams(vmem_limit_bytes=40 * 1024 * 1024),
        name=name,
    )(*args)


def per_device(queries, keys, values, block_ids):
    count_x = lax.axis_size("sx")
    count_y = lax.axis_size("sy")
    count_z = count_x // 2
    tokens = keys.shape[0]
    cores = [[2 * z, 2 * z + 1] for z in range(count_z)]
    ask_groups, answer_groups = (
        [[2 * z + c for z in z_order(count_z, first)] for c in range(2)] for first in (ASK_FIRST, ANSWER_FIRST)
    )
    partners = [
        (x * count_y + y, x * count_y + (y ^ PARTNER[x % 2])) for x in range(count_x) for y in range(count_y)
    ]

    def exchange(x, axis, groups=None):
        return lax.all_to_all(x, axis, split_axis=0, concat_axis=0, tiled=True, axis_index_groups=groups)

    def half(*shape):
        return jax.ShapeDtypeStruct(shape, jnp.bfloat16)

    def full(*shape):
        return jax.ShapeDtypeStruct(shape, jnp.float32)

    own = call(copies_kernel, half(count_z, KEY_HEADS, FEAT), "copies", queries)
    rows = exchange(own, "sx", ask_groups)

    hbm = pl.BlockSpec(memory_space=pltpu.HBM)
    width = HALF * HEAD_WIDTH
    kv = pl.pallas_call(
        relay_kernel,
        out_shape=half(2 * tokens, width),
        in_specs=[hbm, hbm],
        out_specs=hbm,
        scratch_shapes=[
            pltpu.VMEM((2 * tokens, width), jnp.bfloat16),
            pltpu.SemaphoreType.DMA((2, 4)),
            pltpu.SemaphoreType.DMA((2, 4)),
        ],
        compiler_params=pltpu.CompilerParams(vmem_limit_bytes=60 * 1024 * 1024),
        name="relay",
    )(keys, values)
    kv = lax.ppermute(kv, ("sx", "sy"), partners)

    pos = full(8, count_x * KEY_HEADS)
    ask_pos, answer_pos = call(find_kernel, [pos, pos], "find", block_ids.T)
    rows = lax.all_gather(rows, "sx", axis=0, axis_index_groups=cores)
    rows = rows.reshape(count_x, KEY_HEADS, FEAT)
    asked = call(
        select_kernel,
        half(count_y, SLOTS, HALF * FEAT),
        "select",
        ask_pos,
        rows,
        scratch=[pltpu.VMEM((2, 2, SLOTS, HALF * FEAT), jnp.bfloat16)],
    )
    asked = exchange(asked, "sy")
    part = call(attend_kernel, half(count_y, SLOTS, HALF * FEAT + STAT), "attend", asked, keys, values, kv)
    part = exchange(part, "sy")
    side = full(count_z * KEY_HEADS, FEAT + STAT)
    mine, theirs = call(merge_kernel, [side, side], "merge", answer_pos, part)
    pair = lax.all_gather(theirs, "sx", axis=0, axis_index_groups=cores)
    part = call(pair_kernel, half(count_z, KEY_HEADS, FEAT + STAT), "pair", mine, pair)
    part = exchange(part, "sx", answer_groups)
    return call(last_kernel, half(1, KEY_HEADS * FEAT), "last", part)


def solution(mesh):
    return jax.shard_map(
        per_device,
        mesh=mesh,
        in_specs=(P(("sx", "sy"), None), P(("sx", "sy"), None), P(("sx", "sy"), None), P()),
        out_specs=P(("sx", "sy"), None),
        check_vma=False,
    )
```

```python
import functools

import jax
import jax.numpy as jnp
from jax import lax
from jax.experimental import pallas as pl
from jax.experimental.pallas import tpu as pltpu
from jax.sharding import PartitionSpec as P

QUERY_HEADS = 32
KEY_HEADS = 8
HEAD_WIDTH = 128
BLOCK = 4096
QUERY_PER_KEY = 4
LOG2E = 1.4426950408889634
NEVER = -1e30

FEAT = QUERY_PER_KEY * HEAD_WIDTH
SLOTS = 8
SLABS = 8
HALF = KEY_HEADS // 2
PARTNER = (1, 4)
STAT = 128
ONE_LANE = 12


ASK_FIRST = 11
ANSWER_FIRST = 8


COLUMN_FIRST = 10


def listed_from(first, count):
    return [(i + first) % count for i in range(count)]


def column_at(i):
    return (i - COLUMN_FIRST) % (2 * SLABS)


def half_of(core, s):
    return jnp.where(core == 0, s % 2, s // 4)


def pieces(x):
    hi = x.astype(jnp.bfloat16).astype(jnp.float32)
    rest = x - hi
    mid = rest.astype(jnp.bfloat16).astype(jnp.float32)
    return hi, mid, rest - mid


def stat_lanes(lse):
    lane = lax.broadcasted_iota(jnp.int32, (lse[0].shape[0], STAT), 1)
    stat = jnp.zeros(lane.shape, jnp.float32)
    for at, x in enumerate(lse):
        for k, piece in enumerate(pieces(x)):
            stat = jnp.where(lane == at * 3 + k, piece, stat)
    return stat


def find_kernel(ids_ref, ask_ref, answer_ref):
    count_x, count_y = lax.axis_size("sx"), lax.axis_size("sy")
    index_x, index_y = lax.axis_index("sx"), lax.axis_index("sy")
    count_z = count_x // 2
    lanes = 128
    r = lax.broadcasted_iota(jnp.int32, (count_x * count_y, lanes), 0)
    c = lax.broadcasted_iota(jnp.int32, (count_x * count_y, lanes), 1)
    own = jnp.where((r == c * count_y + index_y) & (c < count_x), 1.0, 0.0).astype(jnp.bfloat16)
    ids = ids_ref[...].astype(jnp.float32).astype(jnp.bfloat16)
    column = jnp.dot(ids, own, preferred_element_type=jnp.float32)
    b = lax.broadcasted_iota(jnp.int32, (8, lanes), 0)
    c = lax.broadcasted_iota(jnp.int32, (8, lanes), 1)
    named = jnp.zeros((8, lanes), jnp.float32)
    for block in range(2):
        wanted = (index_x * 2 + block).astype(jnp.float32)
        hit = jnp.max(jnp.where(column == wanted, 1.0, 0.0), axis=0, keepdims=True)
        named = jnp.where((b == block) & (c < count_x), hit, named)
    r = lax.broadcasted_iota(jnp.int32, (lanes, lanes), 0)
    c = lax.broadcasted_iota(jnp.int32, (lanes, lanes), 1)
    before = jnp.where(r < c, 1.0, 0.0).astype(jnp.bfloat16)
    rank = jnp.dot(named.astype(jnp.bfloat16), before, preferred_element_type=jnp.float32)
    pos = jnp.where(named > 0.5, rank, -1.0).astype(jnp.bfloat16)
    for out_ref, first in ((ask_ref, ASK_FIRST), (answer_ref, ANSWER_FIRST)):
        shape = (lanes, out_ref.shape[1])
        r = lax.broadcasted_iota(jnp.int32, shape, 0)
        c = lax.broadcasted_iota(jnp.int32, shape, 1) // KEY_HEADS
        row = ((c + first) % count_z) * 2 + c // count_z
        spread = jnp.where(r == row, 1.0, 0.0).astype(jnp.bfloat16)
        out_ref[...] = jnp.dot(pos, spread, preferred_element_type=jnp.float32)


def slot_onehot(pos):
    shape = (KEY_HEADS * SLOTS, pos.shape[1])
    r = lax.broadcasted_iota(jnp.int32, shape, 0)
    c = lax.broadcasted_iota(jnp.int32, shape, 1)
    hit = (pos == (r % SLOTS).astype(jnp.float32)) & (r // SLOTS == c % KEY_HEADS)
    return jnp.where(hit, 1.0, 0.0).astype(jnp.bfloat16)


def copies_kernel(q_ref, out_ref):
    q = q_ref[...].astype(jnp.float32)
    q = jnp.concatenate([q[:, h * FEAT : (h + 1) * FEAT] for h in range(KEY_HEADS)], axis=0).astype(jnp.bfloat16)
    for z in range(out_ref.shape[0]):
        out_ref[z] = q


def relay_kernel(k_ref, v_ref, out_ref, here, in_sems, out_sems):
    core = lax.axis_index("sx") % 2
    theirs = 1 - half_of(core, lax.axis_index("sy") % SLABS)
    tokens, width = k_ref.shape[0], out_ref.shape[1]
    lanes = pl.ds(pl.multiple_of(theirs * width, width), width)
    chunks = in_sems.shape[1]
    step = tokens // chunks
    pairs = [(i, j) for i in range(chunks) for j in range(2)]
    there = (k_ref, v_ref)
    arriving, leaving = {}, []
    for i, j in pairs:
        to = pl.ds(j * tokens + i * step, step)
        arriving[i, j] = pltpu.make_async_copy(there[j].at[pl.ds(i * step, step), lanes], here.at[to], in_sems.at[j, i])
        arriving[i, j].start()
    for i, j in pairs:
        arriving[i, j].wait()
        to = pl.ds(j * tokens + i * step, step)
        leaving.append(pltpu.make_async_copy(here.at[to], out_ref.at[to], out_sems.at[j, i]))
        leaving[-1].start()
    for copy in leaving:
        copy.wait()


def select_kernel(pos_ref, q_ref, out_ref, halves):
    core = lax.axis_index("sx") % 2
    q = q_ref[...].astype(jnp.float32).reshape(-1, FEAT).astype(jnp.bfloat16)
    for p in range(2):
        hot = slot_onehot(pos_ref[p : p + 1, :])
        picked = jnp.dot(hot, q, preferred_element_type=jnp.float32)
        for h in range(KEY_HEADS):
            lanes = slice((h % HALF) * FEAT, (h % HALF + 1) * FEAT)
            halves[p, h // HALF, :, lanes] = picked[h * SLOTS : (h + 1) * SLOTS].astype(jnp.bfloat16)
        for s in range(SLABS):
            out_ref[column_at(p * SLABS + s)] = halves[p, half_of(core, s)]


def attend_kernel(x_ref, k_ref, v_ref, kv_ref, y_ref):
    scale = HEAD_WIDTH ** (-0.5) * LOG2E
    mine = half_of(lax.axis_index("sx") % 2, lax.axis_index("sy") % SLABS)
    columns, tokens = x_ref.shape[0], k_ref.shape[0]
    rows = columns * SLOTS
    ones = jnp.ones((tokens, HEAD_WIDTH), jnp.bfloat16)
    ends = []
    for h in range(HALF):
        x = x_ref[:, :, h * FEAT : (h + 1) * FEAT].astype(jnp.float32).reshape(rows, FEAT).astype(jnp.bfloat16)
        q = [x[:, g * HEAD_WIDTH : (g + 1) * HEAD_WIDTH] for g in range(QUERY_PER_KEY)]
        q = jnp.concatenate(q, axis=0)
        there = pl.ds(pl.multiple_of((mine * HALF + h) * HEAD_WIDTH, HEAD_WIDTH), HEAD_WIDTH)
        here = slice(h * HEAD_WIDTH, (h + 1) * HEAD_WIDTH)
        slabs = ((k_ref[:, there], v_ref[:, there]), (kv_ref[:tokens, here], kv_ref[tokens:, here]))
        tops, sums = [], []
        for k, v in slabs:
            v = jnp.concatenate([v, ones], axis=1)
            s = lax.dot_general(q, k, (((1,), (1,)), ((), ())), preferred_element_type=jnp.float32)
            m = jnp.max(s, axis=1, keepdims=True)
            w = jnp.exp2((s - m) * scale).astype(jnp.bfloat16)
            tops.append(m)
            sums.append(jnp.dot(w, v, preferred_element_type=jnp.float32))
        top = functools.reduce(jnp.maximum, tops)
        both = functools.reduce(jnp.add, [jnp.exp2((m - top) * scale) * o for m, o in zip(tops, sums)])
        total = both[:, HEAD_WIDTH:]
        out = both[:, :HEAD_WIDTH] / total
        lse = top * scale + jnp.log2(total[:, :1])
        for g in range(QUERY_PER_KEY):
            part = out[g * rows : (g + 1) * rows].reshape(columns, SLOTS, HEAD_WIDTH).astype(jnp.bfloat16)
            at = (h * QUERY_PER_KEY + g) * HEAD_WIDTH
            y_ref[:, :, at : at + HEAD_WIDTH] = part
            ends.append(lse[g * rows : (g + 1) * rows])
    stat = stat_lanes(ends).reshape(columns, SLOTS, STAT).astype(jnp.bfloat16)
    y_ref[:, :, HALF * FEAT :] = stat


def merge_kernel(pos_ref, y_ref, mine_ref, theirs_ref):
    core = lax.axis_index("sx") % 2
    flip = (((0,), (0,)), ((), ()))
    lane = lax.broadcasted_iota(jnp.int32, (SLOTS, STAT), 1)
    data, lse = [], []
    for p in range(2):
        tall = []
        for half in range(2):
            froms = [
                jnp.where(core == 0, column_at(p * SLABS + 2 * t + half), column_at(p * SLABS + HALF * half + t))
                for t in range(4)
            ]
            ends = []
            for s in froms:
                stat = y_ref[s, :, HALF * FEAT :].astype(jnp.float32)
                ends.append(stat + (pltpu.roll(stat, STAT - 1, 1) + pltpu.roll(stat, STAT - 2, 1)))
            top = functools.reduce(jnp.maximum, ends)
            weights = [jnp.exp2(x - top) for x in ends]
            total = functools.reduce(jnp.add, weights)
            inverse = 1.0 / total
            weights = [w * inverse for w in weights]
            block = top + jnp.log2(total)
            for h in range(HALF):
                heads = []
                for g in range(QUERY_PER_KEY):
                    n = h * QUERY_PER_KEY + g
                    lanes = slice(n * HEAD_WIDTH, (n + 1) * HEAD_WIDTH)
                    terms = [w[:, 3 * n : 3 * n + 1] * y_ref[s, :, lanes].astype(jnp.float32) for w, s in zip(weights, froms)]
                    heads.append(functools.reduce(jnp.add, terms))
                shift = 3 * h * QUERY_PER_KEY
                stat = block if shift == 0 else pltpu.roll(block, STAT - shift, 1)
                stat = jnp.where(lane == ONE_LANE, 1.0, jnp.where(lane < ONE_LANE, stat, 0.0))
                tall.append(jnp.concatenate(heads + [stat], axis=1))
        tall = jnp.concatenate([x.astype(jnp.bfloat16) for x in pieces(jnp.concatenate(tall, axis=0))], axis=0)
        hot = jnp.concatenate([slot_onehot(pos_ref[p : p + 1, :])] * 3, axis=0)
        dense = lax.dot_general(hot, tall, flip, preferred_element_type=jnp.float32)
        named = dense[:, FEAT + ONE_LANE : FEAT + ONE_LANE + 1] > 0.5
        data.append(dense)
        lse.append(
            [jnp.where(named, dense[:, FEAT + 3 * g : FEAT + 3 * g + 1], NEVER) for g in range(QUERY_PER_KEY)]
        )
    rows = mine_ref.shape[0]
    for out_ref, is_first in ((mine_ref, core == 0), (theirs_ref, core == 1)):

        def side(x):
            return jnp.where(is_first, x[:rows], x[rows:])

        combine_two([side(x) for x in data], [[side(x) for x in y] for y in lse], out_ref)


def combine_two(data, lse, out_ref):
    shape = out_ref.shape[:-1]
    ends = []
    for g in range(QUERY_PER_KEY):
        a, b = lse[0][g], lse[1][g]
        top = jnp.maximum(a, b)
        wa, wb = jnp.exp2(a - top), jnp.exp2(b - top)
        total = wa + wb
        inverse = 1.0 / total
        lanes = slice(g * HEAD_WIDTH, (g + 1) * HEAD_WIDTH)
        mixed = data[0][:, lanes] * (wa * inverse) + data[1][:, lanes] * (wb * inverse)
        out_ref[..., lanes] = mixed.reshape(*shape, HEAD_WIDTH).astype(out_ref.dtype)
        ends.append(top + jnp.log2(total))
    if out_ref.dtype == jnp.float32:
        lane = lax.broadcasted_iota(jnp.int32, (mixed.shape[0], STAT), 1)
        stat = jnp.zeros(lane.shape, jnp.float32)
        for g in range(QUERY_PER_KEY):
            stat = jnp.where(lane == g, ends[g], stat)
    else:
        stat = stat_lanes(ends)
    out_ref[..., FEAT:] = stat.reshape(*shape, STAT).astype(out_ref.dtype)


def pair_kernel(mine_ref, pair_ref, out_ref):
    other = 1 - lax.axis_index("sx") % 2
    data = [mine_ref[:, :FEAT], pair_ref[other, :, :FEAT]]
    lse = [[x[:, g : g + 1] for g in range(QUERY_PER_KEY)] for x in (mine_ref[:, FEAT:], pair_ref[other, :, FEAT:])]
    combine_two(data, lse, out_ref)


def last_kernel(a_ref, out_ref):
    stat = a_ref[:, :, FEAT:].astype(jnp.float32)
    lse = stat + (pltpu.roll(stat, STAT - 1, 2) + pltpu.roll(stat, STAT - 2, 2))
    weight = jnp.exp2(lse - jnp.max(lse, axis=0, keepdims=True))
    weight = weight / jnp.sum(weight, axis=0, keepdims=True)
    for g in range(QUERY_PER_KEY):
        lanes = slice(g * HEAD_WIDTH, (g + 1) * HEAD_WIDTH)
        mixed = jnp.sum(a_ref[:, :, lanes].astype(jnp.float32) * weight[:, :, 3 * g : 3 * g + 1], axis=0)
        for h in range(KEY_HEADS):
            head = h * FEAT + g * HEAD_WIDTH
            out_ref[:, head : head + HEAD_WIDTH] = mixed[h : h + 1].astype(jnp.bfloat16)


def call(kernel, out, name, *args, scratch=()):
    return pl.pallas_call(
        kernel,
        out_shape=out,
        in_specs=[pl.BlockSpec(memory_space=pltpu.VMEM)] * len(args),
        out_specs=jax.tree.map(lambda _: pl.BlockSpec(memory_space=pltpu.VMEM), out),
        scratch_shapes=list(scratch),
        compiler_params=pltpu.CompilerParams(vmem_limit_bytes=40 * 1024 * 1024),
        name=name,
    )(*args)


def per_device(queries, keys, values, block_ids):
    count_x = lax.axis_size("sx")
    count_y = lax.axis_size("sy")
    count_z = count_x // 2
    tokens = keys.shape[0]
    cores = [[2 * z, 2 * z + 1] for z in range(count_z)]
    ask_groups, answer_groups = (
        [[2 * z + c for z in listed_from(first, count_z)] for c in range(2)] for first in (ASK_FIRST, ANSWER_FIRST)
    )
    columns = [listed_from(COLUMN_FIRST, count_y)]
    partners = [
        (x * count_y + y, x * count_y + (y ^ PARTNER[x % 2])) for x in range(count_x) for y in range(count_y)
    ]

    def exchange(x, axis, groups=None):
        return lax.all_to_all(x, axis, split_axis=0, concat_axis=0, tiled=True, axis_index_groups=groups)

    def half(*shape):
        return jax.ShapeDtypeStruct(shape, jnp.bfloat16)

    def full(*shape):
        return jax.ShapeDtypeStruct(shape, jnp.float32)

    own = call(copies_kernel, half(count_z, KEY_HEADS, FEAT), "copies", queries)
    rows = exchange(own, "sx", ask_groups)

    hbm = pl.BlockSpec(memory_space=pltpu.HBM)
    width = HALF * HEAD_WIDTH
    kv = pl.pallas_call(
        relay_kernel,
        out_shape=half(2 * tokens, width),
        in_specs=[hbm, hbm],
        out_specs=hbm,
        scratch_shapes=[
            pltpu.VMEM((2 * tokens, width), jnp.bfloat16),
            pltpu.SemaphoreType.DMA((2, 4)),
            pltpu.SemaphoreType.DMA((2, 4)),
        ],
        compiler_params=pltpu.CompilerParams(vmem_limit_bytes=60 * 1024 * 1024),
        name="relay",
    )(keys, values)
    kv = lax.ppermute(kv, ("sx", "sy"), partners)

    pos = full(8, count_x * KEY_HEADS)
    ask_pos, answer_pos = call(find_kernel, [pos, pos], "find", block_ids.T)
    rows = lax.all_gather(rows, "sx", axis=0, axis_index_groups=cores)
    rows = rows.reshape(count_x, KEY_HEADS, FEAT)
    asked = call(
        select_kernel,
        half(count_y, SLOTS, HALF * FEAT),
        "select",
        ask_pos,
        rows,
        scratch=[pltpu.VMEM((2, 2, SLOTS, HALF * FEAT), jnp.bfloat16)],
    )
    asked = exchange(asked, "sy", columns)
    part = call(attend_kernel, half(count_y, SLOTS, HALF * FEAT + STAT), "attend", asked, keys, values, kv)
    part = exchange(part, "sy", columns)
    side = full(count_z * KEY_HEADS, FEAT + STAT)
    mine, theirs = call(merge_kernel, [side, side], "merge", answer_pos, part)
    pair = lax.all_gather(theirs, "sx", axis=0, axis_index_groups=cores)
    part = call(pair_kernel, half(count_z, KEY_HEADS, FEAT + STAT), "pair", mine, pair)
    part = exchange(part, "sx", answer_groups)
    return call(last_kernel, half(1, KEY_HEADS * FEAT), "last", part)


def solution(mesh):
    return jax.shard_map(
        per_device,
        mesh=mesh,
        in_specs=(P(("sx", "sy"), None), P(("sx", "sy"), None), P(("sx", "sy"), None), P()),
        out_specs=P(("sx", "sy"), None),
        check_vma=False,
    )
```

```python
import functools

import jax
import jax.numpy as jnp
from jax import lax
from jax.experimental import pallas as pl
from jax.experimental.pallas import tpu as pltpu
from jax.sharding import PartitionSpec as P

QUERY_HEADS = 32
KEY_HEADS = 8
HEAD_WIDTH = 128
BLOCK = 4096
QUERY_PER_KEY = 4
LOG2E = 1.4426950408889634
NEVER = -1e30

FEAT = QUERY_PER_KEY * HEAD_WIDTH
SLOTS = 8
SLABS = 8
HALF = KEY_HEADS // 2
PARTNER = (1, 4)
STAT = 128
ONE_LANE = 12
PART_ROWS = QUERY_HEADS + 2


ASK_FIRST = 11
ANSWER_FIRST = 8


COLUMN_FIRST = 10


def listed_from(first, count):
    return [(i + first) % count for i in range(count)]


def column_at(i):
    return (i - COLUMN_FIRST) % (2 * SLABS)


def half_of(core, s):
    return jnp.where(core == 0, s % 2, s // 4)


def pieces(x):
    hi = x.astype(jnp.bfloat16).astype(jnp.float32)
    rest = x - hi
    mid = rest.astype(jnp.bfloat16).astype(jnp.float32)
    return hi, mid, rest - mid


def spread_pieces(lse):
    lane = lax.broadcasted_iota(jnp.int32, lse.shape, 1)
    hi, mid, lo = pieces(lse)
    return jnp.where(lane % 3 == 0, hi, jnp.where(lane % 3 == 1, pltpu.roll(mid, 1, 1), pltpu.roll(lo, 2, 1)))


def sum_pieces(stat):
    return stat + (pltpu.roll(stat, STAT - 1, 1) + pltpu.roll(stat, STAT - 2, 1))


def find_kernel(ids_ref, ask_ref, answer_ref):
    count_x, count_y = lax.axis_size("sx"), lax.axis_size("sy")
    index_x, index_y = lax.axis_index("sx"), lax.axis_index("sy")
    count_z = count_x // 2
    lanes = 128
    r = lax.broadcasted_iota(jnp.int32, (count_x * count_y, lanes), 0)
    c = lax.broadcasted_iota(jnp.int32, (count_x * count_y, lanes), 1)
    own = jnp.where((r == c * count_y + index_y) & (c < count_x), 1.0, 0.0).astype(jnp.bfloat16)
    ids = ids_ref[...].astype(jnp.float32).astype(jnp.bfloat16)
    column = jnp.dot(ids, own, preferred_element_type=jnp.float32)
    b = lax.broadcasted_iota(jnp.int32, (8, lanes), 0)
    c = lax.broadcasted_iota(jnp.int32, (8, lanes), 1)
    named = jnp.zeros((8, lanes), jnp.float32)
    for block in range(2):
        wanted = (index_x * 2 + block).astype(jnp.float32)
        hit = jnp.max(jnp.where(column == wanted, 1.0, 0.0), axis=0, keepdims=True)
        named = jnp.where((b == block) & (c < count_x), hit, named)
    r = lax.broadcasted_iota(jnp.int32, (lanes, lanes), 0)
    c = lax.broadcasted_iota(jnp.int32, (lanes, lanes), 1)
    before = jnp.where(r < c, 1.0, 0.0).astype(jnp.bfloat16)
    rank = jnp.dot(named.astype(jnp.bfloat16), before, preferred_element_type=jnp.float32)
    pos = jnp.where(named > 0.5, rank, -1.0).astype(jnp.bfloat16)
    for out_ref, first in ((ask_ref, ASK_FIRST), (answer_ref, ANSWER_FIRST)):
        shape = (lanes, out_ref.shape[1])
        r = lax.broadcasted_iota(jnp.int32, shape, 0)
        c = lax.broadcasted_iota(jnp.int32, shape, 1) // KEY_HEADS
        row = ((c + first) % count_z) * 2 + c // count_z
        spread = jnp.where(r == row, 1.0, 0.0).astype(jnp.bfloat16)
        out_ref[...] = jnp.dot(pos, spread, preferred_element_type=jnp.float32)


def slot_onehot(pos):
    shape = (KEY_HEADS * SLOTS, pos.shape[1])
    r = lax.broadcasted_iota(jnp.int32, shape, 0)
    c = lax.broadcasted_iota(jnp.int32, shape, 1)
    hit = (pos == (r % SLOTS).astype(jnp.float32)) & (r // SLOTS == c % KEY_HEADS)
    return jnp.where(hit, 1.0, 0.0).astype(jnp.bfloat16)


def copies_kernel(q_ref, out_ref):
    q = q_ref[...].astype(jnp.float32)
    q = jnp.concatenate([q[:, h * FEAT : (h + 1) * FEAT] for h in range(KEY_HEADS)], axis=0).astype(jnp.bfloat16)
    for z in range(out_ref.shape[0]):
        out_ref[z] = q


def relay_kernel(k_ref, v_ref, out_ref, here, in_sems, out_sems):
    core = lax.axis_index("sx") % 2
    theirs = 1 - half_of(core, lax.axis_index("sy") % SLABS)
    tokens, width = k_ref.shape[0], out_ref.shape[1]
    lanes = pl.ds(pl.multiple_of(theirs * width, width), width)
    chunks = in_sems.shape[1]
    step = tokens // chunks
    pairs = [(i, j) for i in range(chunks) for j in range(2)]
    there = (k_ref, v_ref)
    arriving, leaving = {}, []
    for i, j in pairs:
        to = pl.ds(j * tokens + i * step, step)
        arriving[i, j] = pltpu.make_async_copy(there[j].at[pl.ds(i * step, step), lanes], here.at[to], in_sems.at[j, i])
        arriving[i, j].start()
    for i, j in pairs:
        arriving[i, j].wait()
        to = pl.ds(j * tokens + i * step, step)
        leaving.append(pltpu.make_async_copy(here.at[to], out_ref.at[to], out_sems.at[j, i]))
        leaving[-1].start()
    for copy in leaving:
        copy.wait()


def select_kernel(pos_ref, q_ref, out_ref, halves):
    core = lax.axis_index("sx") % 2
    q = q_ref[...].astype(jnp.float32).reshape(-1, FEAT).astype(jnp.bfloat16)
    for p in range(2):
        hot = slot_onehot(pos_ref[p : p + 1, :])
        picked = jnp.dot(hot, q, preferred_element_type=jnp.float32)
        for h in range(KEY_HEADS):
            lanes = slice((h % HALF) * FEAT, (h % HALF + 1) * FEAT)
            halves[p, h // HALF, :, lanes] = picked[h * SLOTS : (h + 1) * SLOTS].astype(jnp.bfloat16)
        for s in range(SLABS):
            out_ref[column_at(p * SLABS + s)] = halves[p, half_of(core, s)]


def attend_kernel(x_ref, k_ref, v_ref, kv_ref, y_ref):
    scale = HEAD_WIDTH ** (-0.5) * LOG2E
    mine = half_of(lax.axis_index("sx") % 2, lax.axis_index("sy") % SLABS)
    columns, tokens = x_ref.shape[0], k_ref.shape[0]
    rows = columns * SLOTS
    ones = jnp.ones((tokens, HEAD_WIDTH), jnp.bfloat16)
    ends = []
    for h in range(HALF):
        x = x_ref[:, :, h * FEAT : (h + 1) * FEAT].astype(jnp.float32).reshape(rows, FEAT).astype(jnp.bfloat16)
        q = [x[:, g * HEAD_WIDTH : (g + 1) * HEAD_WIDTH] for g in range(QUERY_PER_KEY)]
        q = jnp.concatenate(q, axis=0)
        there = pl.ds(pl.multiple_of((mine * HALF + h) * HEAD_WIDTH, HEAD_WIDTH), HEAD_WIDTH)
        here = slice(h * HEAD_WIDTH, (h + 1) * HEAD_WIDTH)
        slabs = ((k_ref[:, there], v_ref[:, there]), (kv_ref[:tokens, here], kv_ref[tokens:, here]))
        tops, sums = [], []
        for k, v in slabs:
            v = jnp.concatenate([v, ones], axis=1)
            s = lax.dot_general(q, k, (((1,), (1,)), ((), ())), preferred_element_type=jnp.float32)
            m = jnp.max(s, axis=1, keepdims=True)
            w = jnp.exp2((s - m) * scale).astype(jnp.bfloat16)
            tops.append(m)
            sums.append(jnp.dot(w, v, preferred_element_type=jnp.float32))
        top = functools.reduce(jnp.maximum, tops)
        both = functools.reduce(jnp.add, [jnp.exp2((m - top) * scale) * o for m, o in zip(tops, sums)])
        total = both[:, HEAD_WIDTH:]
        out = both[:, :HEAD_WIDTH] / total
        lse = top * scale + jnp.log2(total)
        for g in range(QUERY_PER_KEY):
            part = out[g * rows : (g + 1) * rows].reshape(columns, SLOTS, HEAD_WIDTH).astype(jnp.bfloat16)
            at = (h * QUERY_PER_KEY + g) * HEAD_WIDTH
            y_ref[:, :, at : at + HEAD_WIDTH] = part
            ends.append(lse[g * rows : (g + 1) * rows])
    lane = lax.broadcasted_iota(jnp.int32, (rows, STAT), 1)
    stat = jnp.zeros((rows, STAT), jnp.float32)
    for n, x in enumerate(ends):
        stat = jnp.where(lane // 3 == n, x, stat)
    hi, mid, lo = pieces(stat)
    stat = jnp.where(lane % 3 == 0, hi, jnp.where(lane % 3 == 1, mid, lo))
    y_ref[:, :, HALF * FEAT :] = stat.reshape(columns, SLOTS, STAT).astype(jnp.bfloat16)


def merge_kernel(pos_ref, y_ref, mine_ref, theirs_ref):
    core = lax.axis_index("sx") % 2
    flip = (((0,), (0,)), ((), ()))
    lane = lax.broadcasted_iota(jnp.int32, (SLOTS, STAT), 1)
    data, lse = [], []
    for p in range(2):
        tall = []
        for half in range(2):
            froms = [
                jnp.where(core == 0, column_at(p * SLABS + 2 * t + half), column_at(p * SLABS + HALF * half + t))
                for t in range(4)
            ]
            ends = []
            for s in froms:
                ends.append(sum_pieces(y_ref[s, :, HALF * FEAT :].astype(jnp.float32)))
            top = functools.reduce(jnp.maximum, ends)
            weights = [jnp.exp2(x - top) for x in ends]
            total = functools.reduce(jnp.add, weights)
            inverse = 1.0 / total
            weights = [w * inverse for w in weights]
            block = top + jnp.log2(total)
            for h in range(HALF):
                heads = []
                for g in range(QUERY_PER_KEY):
                    n = h * QUERY_PER_KEY + g
                    lanes = slice(n * HEAD_WIDTH, (n + 1) * HEAD_WIDTH)
                    terms = [w[:, 3 * n : 3 * n + 1] * y_ref[s, :, lanes].astype(jnp.float32) for w, s in zip(weights, froms)]
                    heads.append(functools.reduce(jnp.add, terms))
                shift = 3 * h * QUERY_PER_KEY
                stat = block if shift == 0 else pltpu.roll(block, STAT - shift, 1)
                stat = jnp.where(lane == ONE_LANE, 1.0, jnp.where(lane < ONE_LANE, stat, 0.0))
                tall.append(jnp.concatenate(heads + [stat], axis=1))
        tall = jnp.concatenate([x.astype(jnp.bfloat16) for x in pieces(jnp.concatenate(tall, axis=0))], axis=0)
        hot = jnp.concatenate([slot_onehot(pos_ref[p : p + 1, :])] * 3, axis=0)
        dense = lax.dot_general(hot, tall, flip, preferred_element_type=jnp.float32)
        stat = dense[:, FEAT:]
        data.append(dense)
        lse.append(jnp.where(stat[:, ONE_LANE : ONE_LANE + 1] > 0.5, stat, NEVER))
    mixed = jnp.concatenate(combine_two(data, lse), axis=1)
    rows = mine_ref.shape[0]
    mine_ref[...] = jnp.where(core == 0, mixed[:rows], mixed[rows:])
    theirs_ref[...] = jnp.where(core == 0, mixed[rows:], mixed[:rows])


def combine_two(data, lse):
    top = jnp.maximum(lse[0], lse[1])
    weights = [jnp.exp2(x - top) for x in lse]
    total = weights[0] + weights[1]
    inverse = 1.0 / total
    weights = [w * inverse for w in weights]
    mixed = []
    for g in range(QUERY_PER_KEY):
        lanes = slice(g * HEAD_WIDTH, (g + 1) * HEAD_WIDTH)
        terms = [x[:, lanes] * w[:, 3 * g : 3 * g + 1] for x, w in zip(data, weights)]
        mixed.append(terms[0] + terms[1])
    return mixed + [top + jnp.log2(total)]


def pair_kernel(mine_ref, pair_ref, out_ref, wide, stats):
    other = 1 - lax.axis_index("sx") % 2
    refs = (mine_ref, pair_ref.at[other])
    mixed = combine_two([x[:, :FEAT] for x in refs], [x[:, FEAT:] for x in refs])
    count = out_ref.shape[0] // PART_ROWS
    for z in range(count):
        for g in range(QUERY_PER_KEY):
            part = mixed[g][z * KEY_HEADS : (z + 1) * KEY_HEADS]
            wide[pl.ds(z * PART_ROWS + g, KEY_HEADS, stride=QUERY_PER_KEY), :] = part
    lane = lax.broadcasted_iota(jnp.int32, stats.shape, 1)
    stats[...] = jnp.where(lane < ONE_LANE, spread_pieces(mixed[-1]), 0.0)
    terms = [stats[pl.ds(h, count, stride=KEY_HEADS), :] for h in range(KEY_HEADS)]
    terms = [x if h == 0 else pltpu.roll(x, ONE_LANE * h, 1) for h, x in enumerate(terms)]
    wide[pl.ds(QUERY_HEADS, count, stride=PART_ROWS), :] = functools.reduce(jnp.add, terms)
    wide[pl.ds(QUERY_HEADS + 1, count, stride=PART_ROWS), :] = jnp.zeros((count, STAT), jnp.float32)
    out_ref[...] = wide[...].astype(jnp.bfloat16)


def last_kernel(a_ref, out_ref, wide):
    count = a_ref.shape[0] // PART_ROWS
    wide[...] = a_ref[...].astype(jnp.float32)
    lse = sum_pieces(wide[pl.ds(QUERY_HEADS, count, stride=PART_ROWS), :])
    weight = jnp.exp2(lse - jnp.max(lse, axis=0, keepdims=True))
    weight = weight / jnp.sum(weight, axis=0, keepdims=True)
    for n in range(QUERY_HEADS):
        part = wide[pl.ds(n, count, stride=PART_ROWS), :] * weight[:, 3 * n : 3 * n + 1]
        part = jnp.sum(part, axis=0, keepdims=True)
        out_ref[:, n * HEAD_WIDTH : (n + 1) * HEAD_WIDTH] = part.astype(jnp.bfloat16)


def call(kernel, out, name, *args, scratch=()):
    return pl.pallas_call(
        kernel,
        out_shape=out,
        in_specs=[pl.BlockSpec(memory_space=pltpu.VMEM)] * len(args),
        out_specs=jax.tree.map(lambda _: pl.BlockSpec(memory_space=pltpu.VMEM), out),
        scratch_shapes=list(scratch),
        compiler_params=pltpu.CompilerParams(vmem_limit_bytes=40 * 1024 * 1024),
        name=name,
    )(*args)


def per_device(queries, keys, values, block_ids):
    count_x = lax.axis_size("sx")
    count_y = lax.axis_size("sy")
    count_z = count_x // 2
    tokens = keys.shape[0]
    cores = [[2 * z, 2 * z + 1] for z in range(count_z)]
    ask_groups, answer_groups = (
        [[2 * z + c for z in listed_from(first, count_z)] for c in range(2)] for first in (ASK_FIRST, ANSWER_FIRST)
    )
    columns = [listed_from(COLUMN_FIRST, count_y)]
    partners = [
        (x * count_y + y, x * count_y + (y ^ PARTNER[x % 2])) for x in range(count_x) for y in range(count_y)
    ]

    def exchange(x, axis, groups=None):
        return lax.all_to_all(x, axis, split_axis=0, concat_axis=0, tiled=True, axis_index_groups=groups)

    def half(*shape):
        return jax.ShapeDtypeStruct(shape, jnp.bfloat16)

    def full(*shape):
        return jax.ShapeDtypeStruct(shape, jnp.float32)

    own = call(copies_kernel, half(count_z, KEY_HEADS, FEAT), "copies", queries)
    rows = exchange(own, "sx", ask_groups)

    hbm = pl.BlockSpec(memory_space=pltpu.HBM)
    width = HALF * HEAD_WIDTH
    kv = pl.pallas_call(
        relay_kernel,
        out_shape=half(2 * tokens, width),
        in_specs=[hbm, hbm],
        out_specs=hbm,
        scratch_shapes=[
            pltpu.VMEM((2 * tokens, width), jnp.bfloat16),
            pltpu.SemaphoreType.DMA((2, 4)),
            pltpu.SemaphoreType.DMA((2, 4)),
        ],
        compiler_params=pltpu.CompilerParams(vmem_limit_bytes=60 * 1024 * 1024),
        name="relay",
    )(keys, values)
    kv = lax.ppermute(kv, ("sx", "sy"), partners)

    pos = full(8, count_x * KEY_HEADS)
    ask_pos, answer_pos = call(find_kernel, [pos, pos], "find", block_ids.T)
    rows = lax.all_gather(rows, "sx", axis=0, axis_index_groups=cores)
    rows = rows.reshape(count_x, KEY_HEADS, FEAT)
    asked = call(
        select_kernel,
        half(count_y, SLOTS, HALF * FEAT),
        "select",
        ask_pos,
        rows,
        scratch=[pltpu.VMEM((2, 2, SLOTS, HALF * FEAT), jnp.bfloat16)],
    )
    asked = exchange(asked, "sy", columns)
    part = call(attend_kernel, half(count_y, SLOTS, HALF * FEAT + STAT), "attend", asked, keys, values, kv)
    part = exchange(part, "sy", columns)
    side = full(count_z * KEY_HEADS, FEAT + STAT)
    mine, theirs = call(merge_kernel, [side, side], "merge", answer_pos, part)
    pair = lax.all_gather(theirs, "sx", axis=0, axis_index_groups=cores)
    wide = pltpu.VMEM((count_z * PART_ROWS, HEAD_WIDTH), jnp.float32)
    stats = pltpu.VMEM((count_z * KEY_HEADS, STAT), jnp.float32)
    part = call(pair_kernel, half(*wide.shape), "pair", mine, pair, scratch=[wide, stats])
    part = exchange(part.reshape(count_z, PART_ROWS // 2, 2, HEAD_WIDTH), "sx", answer_groups)
    return call(last_kernel, half(1, KEY_HEADS * FEAT), "last", part.reshape(wide.shape), scratch=[wide])


def solution(mesh):
    return jax.shard_map(
        per_device,
        mesh=mesh,
        in_specs=(P(("sx", "sy"), None), P(("sx", "sy"), None), P(("sx", "sy"), None), P()),
        out_specs=P(("sx", "sy"), None),
        check_vma=False,
    )
```

```python
import functools

import jax
import jax.numpy as jnp
from jax import lax
from jax.experimental import pallas as pl
from jax.experimental.pallas import tpu as pltpu
from jax.sharding import PartitionSpec as P

QUERY_HEADS = 32
KEY_HEADS = 8
HEAD_WIDTH = 128
BLOCK = 4096
QUERY_PER_KEY = 4
LOG2E = 1.4426950408889634
NEVER = -1e30

FEAT = QUERY_PER_KEY * HEAD_WIDTH
SLOTS = 8
SLABS = 8
HALF = KEY_HEADS // 2
PARTNER = (1, 4)
STAT = 128
ONE_LANE = 12
PART_ROWS = QUERY_HEADS + 2


ASK_FIRST = 11
ANSWER_FIRST = 8


COLUMN_FIRST = 10


def listed_from(first, count):
    return [(i + first) % count for i in range(count)]


def column_at(i):
    return (i - COLUMN_FIRST) % (2 * SLABS)


def half_of(core, s):
    return jnp.where(core == 0, s % 2, s // 4)


def pieces(x):
    hi = x.astype(jnp.bfloat16).astype(jnp.float32)
    rest = x - hi
    mid = rest.astype(jnp.bfloat16).astype(jnp.float32)
    return hi, mid, rest - mid


def spread_pieces(lse):
    lane = lax.broadcasted_iota(jnp.int32, lse.shape, 1)
    hi, mid, lo = pieces(lse)
    return jnp.where(lane % 3 == 0, hi, jnp.where(lane % 3 == 1, pltpu.roll(mid, 1, 1), pltpu.roll(lo, 2, 1)))


def sum_pieces(stat):
    return stat + (pltpu.roll(stat, STAT - 1, 1) + pltpu.roll(stat, STAT - 2, 1))


def find_kernel(ids_ref, ask_ref, answer_ref):
    count_x, count_y = lax.axis_size("sx"), lax.axis_size("sy")
    index_x, index_y = lax.axis_index("sx"), lax.axis_index("sy")
    count_z = count_x // 2
    lanes = 128
    r = lax.broadcasted_iota(jnp.int32, (count_x * count_y, lanes), 0)
    c = lax.broadcasted_iota(jnp.int32, (count_x * count_y, lanes), 1)
    own = jnp.where((r == c * count_y + index_y) & (c < count_x), 1.0, 0.0).astype(jnp.bfloat16)
    ids = ids_ref[...].astype(jnp.float32).astype(jnp.bfloat16)
    column = jnp.dot(ids, own, preferred_element_type=jnp.float32)
    b = lax.broadcasted_iota(jnp.int32, (8, lanes), 0)
    c = lax.broadcasted_iota(jnp.int32, (8, lanes), 1)
    named = jnp.zeros((8, lanes), jnp.float32)
    for block in range(2):
        wanted = (index_x * 2 + block).astype(jnp.float32)
        hit = jnp.max(jnp.where(column == wanted, 1.0, 0.0), axis=0, keepdims=True)
        named = jnp.where((b == block) & (c < count_x), hit, named)
    r = lax.broadcasted_iota(jnp.int32, (lanes, lanes), 0)
    c = lax.broadcasted_iota(jnp.int32, (lanes, lanes), 1)
    before = jnp.where(r < c, 1.0, 0.0).astype(jnp.bfloat16)
    rank = jnp.dot(named.astype(jnp.bfloat16), before, preferred_element_type=jnp.float32)
    pos = jnp.where(named > 0.5, rank, -1.0).astype(jnp.bfloat16)
    shape = (lanes, ask_ref.shape[1])
    r = lax.broadcasted_iota(jnp.int32, shape, 0)
    c = lax.broadcasted_iota(jnp.int32, shape, 1) // KEY_HEADS
    row = ((c + ASK_FIRST) % count_z) * 2 + c // count_z
    spread = jnp.where(r == row, 1.0, 0.0).astype(jnp.bfloat16)
    ask_ref[...] = jnp.dot(pos, spread, preferred_element_type=jnp.float32)
    shape = (answer_ref.shape[0], lanes)
    r = lax.broadcasted_iota(jnp.int32, shape, 0) // KEY_HEADS
    c = lax.broadcasted_iota(jnp.int32, shape, 1)
    row = ((r + ANSWER_FIRST) % count_z) * 2 + r // count_z
    spread = jnp.where(c == row, 1.0, 0.0).astype(jnp.bfloat16)
    across = (((1,), (1,)), ((), ()))
    answer_ref[...] = lax.dot_general(spread, pos, across, preferred_element_type=jnp.float32)


def slot_onehot(pos):
    shape = (KEY_HEADS * SLOTS, pos.shape[1])
    r = lax.broadcasted_iota(jnp.int32, shape, 0)
    c = lax.broadcasted_iota(jnp.int32, shape, 1)
    hit = (pos == (r % SLOTS).astype(jnp.float32)) & (r // SLOTS == c % KEY_HEADS)
    return jnp.where(hit, 1.0, 0.0).astype(jnp.bfloat16)


def copies_kernel(q_ref, out_ref):
    q = q_ref[...].astype(jnp.float32)
    q = jnp.concatenate([q[:, h * FEAT : (h + 1) * FEAT] for h in range(KEY_HEADS)], axis=0).astype(jnp.bfloat16)
    for z in range(out_ref.shape[0]):
        out_ref[z] = q


def relay_kernel(k_ref, v_ref, out_ref, here, in_sems, out_sems):
    core = lax.axis_index("sx") % 2
    theirs = 1 - half_of(core, lax.axis_index("sy") % SLABS)
    tokens, width = k_ref.shape[0], out_ref.shape[1]
    lanes = pl.ds(pl.multiple_of(theirs * width, width), width)
    chunks = in_sems.shape[1]
    step = tokens // chunks
    pairs = [(i, j) for i in range(chunks) for j in range(2)]
    there = (k_ref, v_ref)
    arriving, leaving = {}, []
    for i, j in pairs:
        to = pl.ds(j * tokens + i * step, step)
        arriving[i, j] = pltpu.make_async_copy(there[j].at[pl.ds(i * step, step), lanes], here.at[to], in_sems.at[j, i])
        arriving[i, j].start()
    for i, j in pairs:
        arriving[i, j].wait()
        to = pl.ds(j * tokens + i * step, step)
        leaving.append(pltpu.make_async_copy(here.at[to], out_ref.at[to], out_sems.at[j, i]))
        leaving[-1].start()
    for copy in leaving:
        copy.wait()


def select_kernel(pos_ref, q_ref, out_ref, halves):
    core = lax.axis_index("sx") % 2
    q = q_ref[...].astype(jnp.float32).reshape(-1, FEAT).astype(jnp.bfloat16)
    for p in range(2):
        hot = slot_onehot(pos_ref[p : p + 1, :])
        picked = jnp.dot(hot, q, preferred_element_type=jnp.float32)
        for h in range(KEY_HEADS):
            lanes = slice((h % HALF) * FEAT, (h % HALF + 1) * FEAT)
            halves[p, h // HALF, :, lanes] = picked[h * SLOTS : (h + 1) * SLOTS].astype(jnp.bfloat16)
        for s in range(SLABS):
            out_ref[column_at(p * SLABS + s)] = halves[p, half_of(core, s)]


def attend_kernel(x_ref, k_ref, v_ref, kv_ref, y_ref):
    scale = HEAD_WIDTH ** (-0.5) * LOG2E
    mine = half_of(lax.axis_index("sx") % 2, lax.axis_index("sy") % SLABS)
    columns, tokens = x_ref.shape[0], k_ref.shape[0]
    rows = columns * SLOTS
    ones = jnp.ones((tokens, HEAD_WIDTH), jnp.bfloat16)
    ends = []
    for h in range(HALF):
        x = x_ref[:, :, h * FEAT : (h + 1) * FEAT].astype(jnp.float32).reshape(rows, FEAT).astype(jnp.bfloat16)
        q = [x[:, g * HEAD_WIDTH : (g + 1) * HEAD_WIDTH] for g in range(QUERY_PER_KEY)]
        q = jnp.concatenate(q, axis=0)
        there = pl.ds(pl.multiple_of((mine * HALF + h) * HEAD_WIDTH, HEAD_WIDTH), HEAD_WIDTH)
        here = slice(h * HEAD_WIDTH, (h + 1) * HEAD_WIDTH)
        slabs = ((k_ref[:, there], v_ref[:, there]), (kv_ref[:tokens, here], kv_ref[tokens:, here]))
        tops, sums = [], []
        for k, v in slabs:
            v = jnp.concatenate([v, ones], axis=1)
            s = lax.dot_general(q, k, (((1,), (1,)), ((), ())), preferred_element_type=jnp.float32)
            m = jnp.max(s, axis=1, keepdims=True)
            w = jnp.exp2((s - m) * scale).astype(jnp.bfloat16)
            tops.append(m)
            sums.append(jnp.dot(w, v, preferred_element_type=jnp.float32))
        top = functools.reduce(jnp.maximum, tops)
        both = functools.reduce(jnp.add, [jnp.exp2((m - top) * scale) * o for m, o in zip(tops, sums)])
        total = both[:, HEAD_WIDTH:]
        out = both[:, :HEAD_WIDTH] / total
        lse = top * scale + jnp.log2(total)
        for g in range(QUERY_PER_KEY):
            part = out[g * rows : (g + 1) * rows].reshape(columns, SLOTS, HEAD_WIDTH).astype(jnp.bfloat16)
            at = (h * QUERY_PER_KEY + g) * HEAD_WIDTH
            y_ref[:, :, at : at + HEAD_WIDTH] = part
            ends.append(lse[g * rows : (g + 1) * rows])
    lane = lax.broadcasted_iota(jnp.int32, (rows, STAT), 1)
    stat = jnp.zeros((rows, STAT), jnp.float32)
    for n, x in enumerate(ends):
        stat = jnp.where(lane // 3 == n, x, stat)
    hi, mid, lo = pieces(stat)
    stat = jnp.where(lane % 3 == 0, hi, jnp.where(lane % 3 == 1, mid, lo))
    y_ref[:, :, HALF * FEAT :] = stat.reshape(columns, SLOTS, STAT).astype(jnp.bfloat16)


def merge_kernel(pos_ref, y_ref, mine_ref, theirs_ref):
    core = lax.axis_index("sx") % 2
    lane = lax.broadcasted_iota(jnp.int32, (SLOTS, STAT), 1)
    data, lse = [], []
    for p in range(2):
        tall = []
        for half in range(2):
            froms = [
                jnp.where(core == 0, column_at(p * SLABS + 2 * t + half), column_at(p * SLABS + HALF * half + t))
                for t in range(4)
            ]
            ends = []
            for s in froms:
                ends.append(sum_pieces(y_ref[s, :, HALF * FEAT :].astype(jnp.float32)))
            top = functools.reduce(jnp.maximum, ends)
            weights = [jnp.exp2(x - top) for x in ends]
            total = functools.reduce(jnp.add, weights)
            inverse = 1.0 / total
            weights = [w * inverse for w in weights]
            block = top + jnp.log2(total)
            for h in range(HALF):
                heads = []
                for g in range(QUERY_PER_KEY):
                    n = h * QUERY_PER_KEY + g
                    lanes = slice(n * HEAD_WIDTH, (n + 1) * HEAD_WIDTH)
                    terms = [w[:, 3 * n : 3 * n + 1] * y_ref[s, :, lanes].astype(jnp.float32) for w, s in zip(weights, froms)]
                    heads.append(functools.reduce(jnp.add, terms))
                shift = 3 * h * QUERY_PER_KEY
                stat = block if shift == 0 else pltpu.roll(block, STAT - shift, 1)
                stat = jnp.where(lane == ONE_LANE, 1.0, jnp.where(lane < ONE_LANE, stat, 0.0))
                tall.append(jnp.concatenate(heads + [stat], axis=1))
        tall = jnp.concatenate([x.astype(jnp.bfloat16) for x in pieces(jnp.concatenate(tall, axis=0))], axis=0)
        shape = (pos_ref.shape[0], 3 * KEY_HEADS * SLOTS)
        r = lax.broadcasted_iota(jnp.int32, shape, 0)
        c = lax.broadcasted_iota(jnp.int32, shape, 1)
        hit = (pos_ref[:, p : p + 1] == (c % SLOTS).astype(jnp.float32)) & (c // SLOTS % KEY_HEADS == r % KEY_HEADS)
        hot = jnp.where(hit, 1.0, 0.0).astype(jnp.bfloat16)
        dense = jnp.dot(hot, tall, preferred_element_type=jnp.float32)
        stat = dense[:, FEAT:]
        data.append(dense)
        lse.append(jnp.where(stat[:, ONE_LANE : ONE_LANE + 1] > 0.5, stat, NEVER))
    mixed = jnp.concatenate(combine_two(data, lse), axis=1)
    rows = mine_ref.shape[0]
    mine_ref[...] = jnp.where(core == 0, mixed[:rows], mixed[rows:])
    theirs_ref[...] = jnp.where(core == 0, mixed[rows:], mixed[:rows])


def combine_two(data, lse):
    top = jnp.maximum(lse[0], lse[1])
    weights = [jnp.exp2(x - top) for x in lse]
    total = weights[0] + weights[1]
    inverse = 1.0 / total
    weights = [w * inverse for w in weights]
    mixed = []
    for g in range(QUERY_PER_KEY):
        lanes = slice(g * HEAD_WIDTH, (g + 1) * HEAD_WIDTH)
        terms = [x[:, lanes] * w[:, 3 * g : 3 * g + 1] for x, w in zip(data, weights)]
        mixed.append(terms[0] + terms[1])
    return mixed + [top + jnp.log2(total)]


def pair_kernel(mine_ref, pair_ref, out_ref, wide, stats):
    other = 1 - lax.axis_index("sx") % 2
    refs = (mine_ref, pair_ref.at[other])
    mixed = combine_two([x[:, :FEAT] for x in refs], [x[:, FEAT:] for x in refs])
    count = out_ref.shape[0] // PART_ROWS
    for z in range(count):
        for g in range(QUERY_PER_KEY):
            part = mixed[g][z * KEY_HEADS : (z + 1) * KEY_HEADS]
            wide[pl.ds(z * PART_ROWS + g, KEY_HEADS, stride=QUERY_PER_KEY), :] = part
    stat = spread_pieces(mixed[-1])
    lane = lax.broadcasted_iota(jnp.int32, stat.shape, 1)
    stats[: stat.shape[0]] = jnp.where(lane < ONE_LANE, stat, 0.0)
    terms = [stats[pl.ds(h, count, stride=KEY_HEADS), :] for h in range(KEY_HEADS)]
    terms = [x if h == 0 else pltpu.roll(x, ONE_LANE * h, 1) for h, x in enumerate(terms)]
    wide[pl.ds(QUERY_HEADS, count, stride=PART_ROWS), :] = functools.reduce(jnp.add, terms)
    wide[pl.ds(QUERY_HEADS + 1, count, stride=PART_ROWS), :] = jnp.zeros((count, STAT), jnp.float32)
    out_ref[...] = wide[: out_ref.shape[0]].astype(jnp.bfloat16)


def last_kernel(a_ref, out_ref, wide):
    count = a_ref.shape[0] // PART_ROWS
    wide[: a_ref.shape[0]] = a_ref[...].astype(jnp.float32)
    lse = sum_pieces(wide[pl.ds(QUERY_HEADS, count, stride=PART_ROWS), :])
    weight = jnp.exp2(lse - jnp.max(lse, axis=0, keepdims=True))
    weight = weight / jnp.sum(weight, axis=0, keepdims=True)
    parts = []
    for n in range(QUERY_HEADS):
        part = wide[pl.ds(n, count, stride=PART_ROWS), :] * weight[:, 3 * n : 3 * n + 1]
        parts.append(jnp.sum(part, axis=0, keepdims=True))
    out_ref[...] = jnp.concatenate(parts, axis=1).astype(jnp.bfloat16)


def call(kernel, out, name, *args, scratch=()):
    return pl.pallas_call(
        kernel,
        out_shape=out,
        in_specs=[pl.BlockSpec(memory_space=pltpu.VMEM)] * len(args),
        out_specs=jax.tree.map(lambda _: pl.BlockSpec(memory_space=pltpu.VMEM), out),
        scratch_shapes=list(scratch),
        compiler_params=pltpu.CompilerParams(vmem_limit_bytes=40 * 1024 * 1024),
        name=name,
    )(*args)


def per_device(queries, keys, values, block_ids):
    count_x = lax.axis_size("sx")
    count_y = lax.axis_size("sy")
    count_z = count_x // 2
    tokens = keys.shape[0]
    cores = [[2 * z, 2 * z + 1] for z in range(count_z)]
    ask_groups, answer_groups = (
        [[2 * z + c for z in listed_from(first, count_z)] for c in range(2)] for first in (ASK_FIRST, ANSWER_FIRST)
    )
    columns = [listed_from(COLUMN_FIRST, count_y)]
    partners = [
        (x * count_y + y, x * count_y + (y ^ PARTNER[x % 2])) for x in range(count_x) for y in range(count_y)
    ]

    def exchange(x, axis, groups=None):
        return lax.all_to_all(x, axis, split_axis=0, concat_axis=0, tiled=True, axis_index_groups=groups)

    def half(*shape):
        return jax.ShapeDtypeStruct(shape, jnp.bfloat16)

    def full(*shape):
        return jax.ShapeDtypeStruct(shape, jnp.float32)

    own = call(copies_kernel, half(count_z, KEY_HEADS, FEAT), "copies", queries)
    rows = exchange(own, "sx", ask_groups)

    hbm = pl.BlockSpec(memory_space=pltpu.HBM)
    width = HALF * HEAD_WIDTH
    kv = pl.pallas_call(
        relay_kernel,
        out_shape=half(2 * tokens, width),
        in_specs=[hbm, hbm],
        out_specs=hbm,
        scratch_shapes=[
            pltpu.VMEM((2 * tokens, width), jnp.bfloat16),
            pltpu.SemaphoreType.DMA((2, 4)),
            pltpu.SemaphoreType.DMA((2, 4)),
        ],
        compiler_params=pltpu.CompilerParams(vmem_limit_bytes=60 * 1024 * 1024),
        name="relay",
    )(keys, values)
    kv = lax.ppermute(kv, ("sx", "sy"), partners)

    rows_heads = count_x * KEY_HEADS
    ask_pos, answer_pos = call(find_kernel, [full(8, rows_heads), full(rows_heads, 8)], "find", block_ids.T)
    rows = lax.all_gather(rows, "sx", axis=0, axis_index_groups=cores)
    rows = rows.reshape(count_x, KEY_HEADS, FEAT)
    asked = call(
        select_kernel,
        half(count_y, SLOTS, HALF * FEAT),
        "select",
        ask_pos,
        rows,
        scratch=[pltpu.VMEM((2, 2, SLOTS, HALF * FEAT), jnp.bfloat16)],
    )
    asked = exchange(asked, "sy", columns)
    part = call(attend_kernel, half(count_y, SLOTS, HALF * FEAT + STAT), "attend", asked, keys, values, kv)
    part = exchange(part, "sy", columns)
    side = full(count_z * KEY_HEADS, FEAT + STAT)
    mine, theirs = call(merge_kernel, [side, side], "merge", answer_pos, part)
    pair = lax.all_gather(theirs, "sx", axis=0, axis_index_groups=cores)
    flat = (count_z * PART_ROWS, HEAD_WIDTH)
    wide = pltpu.VMEM(((count_z + 2) * PART_ROWS, HEAD_WIDTH), jnp.float32)
    stats = pltpu.VMEM(((count_z + 1) * KEY_HEADS, STAT), jnp.float32)
    part = call(pair_kernel, half(*flat), "pair", mine, pair, scratch=[wide, stats])
    part = exchange(part.reshape(count_z, PART_ROWS // 2, 2, HEAD_WIDTH), "sx", answer_groups)
    return call(last_kernel, half(1, KEY_HEADS * FEAT), "last", part.reshape(flat), scratch=[wide])


def solution(mesh):
    return jax.shard_map(
        per_device,
        mesh=mesh,
        in_specs=(P(("sx", "sy"), None), P(("sx", "sy"), None), P(("sx", "sy"), None), P()),
        out_specs=P(("sx", "sy"), None),
        check_vma=False,
    )
```
